32 devices in a mesh: freq: 4 (over y, x), rtile: 4 (over z), rep: 2 (over core).
Axes of the slice: x: 2, y: 2, z: 4, core: 2. Of those that a mesh axis runs over, the one named last changes fastest.
Arguments:
- model: bfloat16 [4, 512, 32, 1024], P('rtile', 'freq'), may hold values from -0.1796875 to 0.1796875
- green_left: bfloat16 [2, 12, 8, 8, 48, 256], P(None, 'freq', 'rep', 'rtile'), may hold values from -0.21875 to 0.21875
- green_right: bfloat16 [2, 12, 8, 8, 48, 256], P(None, 'freq', 'rep', 'rtile'), may hold values from -0.25 to 0.25
- ranks: int32 [12, 8, 8], P('freq', 'rep', 'rtile'), may hold values from 8 to 48
- data: float32 [2, 384, 2048], P(None, ('freq', 'rtile'), 'rep'), may hold values from -3 to 3
Outputs:
- residual: float32 [2, 384, 2048], P(None, ('freq', 'rtile'), 'rep')
- gradient: bfloat16 [4, 512, 32, 1024], P('rtile', ('freq', 'rep'))
The draws below stay inside these ranges and needn't reach their ends.
All inputs are finite; a program needn't handle non-finite values.
Results may differ from the reference program's by a relative error of at most 0.014.
Values may be sent and summed in bfloat16 or wider, within the bound.
No kernel may reach another device: no remote copies, remote signals or barrier semaphores. Data moves between devices by JAX's collectives and lax.ppermute only.
A program may use at most 64 MiB of HBM per device.

```python
import math
import jax
import jax.numpy as jnp
from jax import lax

TILE = 256
RANK = 48
NS = 2048
NT = 1024
RHS = 32
CW = 512
NCT = 8
NR = 2048
ROWT = 8
NF = 12
N_RTILE = 4


def plant(drawn, rng, smallest, largest):
    place = [jax.random.randint(jax.random.fold_in(rng, axis), (), 0, length) for axis, length in enumerate(drawn.shape)]
    longest = drawn.shape.index(max(drawn.shape))
    beside = place[:longest] + [(place[longest] + 1) % drawn.shape[longest]] + place[longest + 1:]
    return drawn.at[tuple(place)].set(smallest).at[tuple(beside)].set(largest)


def block_levels(key, shape, shards, least, high):
    def one(dim, parts):
        draws = jax.random.uniform(jax.random.fold_in(jax.random.fold_in(key, 6), dim), (parts,), jnp.float32, least / len(shards), high / len(shards))
        return jnp.repeat(jnp.exp(draws), shape[dim] // parts).reshape((-1,) + (1,) * (len(shape) - dim - 1))

    level = one(*shards[0])
    for cut in shards[1:]:
        level = level * one(*cut)
    return level


def centred(key, dims, deviation, most, split=(), kind=jnp.bfloat16):
    loudness = block_levels(key, dims, split, -0.22, 0.18) if split else 1.0
    drawn = jax.random.normal(key, dims, jnp.float32) * deviation * loudness
    return jnp.minimum(jnp.maximum(drawn, -most), most).astype(kind)


def setup_inputs(seed: int = 0) -> dict:
    key_list = jax.random.split(jax.random.key(seed), 6)
    return {
        "model": centred(key_list[0], (N_RTILE, CW, RHS, NT), 0.03, 0.1796875, ((0, 4), (1, 4))),
        "green_left": centred(key_list[1], (2, NF, ROWT, NCT, RANK, TILE), (2 * RANK * NCT) ** -0.5, 0.21875, ((1, 4), (2, 2), (3, 4))),
        "green_right": centred(key_list[2], (2, NF, ROWT, NCT, RANK, TILE), (2 * TILE) ** -0.5, 0.25, ((1, 4), (2, 2), (3, 4))),
        "ranks": plant(jax.random.randint(key_list[3], (NF, ROWT, NCT), RANK // 6, RANK + 1), jax.random.fold_in(key_list[3], 1), RANK // 6, RANK).astype(jnp.int32),
        "data": centred(key_list[4], (2, NF * RHS, NS), 0.5, 3.0, ((1, 16), (2, 2)), jnp.float32),
    }


def tables(count, length):
    freq_bins = 1 + jnp.arange(count, dtype=jnp.int32)
    samples = jnp.arange(length, dtype=jnp.int32)
    phases = ((samples[:, None] * freq_bins[None, :]) % length).astype(jnp.float32) * (2.0 * math.pi / length)
    return jnp.cos(phases).astype(jnp.bfloat16), (-jnp.sin(phases)).astype(jnp.bfloat16)


def per_freq(inputs):
    left, right, spec, rank_row, observed = inputs
    left_re = left[0].astype(jnp.float32)
    left_im = left[1].astype(jnp.float32)
    right_re = right[0].astype(jnp.float32)
    right_im = right[1].astype(jnp.float32)
    spec_re = spec[0].astype(jnp.float32)
    spec_im = spec[1].astype(jnp.float32)
    rank_mask = (jnp.arange(RANK, dtype=jnp.int32)[None, None, :] < rank_row[:, :, None]).astype(jnp.float32)[..., None]
    proj_re = jnp.einsum("ijkn,jnr->ijkr", right_re, spec_re) + jnp.einsum("ijkn,jnr->ijkr", right_im, spec_im)
    proj_im = jnp.einsum("ijkn,jnr->ijkr", right_re, spec_im) - jnp.einsum("ijkn,jnr->ijkr", right_im, spec_re)
    proj_re = (proj_re * rank_mask).astype(jnp.bfloat16).astype(jnp.float32)
    proj_im = (proj_im * rank_mask).astype(jnp.bfloat16).astype(jnp.float32)
    out_re = jnp.einsum("ijks,ijkr->ris", left_re, proj_re) - jnp.einsum("ijks,ijkr->ris", left_im, proj_im)
    out_im = jnp.einsum("ijks,ijkr->ris", left_re, proj_im) + jnp.einsum("ijks,ijkr->ris", left_im, proj_re)
    predicted = jnp.stack([out_re, out_im]).reshape(2, RHS, NS)
    residual = predicted - observed
    misfit_low = residual.astype(jnp.bfloat16).astype(jnp.float32).reshape(2, RHS, ROWT, TILE)
    back_re = jnp.einsum("ijks,ris->ijkr", left_re, misfit_low[0]) + jnp.einsum("ijks,ris->ijkr", left_im, misfit_low[1])
    back_im = jnp.einsum("ijks,ris->ijkr", left_re, misfit_low[1]) - jnp.einsum("ijks,ris->ijkr", left_im, misfit_low[0])
    back_re = (back_re * rank_mask).astype(jnp.bfloat16).astype(jnp.float32)
    back_im = (back_im * rank_mask).astype(jnp.bfloat16).astype(jnp.float32)
    grad_re = jnp.einsum("ijkn,ijkr->jnr", right_re, back_re) - jnp.einsum("ijkn,ijkr->jnr", right_im, back_im)
    grad_im = jnp.einsum("ijkn,ijkr->jnr", right_re, back_im) + jnp.einsum("ijkn,ijkr->jnr", right_im, back_re)
    return residual, jnp.stack([grad_re, grad_im]).astype(jnp.bfloat16)


def reference(model, green_left, green_right, ranks, data):
    cosine, sine_neg = tables(NF, NT)
    traces = model.reshape(NR, RHS, NT).astype(jnp.float32)
    spec_re = jnp.einsum("mrt,tq->qmr", traces, cosine.astype(jnp.float32))
    spec_im = jnp.einsum("mrt,tq->qmr", traces, sine_neg.astype(jnp.float32))
    spectrum = jnp.stack([spec_re, spec_im], axis=1).astype(jnp.bfloat16).reshape(NF, 2, NCT, TILE, RHS)
    left_freq = jnp.moveaxis(green_left, 1, 0)
    right_freq = jnp.moveaxis(green_right, 1, 0)
    data_freq = jnp.moveaxis(data.reshape(2, NF, RHS, NS), 1, 0)
    residual, grad_spec = lax.map(per_freq, (left_freq, right_freq, spectrum, ranks, data_freq))
    residual = jnp.moveaxis(residual, 1, 0).reshape(2, NF * RHS, NS)
    grad_spec = grad_spec.reshape(NF, 2, NR, RHS).astype(jnp.float32)
    gradient = jnp.einsum("qmr,tq->mrt", grad_spec[:, 0], cosine.astype(jnp.float32))
    gradient = gradient + jnp.einsum("qmr,tq->mrt", grad_spec[:, 1], sine_neg.astype(jnp.float32))
    gradient = gradient.astype(jnp.bfloat16).reshape(N_RTILE, CW, RHS, NT)
    return residual, gradient
```

```python
import functools
import math

import jax
import jax.numpy as jnp
import numpy as np
from jax import lax
from jax.experimental import pallas as pl
from jax.experimental.pallas import tpu as pltpu
from jax.sharding import PartitionSpec as P

LANES = 128
VMEM_LIMIT = 48 * 1024 * 1024


def tables(count, length):
    freq_bins = 1 + np.arange(count, dtype=np.int32)
    samples = np.arange(length, dtype=np.int32)
    phases = (freq_bins[:, None] * samples[None, :] % length).astype(np.float32)
    phases = phases * np.float32(2.0 * math.pi / length)
    rows = np.concatenate([np.cos(phases), -np.sin(phases)])
    return jnp.asarray(rows.astype(jnp.bfloat16))


def dot(first, second, first_dim, second_dim):
    return lax.dot_general(
        first,
        second,
        (((first_dim,), (second_dim,)), ((), ())),
        preferred_element_type=jnp.float32,
    )


def turned(pair):
    half = pair.shape[1] // 2
    return jnp.concatenate([-pair[:, half:], pair[:, :half]], axis=1)


def spectrum_kernel(table_ref, model_ref, out_ref, rows_ref):
    step = pl.program_id(0)
    high, part, rhs, length = model_ref.shape
    dests, freqs, _, low, lanes = out_ref.shape
    table = table_ref[...]
    bins = table.shape[0]
    for start in range(0, part, 2):
        width = min(2, part - start)
        block = jnp.concatenate(
            [model_ref[:, start + at].reshape(high * rhs, length) for at in range(width)]
        )
        sums = dot(table, block, 1, 1)
        for at in range(width):
            rows = pl.ds((step * part + start + at) * bins, bins)
            rows_ref[rows, :] = sums[:, at * lanes : (at + 1) * lanes]

    @pl.when(step == pl.num_programs(0) - 1)
    def _():
        for dest in range(dests):
            for f in range(freqs):
                for c in range(2):
                    q = c * dests * freqs + dest * freqs + f
                    picked = rows_ref[pl.ds(q, low, stride=bins), :]
                    out_ref[dest, f, c] = picked.astype(out_ref.dtype)


def spectrum_of(model, table, dests, freqs):
    traces, rhs, length = model.shape
    high = LANES // rhs
    low = traces // high
    steps = 4 if low % 4 == 0 else 1
    bins = table.shape[0]
    return pl.pallas_call(
        spectrum_kernel,
        grid=(steps,),
        in_specs=[
            pl.BlockSpec((bins, length), lambda s: (0, 0)),
            pl.BlockSpec((high, low // steps, rhs, length), lambda s: (0, s, 0, 0)),
        ],
        out_specs=pl.BlockSpec((dests, freqs, 2, low, LANES), lambda s: (0, 0, 0, 0, 0)),
        out_shape=jax.ShapeDtypeStruct((dests, freqs, 2, low, LANES), jnp.bfloat16),
        scratch_shapes=[pltpu.VMEM((low * bins, LANES), jnp.float32)],
        compiler_params=pltpu.CompilerParams(vmem_limit_bytes=VMEM_LIMIT),
        name="spectrum",
    )(table, model.reshape(high, low, rhs, length))


def masked(product, ranks_ref, places, size):
    row = lax.broadcasted_iota(jnp.int32, (size, product.shape[1]), 0)
    kept = [
        jnp.where(row < ranks_ref[place], product[at * size : (at + 1) * size], 0.0)
        for at, place in enumerate(places)
    ]
    return [part.astype(jnp.bfloat16) for part in kept]


def predict_kernel(ranks_ref, spec_ref, right_ref, left_ref, out_ref, sum_ref):
    groups, freqs, _, low, lanes = spec_ref.shape
    _, _, row_tiles, col_tiles, size, tile = left_ref.shape
    parts, _, pairs, _ = out_ref.shape
    rhs = parts * pairs // freqs
    high = lanes // rhs
    per_tile = groups // col_tiles
    for f in range(freqs):
        projected = []
        for j in range(col_tiles):
            halves = []
            for c in range(2):
                blocks = []
                for g in range(j * per_tile, (j + 1) * per_tile):
                    got = spec_ref[g, f, c].astype(jnp.float32)
                    blocks += [got[:, h * rhs : (h + 1) * rhs] for h in range(high)]
                halves.append(jnp.concatenate(blocks))
            first = jnp.concatenate(halves, axis=1).astype(jnp.bfloat16)
            second = jnp.concatenate([halves[1], -halves[0]], axis=1).astype(jnp.bfloat16)
            right = [right_ref[c, f, :, j].reshape(row_tiles * size, tile) for c in range(2)]
            product = dot(right[0], first, 1, 0) + dot(right[1], second, 1, 0)
            places = [(f, i, j) for i in range(row_tiles)]
            projected.append(masked(product, ranks_ref, places, size))
        for i in range(row_tiles):
            straight = [projected[j][i] for j in range(col_tiles)]
            factors = jnp.concatenate(straight + [turned(part) for part in straight])
            left = left_ref[:, f, i].reshape(2 * col_tiles * size, tile)
            predicted = dot(factors, left, 0, 0)
            for c in range(2):
                sum_ref[c, f * rhs : (f + 1) * rhs, i * tile : (i + 1) * tile] = predicted[
                    c * rhs : (c + 1) * rhs
                ]
    for part in range(parts):
        for c in range(2):
            out_ref[part, c] = sum_ref[c, part * pairs : (part + 1) * pairs].astype(out_ref.dtype)


def predict(ranks, spectrum, green_right, green_left, parts):
    freqs, row_tiles = ranks.shape[:2]
    tile = green_left.shape[5]
    rhs = LANES * spectrum.shape[0] * spectrum.shape[3] // (green_left.shape[3] * tile)
    pairs = freqs * rhs
    sources = row_tiles * tile
    return pl.pallas_call(
        predict_kernel,
        in_specs=[pl.BlockSpec(memory_space=pltpu.SMEM)]
        + [pl.BlockSpec(memory_space=pltpu.VMEM)] * 3,
        out_specs=pl.BlockSpec(memory_space=pltpu.VMEM),
        out_shape=jax.ShapeDtypeStruct((parts, 2, pairs // parts, sources), jnp.bfloat16),
        scratch_shapes=[pltpu.VMEM((2, pairs, sources), jnp.float32)],
        compiler_params=pltpu.CompilerParams(vmem_limit_bytes=VMEM_LIMIT),
        name="predict",
    )(ranks, spectrum, green_right, green_left)


def back_kernel(ranks_ref, misfit_ref, right_ref, left_ref, out_ref, misfit_all_ref):
    parts, _, pairs, _ = misfit_ref.shape
    _, freqs, row_tiles, col_tiles, size, tile = left_ref.shape
    dests, _, _, low, lanes = out_ref.shape
    rhs = parts * pairs // freqs
    high = lanes // rhs
    per_tile = dests // col_tiles
    for part in range(parts):
        for c in range(2):
            misfit_all_ref[c, part * pairs : (part + 1) * pairs] = misfit_ref[part, c].astype(
                jnp.float32
            )
    for f in range(freqs):
        back = []
        for i in range(row_tiles):
            rows = [
                misfit_all_ref[c, f * rhs : (f + 1) * rhs, i * tile : (i + 1) * tile]
                for c in range(2)
            ]
            first = jnp.concatenate(rows).astype(jnp.bfloat16)
            second = jnp.concatenate([rows[1], -rows[0]]).astype(jnp.bfloat16)
            left = [left_ref[c, f, i].reshape(col_tiles * size, tile) for c in range(2)]
            product = dot(left[0], first, 1, 1) + dot(left[1], second, 1, 1)
            places = [(f, i, j) for j in range(col_tiles)]
            back.append(masked(product, ranks_ref, places, size))
        for j in range(col_tiles):
            straight = [back[i][j] for i in range(row_tiles)]
            factors = jnp.concatenate(straight + [turned(part) for part in straight])
            right = jnp.concatenate(
                [right_ref[c, f, :, j].reshape(row_tiles * size, tile) for c in range(2)]
            )
            grad = dot(factors, right, 0, 0).T
            for at in range(per_tile):
                rows = at * high * low
                for c in range(2):
                    blocks = [
                        grad[rows + h * low : rows + (h + 1) * low, c * rhs : (c + 1) * rhs]
                        for h in range(high)
                    ]
                    out_ref[j * per_tile + at, f, c] = jnp.concatenate(blocks, axis=1).astype(
                        out_ref.dtype
                    )


def back_project(ranks, misfit, green_right, green_left, dests):
    freqs = ranks.shape[0]
    parts, _, pairs, _ = misfit.shape
    rhs = parts * pairs // freqs
    low = green_left.shape[3] * green_left.shape[5] * rhs // (dests * LANES)
    return pl.pallas_call(
        back_kernel,
        in_specs=[pl.BlockSpec(memory_space=pltpu.SMEM)]
        + [pl.BlockSpec(memory_space=pltpu.VMEM)] * 3,
        out_specs=pl.BlockSpec(memory_space=pltpu.VMEM),
        out_shape=jax.ShapeDtypeStruct((dests, freqs, 2, low, LANES), jnp.bfloat16),
        scratch_shapes=[pltpu.VMEM((2, parts * pairs, misfit.shape[3]), jnp.float32)],
        compiler_params=pltpu.CompilerParams(vmem_limit_bytes=VMEM_LIMIT),
        name="back_project",
    )(ranks, misfit, green_right, green_left)


def gradient_kernel(table_ref, parts_ref, out_ref, rows_ref):
    step = pl.program_id(0)
    groups, reps, freqs, _, low, lanes = parts_ref.shape
    high, part, rhs, length = out_ref.shape
    bins = table_ref.shape[0]

    @pl.when(step == 0)
    def _():
        for g in range(groups):
            for f in range(freqs):
                for c in range(2):
                    total = parts_ref[g, 0, f, c].astype(jnp.float32)
                    for rep in range(1, reps):
                        total = total + parts_ref[g, rep, f, c].astype(jnp.float32)
                    rows_ref[pl.ds(c * groups * freqs + g * freqs + f, low, stride=bins), :] = total

    table = table_ref[...]
    for at in range(part):
        coefficients = rows_ref[pl.ds((step * part + at) * bins, bins), :].astype(jnp.bfloat16)
        traces = dot(coefficients, table, 0, 0).astype(out_ref.dtype)
        out_ref[:, at] = traces.reshape(high, rhs, length)


def gradient_of(parts, table, rhs):
    groups, reps, freqs, _, low, lanes = parts.shape
    bins, length = table.shape
    high = lanes // rhs
    steps = 4 if low % 4 == 0 else 1
    out = pl.pallas_call(
        gradient_kernel,
        grid=(steps,),
        in_specs=[
            pl.BlockSpec((bins, length), lambda s: (0, 0)),
            pl.BlockSpec(parts.shape, lambda s: (0,) * 6),
        ],
        out_specs=pl.BlockSpec((high, low // steps, rhs, length), lambda s: (0, s, 0, 0)),
        out_shape=jax.ShapeDtypeStruct((high, low, rhs, length), jnp.bfloat16),
        scratch_shapes=[pltpu.VMEM((low * bins, lanes), jnp.float32)],
        compiler_params=pltpu.CompilerParams(vmem_limit_bytes=VMEM_LIMIT),
        name="gradient",
    )(table, parts)
    return out.reshape(1, high * low, rhs, length)


def shards(model, green_left, green_right, ranks, data):
    freq_count = lax.axis_size("freq")
    tile_count = lax.axis_size("rtile")
    rep_count = lax.axis_size("rep")
    freq_local = ranks.shape[0]
    rhs_count = model.shape[2]
    table = tables(freq_local * freq_count, model.shape[3])
    spectrum = spectrum_of(model[0], table, freq_count, freq_local)
    spectrum = lax.all_to_all(spectrum, "freq", split_axis=0, concat_axis=0, tiled=True)
    predicted = predict(ranks, spectrum, green_right, green_left, tile_count)
    arrived = lax.all_to_all(predicted, "rtile", split_axis=0, concat_axis=0, tiled=True)
    residual = jnp.sum(arrived.astype(jnp.float32), axis=0) - data
    misfit = lax.all_gather(residual.astype(jnp.bfloat16), "rtile", axis=0)
    partial = back_project(ranks, misfit, green_right, green_left, freq_count * rep_count)
    arrived = lax.all_to_all(partial, ("freq", "rep"), split_axis=0, concat_axis=0, tiled=True)
    arrived = arrived.reshape((freq_count, rep_count) + arrived.shape[1:])
    return (residual, gradient_of(arrived, table, rhs_count))


def solution(mesh):
    return jax.shard_map(
        shards,
        mesh=mesh,
        in_specs=(
            P("rtile", "freq", None, None),
            P(None, "freq", "rep", "rtile", None, None),
            P(None, "freq", "rep", "rtile", None, None),
            P("freq", "rep", "rtile"),
            P(None, ("freq", "rtile"), "rep"),
        ),
        out_specs=(P(None, ("freq", "rtile"), "rep"), P("rtile", ("freq", "rep"), None, None)),
        check_vma=False,
    )
```

```python
import functools
import math

import jax
import jax.numpy as jnp
import numpy as np
from jax import lax
from jax.experimental import pallas as pl
from jax.experimental.pallas import tpu as pltpu
from jax.sharding import PartitionSpec as P

LANES = 128
VMEM_LIMIT = 48 * 1024 * 1024


def tables(count, length):
    freq_bins = 1 + np.arange(count, dtype=np.int32)
    samples = np.arange(length, dtype=np.int32)
    phases = (freq_bins[:, None] * samples[None, :] % length).astype(np.float32)
    phases = phases * np.float32(2.0 * math.pi / length)
    rows = np.concatenate([np.cos(phases), -np.sin(phases)])
    return jnp.asarray(rows.astype(jnp.bfloat16))


def dot(first, second, first_dim, second_dim):
    return lax.dot_general(
        first,
        second,
        (((first_dim,), (second_dim,)), ((), ())),
        preferred_element_type=jnp.float32,
    )


def turned(pair):
    half = pair.shape[1] // 2
    return jnp.concatenate([-pair[:, half:], pair[:, :half]], axis=1)


def target(me, step, count):
    return me ^ step if count & (count - 1) == 0 else lax.rem(me + step, count)


def origin(me, step, count):
    return me ^ step if count & (count - 1) == 0 else lax.rem(me + count - step, count)


def exchange(blocks, axis):
    count = len(blocks)
    arrived = [blocks[0]]
    for step in range(1, count):
        pairs = [(me, me ^ step if count & (count - 1) == 0 else (me + step) % count) for me in range(count)]
        arrived.append(lax.ppermute(blocks[step], axis, pairs))
    return arrived


def spectrum_kernel(table_ref, model_ref, *refs):
    out_refs, rows_ref = refs[:-1], refs[-1]
    step = pl.program_id(0)
    high, part, rhs, length = model_ref.shape
    dests = len(out_refs)
    freqs, _, low, lanes = out_refs[0].shape
    table = table_ref[...]
    bins = table.shape[0]
    for start in range(0, part, 2):
        width = min(2, part - start)
        block = jnp.concatenate(
            [model_ref[:, start + at].reshape(high * rhs, length) for at in range(width)]
        )
        sums = dot(table, block, 1, 1)
        for at in range(width):
            rows = pl.ds((step * part + start + at) * bins, bins)
            rows_ref[rows, :] = sums[:, at * lanes : (at + 1) * lanes]

    @pl.when(step == pl.num_programs(0) - 1)
    def _():
        me = lax.axis_index("freq")
        for at, out_ref in enumerate(out_refs):
            dest = target(me, at, dests)
            for f in range(freqs):
                for c in range(2):
                    q = c * dests * freqs + dest * freqs + f
                    picked = rows_ref[pl.ds(q, low, stride=bins), :]
                    out_ref[f, c] = picked.astype(out_ref.dtype)


def spectrum_of(model, table, dests, freqs):
    traces, rhs, length = model.shape
    high = LANES // rhs
    low = traces // high
    steps = 4 if low % 4 == 0 else 1
    bins = table.shape[0]
    return pl.pallas_call(
        spectrum_kernel,
        grid=(steps,),
        in_specs=[
            pl.BlockSpec((bins, length), lambda s: (0, 0)),
            pl.BlockSpec((high, low // steps, rhs, length), lambda s: (0, s, 0, 0)),
        ],
        out_specs=[pl.BlockSpec((freqs, 2, low, LANES), lambda s: (0, 0, 0, 0))] * dests,
        out_shape=[jax.ShapeDtypeStruct((freqs, 2, low, LANES), jnp.bfloat16)] * dests,
        scratch_shapes=[pltpu.VMEM((low * bins, LANES), jnp.float32)],
        compiler_params=pltpu.CompilerParams(vmem_limit_bytes=VMEM_LIMIT),
        name="spectrum",
    )(table, model.reshape(high, low, rhs, length))


def masked(product, ranks_ref, places, size):
    row = lax.broadcasted_iota(jnp.int32, (size, product.shape[1]), 0)
    kept = [
        jnp.where(row < ranks_ref[place], product[at * size : (at + 1) * size], 0.0)
        for at, place in enumerate(places)
    ]
    return [part.astype(jnp.bfloat16) for part in kept]


def spans(first, count, size):
    found = []
    at = first
    while at < first + count:
        length = min(size - at % size, first + count - at)
        found.append((at // size, at % size, length))
        at += length
    return found


def predict_kernel(groups, parts, ranks_ref, right_ref, left_ref, *refs):
    arrived_refs, out_refs = refs[:groups], refs[groups : groups + parts]
    spec_ref, sum_ref = refs[groups + parts :]
    _, freqs, _, low, lanes = spec_ref.shape
    _, _, row_tiles, col_tiles, size, tile = left_ref.shape
    _, pairs, _ = out_refs[0].shape
    me = lax.axis_index("freq")
    for at, arrived_ref in enumerate(arrived_refs):
        spec_ref[origin(me, at, groups)] = arrived_ref[...]
    rhs = parts * pairs // freqs
    high = lanes // rhs
    per_tile = groups // col_tiles
    for f in range(freqs):
        projected = []
        for j in range(col_tiles):
            halves = []
            for c in range(2):
                blocks = []
                for g in range(j * per_tile, (j + 1) * per_tile):
                    got = spec_ref[g, f, c].astype(jnp.float32)
                    blocks += [got[:, h * rhs : (h + 1) * rhs] for h in range(high)]
                halves.append(jnp.concatenate(blocks))
            first = jnp.concatenate(halves, axis=1).astype(jnp.bfloat16)
            second = jnp.concatenate([halves[1], -halves[0]], axis=1).astype(jnp.bfloat16)
            right = [right_ref[c, f, :, j].reshape(row_tiles * size, tile) for c in range(2)]
            product = dot(right[0], first, 1, 0) + dot(right[1], second, 1, 0)
            places = [(f, i, j) for i in range(row_tiles)]
            projected.append(masked(product, ranks_ref, places, size))
        for i in range(row_tiles):
            straight = [projected[j][i] for j in range(col_tiles)]
            factors = jnp.concatenate(straight + [turned(part) for part in straight])
            left = left_ref[:, f, i].reshape(2 * col_tiles * size, tile)
            predicted = dot(factors, left, 0, 0)
            for c in range(2):
                row = c * rhs
                for part, start, length in spans(f * rhs, rhs, pairs):
                    sum_ref[part, c, start : start + length, i * tile : (i + 1) * tile] = predicted[
                        row : row + length
                    ]
                    row += length
    me = lax.axis_index("rtile")
    for at, out_ref in enumerate(out_refs):
        out_ref[...] = sum_ref[target(me, at, parts)].astype(out_ref.dtype)


def predict(ranks, spectrum, green_right, green_left, parts):
    freqs, row_tiles = ranks.shape[:2]
    tile = green_left.shape[5]
    groups = len(spectrum)
    low = spectrum[0].shape[2]
    rhs = LANES * groups * low // (green_left.shape[3] * tile)
    pairs = freqs * rhs
    sources = row_tiles * tile
    return pl.pallas_call(
        functools.partial(predict_kernel, groups, parts),
        in_specs=[pl.BlockSpec(memory_space=pltpu.SMEM)]
        + [pl.BlockSpec(memory_space=pltpu.VMEM)] * (2 + groups),
        out_specs=[pl.BlockSpec(memory_space=pltpu.VMEM)] * parts,
        out_shape=[jax.ShapeDtypeStruct((2, pairs // parts, sources), jnp.bfloat16)] * parts,
        scratch_shapes=[
            pltpu.VMEM((groups,) + spectrum[0].shape, jnp.bfloat16),
            pltpu.VMEM((parts, 2, pairs // parts, sources), jnp.float32),
        ],
        compiler_params=pltpu.CompilerParams(vmem_limit_bytes=VMEM_LIMIT),
        name="predict",
    )(ranks, green_right, green_left, *spectrum)


def back_kernel(parts, dests, ranks_ref, right_ref, left_ref, *refs):
    misfit_refs, out_refs = refs[:parts], refs[parts : parts + dests]
    misfit_all_ref, grad_ref = refs[parts + dests :]
    _, pairs, _ = misfit_refs[0].shape
    _, freqs, row_tiles, col_tiles, size, tile = left_ref.shape
    _, _, low, lanes = out_refs[0].shape
    rhs = parts * pairs // freqs
    high = lanes // rhs
    per_tile = dests // col_tiles
    me = lax.axis_index("rtile")
    for at, misfit_ref in enumerate(misfit_refs):
        misfit_all_ref[origin(me, at, parts)] = misfit_ref[...].astype(jnp.float32)
    for f in range(freqs):
        back = []
        for i in range(row_tiles):
            rows = [
                jnp.concatenate(
                    [
                        misfit_all_ref[part, c, start : start + length, i * tile : (i + 1) * tile]
                        for part, start, length in spans(f * rhs, rhs, pairs)
                    ]
                )
                for c in range(2)
            ]
            first = jnp.concatenate(rows).astype(jnp.bfloat16)
            second = jnp.concatenate([rows[1], -rows[0]]).astype(jnp.bfloat16)
            left = [left_ref[c, f, i].reshape(col_tiles * size, tile) for c in range(2)]
            product = dot(left[0], first, 1, 1) + dot(left[1], second, 1, 1)
            places = [(f, i, j) for j in range(col_tiles)]
            back.append(masked(product, ranks_ref, places, size))
        for j in range(col_tiles):
            straight = [back[i][j] for i in range(row_tiles)]
            factors = jnp.concatenate(straight + [turned(part) for part in straight])
            right = jnp.concatenate(
                [right_ref[c, f, :, j].reshape(row_tiles * size, tile) for c in range(2)]
            )
            grad = dot(factors, right, 0, 0).T
            for at in range(per_tile):
                rows = at * high * low
                for c in range(2):
                    blocks = [
                        grad[rows + h * low : rows + (h + 1) * low, c * rhs : (c + 1) * rhs]
                        for h in range(high)
                    ]
                    grad_ref[j * per_tile + at, f, c] = jnp.concatenate(blocks, axis=1).astype(
                        grad_ref.dtype
                    )
    me = lax.axis_index(("freq", "rep"))
    for at, out_ref in enumerate(out_refs):
        out_ref[...] = grad_ref[target(me, at, dests)]


def back_project(ranks, misfit, green_right, green_left, dests):
    freqs = ranks.shape[0]
    parts = len(misfit)
    _, pairs, sources = misfit[0].shape
    rhs = parts * pairs // freqs
    low = green_left.shape[3] * green_left.shape[5] * rhs // (dests * LANES)
    return pl.pallas_call(
        functools.partial(back_kernel, parts, dests),
        in_specs=[pl.BlockSpec(memory_space=pltpu.SMEM)]
        + [pl.BlockSpec(memory_space=pltpu.VMEM)] * (2 + parts),
        out_specs=[pl.BlockSpec(memory_space=pltpu.VMEM)] * dests,
        out_shape=[jax.ShapeDtypeStruct((freqs, 2, low, LANES), jnp.bfloat16)] * dests,
        scratch_shapes=[
            pltpu.VMEM((parts, 2, pairs, sources), jnp.float32),
            pltpu.VMEM((dests, freqs, 2, low, LANES), jnp.bfloat16),
        ],
        compiler_params=pltpu.CompilerParams(vmem_limit_bytes=VMEM_LIMIT),
        name="back_project",
    )(ranks, green_right, green_left, *misfit)


def gradient_kernel(reps, table_ref, *refs):
    part_refs, out_ref, rows_ref = refs[:-2], refs[-2], refs[-1]
    step = pl.program_id(0)
    groups = len(part_refs) // reps
    freqs, _, low, lanes = part_refs[0].shape
    high, part, rhs, length = out_ref.shape
    bins = table_ref.shape[0]

    @pl.when(step == 0)
    def _():
        me = lax.axis_index("freq")
        for at in range(groups):
            g = origin(me, at, groups)
            for f in range(freqs):
                for c in range(2):
                    total = part_refs[at * reps][f, c].astype(jnp.float32)
                    for rep in range(1, reps):
                        total = total + part_refs[at * reps + rep][f, c].astype(jnp.float32)
                    rows_ref[pl.ds(c * groups * freqs + g * freqs + f, low, stride=bins), :] = total

    table = table_ref[...]
    for at in range(part):
        coefficients = rows_ref[pl.ds((step * part + at) * bins, bins), :].astype(jnp.bfloat16)
        traces = dot(coefficients, table, 0, 0).astype(out_ref.dtype)
        out_ref[:, at] = traces.reshape(high, rhs, length)


def gradient_of(parts, table, rhs, reps):
    freqs, _, low, lanes = parts[0].shape
    bins, length = table.shape
    high = lanes // rhs
    steps = 4 if low % 4 == 0 else 1
    out = pl.pallas_call(
        functools.partial(gradient_kernel, reps),
        grid=(steps,),
        in_specs=[
            pl.BlockSpec((bins, length), lambda s: (0, 0)),
        ]
        + [pl.BlockSpec(parts[0].shape, lambda s: (0, 0, 0, 0))] * len(parts),
        out_specs=pl.BlockSpec((high, low // steps, rhs, length), lambda s: (0, s, 0, 0)),
        out_shape=jax.ShapeDtypeStruct((high, low, rhs, length), jnp.bfloat16),
        scratch_shapes=[pltpu.VMEM((low * bins, lanes), jnp.float32)],
        compiler_params=pltpu.CompilerParams(vmem_limit_bytes=VMEM_LIMIT),
        name="gradient",
    )(table, *parts)
    return out.reshape(1, high * low, rhs, length)


def shards(model, green_left, green_right, ranks, data):
    freq_count = lax.axis_size("freq")
    tile_count = lax.axis_size("rtile")
    rep_count = lax.axis_size("rep")
    freq_local = ranks.shape[0]
    rhs_count = model.shape[2]
    table = tables(freq_local * freq_count, model.shape[3])
    spectrum = spectrum_of(model[0], table, freq_count, freq_local)
    spectrum = exchange(spectrum, "freq")
    predicted = predict(ranks, spectrum, green_right, green_left, tile_count)
    arrived = exchange(predicted, "rtile")
    residual = sum(block.astype(jnp.float32) for block in arrived) - data
    misfit = exchange([residual.astype(jnp.bfloat16)] * tile_count, "rtile")
    partial = back_project(ranks, misfit, green_right, green_left, freq_count * rep_count)
    arrived = exchange(partial, ("freq", "rep"))
    return (residual, gradient_of(arrived, table, rhs_count, rep_count))


def solution(mesh):
    return jax.shard_map(
        shards,
        mesh=mesh,
        in_specs=(
            P("rtile", "freq", None, None),
            P(None, "freq", "rep", "rtile", None, None),
            P(None, "freq", "rep", "rtile", None, None),
            P("freq", "rep", "rtile"),
            P(None, ("freq", "rtile"), "rep"),
        ),
        out_specs=(P(None, ("freq", "rtile"), "rep"), P("rtile", ("freq", "rep"), None, None)),
        check_vma=False,
    )
```

```python
import functools
import math

import jax
import jax.numpy as jnp
import numpy as np
from jax import lax
from jax.experimental import pallas as pl
from jax.experimental.pallas import tpu as pltpu
from jax.sharding import PartitionSpec as P

LANES = 128
VMEM_LIMIT = 48 * 1024 * 1024


def tables(count, length):
    freq_bins = 1 + np.arange(count, dtype=np.int32)
    samples = np.arange(length, dtype=np.int32)
    phases = (freq_bins[:, None] * samples[None, :] % length).astype(np.float32)
    phases = phases * np.float32(2.0 * math.pi / length)
    rows = np.concatenate([np.cos(phases), -np.sin(phases)])
    return rows.astype(jnp.bfloat16)


def wide_table(table):
    bins = table.shape[0]
    return np.pad(table.T, ((0, 0), (0, -bins % LANES)))


def dot(first, second, first_dim, second_dim):
    return lax.dot_general(
        first,
        second,
        (((first_dim,), (second_dim,)), ((), ())),
        preferred_element_type=jnp.float32,
    )


def turned(pair):
    half = pair.shape[1] // 2
    return jnp.concatenate([-pair[:, half:], pair[:, :half]], axis=1)


def target(me, step, count):
    return me ^ step if count & (count - 1) == 0 else lax.rem(me + step, count)


def origin(me, step, count):
    return me ^ step if count & (count - 1) == 0 else lax.rem(me + count - step, count)


def exchange(blocks, axis):
    count = len(blocks)
    arrived = [blocks[0]]
    for step in range(1, count):
        pairs = [(me, me ^ step if count & (count - 1) == 0 else (me + step) % count) for me in range(count)]
        arrived.append(lax.ppermute(blocks[step], axis, pairs))
    return arrived


def spectrum_kernel(table_hbm, model_hbm, *refs):
    out_refs = refs[:-5]
    table_ref, model_ref, rows_ref, table_sem, model_sems = refs[-5:]
    high, low, rhs, length = model_ref.shape
    dests = len(out_refs)
    freqs = out_refs[0].shape[0]
    bins = 2 * dests * freqs
    chunks = model_sems.shape[0]
    part = low // chunks
    own = model_hbm.at[lax.axis_index("rep")]
    table_copy = pltpu.make_async_copy(table_hbm, table_ref, table_sem)
    table_copy.start()
    copies = []
    for at in range(chunks):
        rows = pl.ds(at * part, part)
        copies.append(
            pltpu.make_async_copy(own.at[:, rows], model_ref.at[:, rows], model_sems.at[at])
        )
        copies[-1].start()
    table_copy.wait()
    table = table_ref[...]
    for at in range(chunks):
        copies[at].wait()
        for row in range(at * part, (at + 1) * part):
            block = model_ref[:, row].reshape(high * rhs, length)
            rows_ref[row * bins : (row + 1) * bins] = dot(block, table, 1, 0).T[:bins]
    me = lax.axis_index("freq")
    for at, out_ref in enumerate(out_refs):
        dest = target(me, at, dests)
        for f in range(freqs):
            for c in range(2):
                q = c * dests * freqs + dest * freqs + f
                out_ref[f, c] = rows_ref[pl.ds(q, low, stride=bins), :].astype(out_ref.dtype)


def spectrum_of(model, table, dests, freqs, reps):
    traces, rhs, length = model.shape
    high = LANES // rhs
    low = traces // (reps * high)
    chunks = math.gcd(low, 8)
    bins = 2 * dests * freqs
    return pl.pallas_call(
        spectrum_kernel,
        in_specs=[pl.BlockSpec(memory_space=pltpu.HBM)] * 2,
        out_specs=[pl.BlockSpec(memory_space=pltpu.VMEM)] * dests,
        out_shape=[jax.ShapeDtypeStruct((freqs, 2, low, LANES), jnp.bfloat16)] * dests,
        scratch_shapes=[
            pltpu.VMEM(table.shape, table.dtype),
            pltpu.VMEM((high, low, rhs, length), model.dtype),
            pltpu.VMEM((low * bins, LANES), jnp.float32),
            pltpu.SemaphoreType.DMA,
            pltpu.SemaphoreType.DMA((chunks,)),
        ],
        compiler_params=pltpu.CompilerParams(vmem_limit_bytes=VMEM_LIMIT),
        name="spectrum",
    )(table, model.reshape(reps, high, low, rhs, length))


def masked(product, ranks_ref, places, size):
    row = lax.broadcasted_iota(jnp.int32, (size, product.shape[1]), 0)
    kept = [
        jnp.where(row < ranks_ref[place], product[at * size : (at + 1) * size], 0.0)
        for at, place in enumerate(places)
    ]
    return [part.astype(jnp.bfloat16) for part in kept]


def spans(first, count, size):
    found = []
    at = first
    while at < first + count:
        length = min(size - at % size, first + count - at)
        found.append((at // size, at % size, length))
        at += length
    return found


def predict_kernel(groups, parts, ranks_ref, right_ref, left_ref, *refs):
    arrived_refs, out_refs = refs[:groups], refs[groups : groups + parts]
    spec_ref, sum_ref = refs[groups + parts :]
    _, freqs, _, low, lanes = spec_ref.shape
    _, _, row_tiles, col_tiles, size, tile = left_ref.shape
    _, pairs, _ = out_refs[0].shape
    me = lax.axis_index(("freq", "rep"))
    for at, arrived_ref in enumerate(arrived_refs):
        spec_ref[origin(me, at, groups)] = arrived_ref[...]
    rhs = parts * pairs // freqs
    high = lanes // rhs
    per_tile = groups // col_tiles
    for f in range(freqs):
        projected = []
        for j in range(col_tiles):
            halves = []
            for c in range(2):
                blocks = []
                for g in range(j * per_tile, (j + 1) * per_tile):
                    got = spec_ref[g, f, c].astype(jnp.float32)
                    blocks += [got[:, h * rhs : (h + 1) * rhs] for h in range(high)]
                halves.append(jnp.concatenate(blocks))
            first = jnp.concatenate(halves, axis=1).astype(jnp.bfloat16)
            second = jnp.concatenate([halves[1], -halves[0]], axis=1).astype(jnp.bfloat16)
            right = [right_ref[c, f, :, j].reshape(row_tiles * size, tile) for c in range(2)]
            product = dot(right[0], first, 1, 0) + dot(right[1], second, 1, 0)
            places = [(f, i, j) for i in range(row_tiles)]
            projected.append(masked(product, ranks_ref, places, size))
        for i in range(row_tiles):
            straight = [projected[j][i] for j in range(col_tiles)]
            factors = jnp.concatenate(straight + [turned(part) for part in straight])
            left = left_ref[:, f, i].reshape(2 * col_tiles * size, tile)
            predicted = dot(factors, left, 0, 0)
            for c in range(2):
                row = c * rhs
                for part, start, length in spans(f * rhs, rhs, pairs):
                    sum_ref[part, c, start : start + length, i * tile : (i + 1) * tile] = predicted[
                        row : row + length
                    ]
                    row += length
    me = lax.axis_index("rtile")
    for at, out_ref in enumerate(out_refs):
        out_ref[...] = sum_ref[target(me, at, parts)].astype(out_ref.dtype)


def predict(ranks, spectrum, green_right, green_left, parts):
    freqs, row_tiles = ranks.shape[:2]
    tile = green_left.shape[5]
    groups = len(spectrum)
    low = spectrum[0].shape[2]
    rhs = LANES * groups * low // (green_left.shape[3] * tile)
    pairs = freqs * rhs
    sources = row_tiles * tile
    return pl.pallas_call(
        functools.partial(predict_kernel, groups, parts),
        in_specs=[pl.BlockSpec(memory_space=pltpu.SMEM)]
        + [pl.BlockSpec(memory_space=pltpu.VMEM)] * (2 + groups),
        out_specs=[pl.BlockSpec(memory_space=pltpu.VMEM)] * parts,
        out_shape=[jax.ShapeDtypeStruct((2, pairs // parts, sources), jnp.bfloat16)] * parts,
        scratch_shapes=[
            pltpu.VMEM((groups,) + spectrum[0].shape, jnp.bfloat16),
            pltpu.VMEM((parts, 2, pairs // parts, sources), jnp.float32),
        ],
        compiler_params=pltpu.CompilerParams(vmem_limit_bytes=VMEM_LIMIT),
        name="predict",
    )(ranks, green_right, green_left, *spectrum)


def back_kernel(parts, dests, ranks_ref, right_ref, left_ref, *refs):
    misfit_refs, out_refs = refs[:parts], refs[parts : parts + dests]
    misfit_all_ref, grad_ref = refs[parts + dests :]
    _, pairs, _ = misfit_refs[0].shape
    _, freqs, row_tiles, col_tiles, size, tile = left_ref.shape
    _, _, low, lanes = out_refs[0].shape
    rhs = parts * pairs // freqs
    high = lanes // rhs
    per_tile = dests // col_tiles
    me = lax.axis_index("rtile")
    for at, misfit_ref in enumerate(misfit_refs):
        misfit_all_ref[origin(me, at, parts)] = misfit_ref[...].astype(jnp.float32)
    for f in range(freqs):
        back = []
        for i in range(row_tiles):
            rows = [
                jnp.concatenate(
                    [
                        misfit_all_ref[part, c, start : start + length, i * tile : (i + 1) * tile]
                        for part, start, length in spans(f * rhs, rhs, pairs)
                    ]
                )
                for c in range(2)
            ]
            first = jnp.concatenate(rows).astype(jnp.bfloat16)
            second = jnp.concatenate([rows[1], -rows[0]]).astype(jnp.bfloat16)
            left = [left_ref[c, f, i].reshape(col_tiles * size, tile) for c in range(2)]
            product = dot(left[0], first, 1, 1) + dot(left[1], second, 1, 1)
            places = [(f, i, j) for j in range(col_tiles)]
            back.append(masked(product, ranks_ref, places, size))
        for j in range(col_tiles):
            straight = [back[i][j] for i in range(row_tiles)]
            factors = jnp.concatenate(straight + [turned(part) for part in straight])
            right = jnp.concatenate(
                [right_ref[c, f, :, j].reshape(row_tiles * size, tile) for c in range(2)]
            )
            grad = dot(factors, right, 0, 0).T
            for at in range(per_tile):
                rows = at * high * low
                for c in range(2):
                    blocks = [
                        grad[rows + h * low : rows + (h + 1) * low, c * rhs : (c + 1) * rhs]
                        for h in range(high)
                    ]
                    grad_ref[j * per_tile + at, f, c] = jnp.concatenate(blocks, axis=1).astype(
                        grad_ref.dtype
                    )
    me = lax.axis_index(("freq", "rep"))
    for at, out_ref in enumerate(out_refs):
        out_ref[...] = grad_ref[target(me, at, dests)]


def back_project(ranks, misfit, green_right, green_left, dests):
    freqs = ranks.shape[0]
    parts = len(misfit)
    _, pairs, sources = misfit[0].shape
    rhs = parts * pairs // freqs
    low = green_left.shape[3] * green_left.shape[5] * rhs // (dests * LANES)
    return pl.pallas_call(
        functools.partial(back_kernel, parts, dests),
        in_specs=[pl.BlockSpec(memory_space=pltpu.SMEM)]
        + [pl.BlockSpec(memory_space=pltpu.VMEM)] * (2 + parts),
        out_specs=[pl.BlockSpec(memory_space=pltpu.VMEM)] * dests,
        out_shape=[jax.ShapeDtypeStruct((freqs, 2, low, LANES), jnp.bfloat16)] * dests,
        scratch_shapes=[
            pltpu.VMEM((parts, 2, pairs, sources), jnp.float32),
            pltpu.VMEM((dests, freqs, 2, low, LANES), jnp.bfloat16),
        ],
        compiler_params=pltpu.CompilerParams(vmem_limit_bytes=VMEM_LIMIT),
        name="back_project",
    )(ranks, green_right, green_left, *misfit)


def gradient_kernel(reps, table_hbm, *refs):
    part_refs = refs[:-6]
    out_hbm, table_ref, out_ref, rows_ref, table_sem, out_sems = refs[-6:]
    groups = len(part_refs) // reps
    freqs, _, low, lanes = part_refs[0].shape
    high, _, rhs, length = out_ref.shape
    bins = table_ref.shape[0]
    chunks = out_sems.shape[0]
    part = low // chunks
    table_copy = pltpu.make_async_copy(table_hbm, table_ref, table_sem)
    table_copy.start()
    me = lax.axis_index("freq")
    for at in range(groups):
        g = origin(me, at, groups)
        for f in range(freqs):
            for c in range(2):
                total = part_refs[at * reps][f, c].astype(jnp.float32)
                for rep in range(1, reps):
                    total = total + part_refs[at * reps + rep][f, c].astype(jnp.float32)
                rows_ref[pl.ds(c * groups * freqs + g * freqs + f, low, stride=bins), :] = total
    table_copy.wait()
    table = table_ref[...]
    copies = []
    for at in range(chunks):
        for row in range(at * part, (at + 1) * part):
            coefficients = rows_ref[row * bins : (row + 1) * bins].astype(jnp.bfloat16)
            traces = dot(coefficients, table, 0, 0).astype(out_ref.dtype)
            out_ref[:, row] = traces.reshape(high, rhs, length)
        rows = pl.ds(at * part, part)
        copies.append(
            pltpu.make_async_copy(out_ref.at[:, rows], out_hbm.at[:, rows], out_sems.at[at])
        )
        copies[-1].start()
    for copy in copies:
        copy.wait()


def gradient_of(parts, table, rhs, reps):
    freqs, _, low, lanes = parts[0].shape
    bins, length = table.shape
    high = lanes // rhs
    chunks = math.gcd(low, 8)
    shape = (high, low, rhs, length)
    out = pl.pallas_call(
        functools.partial(gradient_kernel, reps),
        in_specs=[pl.BlockSpec(memory_space=pltpu.HBM)]
        + [pl.BlockSpec(memory_space=pltpu.VMEM)] * len(parts),
        out_specs=pl.BlockSpec(memory_space=pltpu.HBM),
        out_shape=jax.ShapeDtypeStruct(shape, jnp.bfloat16),
        scratch_shapes=[
            pltpu.VMEM(table.shape, table.dtype),
            pltpu.VMEM(shape, jnp.bfloat16),
            pltpu.VMEM((low * bins, lanes), jnp.float32),
            pltpu.SemaphoreType.DMA,
            pltpu.SemaphoreType.DMA((chunks,)),
        ],
        compiler_params=pltpu.CompilerParams(vmem_limit_bytes=VMEM_LIMIT),
        name="gradient",
    )(table, *parts)
    return out.reshape(1, high * low, rhs, length)


def shards(model, green_left, green_right, ranks, data):
    freq_count = lax.axis_size("freq")
    tile_count = lax.axis_size("rtile")
    rep_count = lax.axis_size("rep")
    freq_local = ranks.shape[0]
    rhs_count = model.shape[2]
    table = tables(freq_local * freq_count, model.shape[3])
    spectrum = spectrum_of(model[0], wide_table(table), freq_count, freq_local, rep_count)
    spectrum = exchange([block for block in spectrum for _ in range(rep_count)], ("freq", "rep"))
    predicted = predict(ranks, spectrum, green_right, green_left, tile_count)
    arrived = exchange(predicted, "rtile")
    residual = sum(block.astype(jnp.float32) for block in arrived) - data
    misfit = exchange([residual.astype(jnp.bfloat16)] * tile_count, "rtile")
    partial = back_project(ranks, misfit, green_right, green_left, freq_count * rep_count)
    arrived = exchange(partial, ("freq", "rep"))
    return (residual, gradient_of(arrived, table, rhs_count, rep_count))


def solution(mesh):
    return jax.shard_map(
        shards,
        mesh=mesh,
        in_specs=(
            P("rtile", "freq", None, None),
            P(None, "freq", "rep", "rtile", None, None),
            P(None, "freq", "rep", "rtile", None, None),
            P("freq", "rep", "rtile"),
            P(None, ("freq", "rtile"), "rep"),
        ),
        out_specs=(P(None, ("freq", "rtile"), "rep"), P("rtile", ("freq", "rep"), None, None)),
        check_vma=False,
    )
```

```python
import functools
import math

import jax
import jax.numpy as jnp
from jax import lax
from jax.experimental import pallas as pl
from jax.experimental.pallas import tpu as pltpu
from jax.sharding import PartitionSpec as P

LANES = 128
VMEM_LIMIT = 48 * 1024 * 1024


def tables(rows, bins, length):
    row = lax.broadcasted_iota(jnp.int32, (rows, length), 0)
    sample = lax.broadcasted_iota(jnp.int32, (rows, length), 1)
    is_sine = row >= bins // 2
    freq_bin = jnp.where(is_sine, row - bins // 2, row) + 1
    phase = lax.rem(freq_bin * sample, length) + jnp.where(is_sine, length // 4, 0)
    quarter = lax.div(phase + length // 8, length // 4)
    angle = (phase - quarter * (length // 4)).astype(jnp.float32) * (2.0 * math.pi / length)
    square = angle * angle
    even = 1.0
    odd = 1.0
    for order in (8, 6, 4, 2):
        even = 1.0 - square * even * (1.0 / (order * (order - 1)))
        odd = 1.0 - square * odd * (1.0 / (order * (order + 1)))
    odd = odd * angle
    quarter = quarter & 3
    value = jnp.where((quarter & 1) == 0, even, odd)
    value = jnp.where((quarter == 1) | (quarter == 2), -value, value)
    return jnp.where(row < bins, value, 0.0).astype(jnp.bfloat16)


def dot(first, second, first_dim, second_dim):
    return lax.dot_general(
        first,
        second,
        (((first_dim,), (second_dim,)), ((), ())),
        preferred_element_type=jnp.float32,
    )


def turned(pair):
    half = pair.shape[1] // 2
    return jnp.concatenate([-pair[:, half:], pair[:, :half]], axis=1)


def target(me, step, count):
    return me ^ step if count & (count - 1) == 0 else lax.rem(me + step, count)


def origin(me, step, count):
    return me ^ step if count & (count - 1) == 0 else lax.rem(me + count - step, count)


def exchange(blocks, axis):
    count = len(blocks)
    arrived = [blocks[0]]
    for step in range(1, count):
        pairs = [(me, me ^ step if count & (count - 1) == 0 else (me + step) % count) for me in range(count)]
        arrived.append(lax.ppermute(blocks[step], axis, pairs))
    return arrived


def spectrum_kernel(model_hbm, table_out_ref, *refs):
    out_refs = refs[:-3]
    model_ref, rows_ref, model_sems = refs[-3:]
    high, low, rhs, length = model_ref.shape
    dests = len(out_refs)
    freqs = out_refs[0].shape[0]
    bins = 2 * dests * freqs
    chunks = model_sems.shape[0]
    part = low // chunks
    copies = []
    for at in range(chunks):
        rows = pl.ds(at * part, part)
        copies.append(
            pltpu.make_async_copy(
                model_hbm.at[:, rows], model_ref.at[:, rows], model_sems.at[at]
            )
        )
        copies[-1].start()
    table = tables(LANES, bins, length)
    table_out_ref[...] = table[:bins]
    for at in range(chunks):
        copies[at].wait()
        block = model_ref[:, at * part : (at + 1) * part].reshape(high * part * rhs, length)
        sums = dot(block, table, 1, 1)
        for row in range(part):
            mine = jnp.concatenate(
                [sums[(h * part + row) * rhs : (h * part + row + 1) * rhs] for h in range(high)]
            )
            place = (at * part + row) * bins
            rows_ref[place : place + bins] = mine.T[:bins]
    me = lax.axis_index("freq")
    for at, out_ref in enumerate(out_refs):
        dest = target(me, at, dests)
        for f in range(freqs):
            for c in range(2):
                q = c * dests * freqs + dest * freqs + f
                out_ref[f, c] = rows_ref[pl.ds(q, low, stride=bins), :].astype(out_ref.dtype)


def spectrum_of(model, dests, freqs):
    traces, rhs, length = model.shape
    high = LANES // rhs
    low = traces // high
    chunks = math.gcd(low, 4)
    bins = 2 * dests * freqs
    table, *blocks = pl.pallas_call(
        spectrum_kernel,
        in_specs=[pl.BlockSpec(memory_space=pltpu.HBM)],
        out_specs=[pl.BlockSpec(memory_space=pltpu.VMEM)] * (1 + dests),
        out_shape=[jax.ShapeDtypeStruct((bins, length), jnp.bfloat16)]
        + [jax.ShapeDtypeStruct((freqs, 2, low, LANES), jnp.bfloat16)] * dests,
        scratch_shapes=[
            pltpu.VMEM((high, low, rhs, length), model.dtype),
            pltpu.VMEM((low * bins, LANES), jnp.float32),
            pltpu.SemaphoreType.DMA((chunks,)),
        ],
        compiler_params=pltpu.CompilerParams(vmem_limit_bytes=VMEM_LIMIT),
        name="spectrum",
    )(model.reshape(high, low, rhs, length))
    return table, blocks


def masked(product, ranks_ref, places, size):
    row = lax.broadcasted_iota(jnp.int32, (size, product.shape[1]), 0)
    kept = [
        jnp.where(row < ranks_ref[place], product[at * size : (at + 1) * size], 0.0)
        for at, place in enumerate(places)
    ]
    return [part.astype(jnp.bfloat16) for part in kept]


def spans(first, count, size):
    found = []
    at = first
    while at < first + count:
        length = min(size - at % size, first + count - at)
        found.append((at // size, at % size, length))
        at += length
    return found


def predict_kernel(groups, parts, ranks_ref, right_ref, left_ref, *refs):
    arrived_refs, out_refs = refs[:groups], refs[groups : groups + parts]
    spec_ref, sum_ref = refs[groups + parts :]
    _, freqs, _, low, lanes = spec_ref.shape
    _, _, row_tiles, col_tiles, size, tile = left_ref.shape
    _, pairs, _ = out_refs[0].shape
    me = lax.axis_index("freq")
    for at, arrived_ref in enumerate(arrived_refs):
        spec_ref[origin(me, at, groups)] = arrived_ref[...]
    rhs = parts * pairs // freqs
    high = lanes // rhs
    per_tile = groups // col_tiles
    for f in range(freqs):
        projected = []
        for j in range(col_tiles):
            halves = []
            for c in range(2):
                blocks = []
                for g in range(j * per_tile, (j + 1) * per_tile):
                    got = spec_ref[g, f, c].astype(jnp.float32)
                    blocks += [got[:, h * rhs : (h + 1) * rhs] for h in range(high)]
                halves.append(jnp.concatenate(blocks))
            first = jnp.concatenate(halves, axis=1).astype(jnp.bfloat16)
            second = jnp.concatenate([halves[1], -halves[0]], axis=1).astype(jnp.bfloat16)
            right = [right_ref[c, f, :, j].reshape(row_tiles * size, tile) for c in range(2)]
            product = dot(right[0], first, 1, 0) + dot(right[1], second, 1, 0)
            places = [(f, i, j) for i in range(row_tiles)]
            projected.append(masked(product, ranks_ref, places, size))
        for i in range(row_tiles):
            straight = [projected[j][i] for j in range(col_tiles)]
            factors = jnp.concatenate(straight + [turned(part) for part in straight])
            left = left_ref[:, f, i].reshape(2 * col_tiles * size, tile)
            predicted = dot(factors, left, 0, 0)
            for c in range(2):
                row = c * rhs
                for part, start, length in spans(f * rhs, rhs, pairs):
                    sum_ref[part, c, start : start + length, i * tile : (i + 1) * tile] = predicted[
                        row : row + length
                    ]
                    row += length
    me = lax.axis_index("rtile")
    for at, out_ref in enumerate(out_refs):
        out_ref[...] = sum_ref[target(me, at, parts)].astype(out_ref.dtype)


def predict(ranks, spectrum, green_right, green_left, parts):
    freqs, row_tiles = ranks.shape[:2]
    tile = green_left.shape[5]
    groups = len(spectrum)
    low = spectrum[0].shape[2]
    rhs = LANES * groups * low // (green_left.shape[3] * tile)
    pairs = freqs * rhs
    sources = row_tiles * tile
    return pl.pallas_call(
        functools.partial(predict_kernel, groups, parts),
        in_specs=[pl.BlockSpec(memory_space=pltpu.SMEM)]
        + [pl.BlockSpec(memory_space=pltpu.VMEM)] * (2 + groups),
        out_specs=[pl.BlockSpec(memory_space=pltpu.VMEM)] * parts,
        out_shape=[jax.ShapeDtypeStruct((2, pairs // parts, sources), jnp.bfloat16)] * parts,
        scratch_shapes=[
            pltpu.VMEM((groups,) + spectrum[0].shape, jnp.bfloat16),
            pltpu.VMEM((parts, 2, pairs // parts, sources), jnp.float32),
        ],
        compiler_params=pltpu.CompilerParams(vmem_limit_bytes=VMEM_LIMIT),
        name="predict",
    )(ranks, green_right, green_left, *spectrum)


def back_kernel(parts, groups, reps, ranks_ref, right_ref, left_ref, *refs):
    misfit_refs, out_refs = refs[:parts], refs[parts : parts + reps]
    misfit_all_ref, grad_ref = refs[parts + reps :]
    dests = groups * reps
    _, pairs, _ = misfit_refs[0].shape
    _, freqs, row_tiles, col_tiles, size, tile = left_ref.shape
    _, _, _, low, lanes = out_refs[0].shape
    rhs = parts * pairs // freqs
    high = lanes // rhs
    per_tile = dests // col_tiles
    me = lax.axis_index("rtile")
    for at, misfit_ref in enumerate(misfit_refs):
        misfit_all_ref[origin(me, at, parts)] = misfit_ref[...].astype(jnp.float32)
    for f in range(freqs):
        back = []
        for i in range(row_tiles):
            rows = [
                jnp.concatenate(
                    [
                        misfit_all_ref[part, c, start : start + length, i * tile : (i + 1) * tile]
                        for part, start, length in spans(f * rhs, rhs, pairs)
                    ]
                )
                for c in range(2)
            ]
            first = jnp.concatenate(rows).astype(jnp.bfloat16)
            second = jnp.concatenate([rows[1], -rows[0]]).astype(jnp.bfloat16)
            left = [left_ref[c, f, i].reshape(col_tiles * size, tile) for c in range(2)]
            product = dot(left[0], first, 1, 1) + dot(left[1], second, 1, 1)
            places = [(f, i, j) for j in range(col_tiles)]
            back.append(masked(product, ranks_ref, places, size))
        for j in range(col_tiles):
            straight = [back[i][j] for i in range(row_tiles)]
            factors = jnp.concatenate(straight + [turned(part) for part in straight])
            right = jnp.concatenate(
                [right_ref[c, f, :, j].reshape(row_tiles * size, tile) for c in range(2)]
            )
            grad = dot(factors, right, 0, 0).T
            for at in range(per_tile):
                rows = at * high * low
                for c in range(2):
                    blocks = [
                        grad[rows + h * low : rows + (h + 1) * low, c * rhs : (c + 1) * rhs]
                        for h in range(high)
                    ]
                    grad_ref[j * per_tile + at, f, c] = jnp.concatenate(blocks, axis=1).astype(
                        grad_ref.dtype
                    )
    me, own = lax.axis_index("freq"), lax.axis_index("rep")
    for at, out_ref in enumerate(out_refs):
        rep = target(own, at, reps)
        for step in range(groups):
            out_ref[step] = grad_ref[target(me, step, groups) * reps + rep]


def back_project(ranks, misfit, green_right, green_left, groups, reps):
    dests = groups * reps
    freqs = ranks.shape[0]
    parts = len(misfit)
    _, pairs, sources = misfit[0].shape
    rhs = parts * pairs // freqs
    low = green_left.shape[3] * green_left.shape[5] * rhs // (dests * LANES)
    return pl.pallas_call(
        functools.partial(back_kernel, parts, groups, reps),
        in_specs=[pl.BlockSpec(memory_space=pltpu.SMEM)]
        + [pl.BlockSpec(memory_space=pltpu.VMEM)] * (2 + parts),
        out_specs=[pl.BlockSpec(memory_space=pltpu.VMEM)] * reps,
        out_shape=[jax.ShapeDtypeStruct((groups, freqs, 2, low, LANES), jnp.bfloat16)] * reps,
        scratch_shapes=[
            pltpu.VMEM((parts, 2, pairs, sources), jnp.float32),
            pltpu.VMEM((dests, freqs, 2, low, LANES), jnp.bfloat16),
        ],
        compiler_params=pltpu.CompilerParams(vmem_limit_bytes=VMEM_LIMIT),
        name="back_project",
    )(ranks, green_right, green_left, *misfit)


def gather_kernel(reps, *refs):
    part_refs, out_refs = refs[:reps], refs[reps:]
    for step, out_ref in enumerate(out_refs):
        total = sum(part_ref[step].astype(jnp.float32) for part_ref in part_refs)
        out_ref[...] = total.astype(out_ref.dtype)


def gather(parts):
    shape = parts[0].shape
    return pl.pallas_call(
        functools.partial(gather_kernel, len(parts)),
        in_specs=[pl.BlockSpec(memory_space=pltpu.VMEM)] * len(parts),
        out_specs=[pl.BlockSpec(memory_space=pltpu.VMEM)] * shape[0],
        out_shape=[jax.ShapeDtypeStruct(shape[1:], jnp.bfloat16)] * shape[0],
        compiler_params=pltpu.CompilerParams(vmem_limit_bytes=VMEM_LIMIT),
        name="gather",
    )(*parts)


def gradient_kernel(table_ref, *refs):
    part_refs = refs[:-4]
    out_hbm, out_ref, rows_ref, out_sems = refs[-4:]
    groups = len(part_refs)
    freqs, _, low, lanes = part_refs[0].shape
    high, _, rhs, length = out_ref.shape
    bins = table_ref.shape[0]
    chunks = out_sems.shape[0]
    part = low // chunks
    me = lax.axis_index("freq")
    for at, part_ref in enumerate(part_refs):
        g = origin(me, at, groups)
        for f in range(freqs):
            for c in range(2):
                rows = pl.ds(c * groups * freqs + g * freqs + f, low, stride=bins)
                rows_ref[rows, :] = part_ref[f, c].astype(jnp.float32)
    table = table_ref[...]
    copies = []
    for at in range(chunks):
        coefficients = jnp.concatenate(
            [rows_ref[row * bins : (row + 1) * bins] for row in range(at * part, (at + 1) * part)],
            axis=1,
        ).astype(jnp.bfloat16)
        traces = dot(coefficients, table, 0, 0).astype(out_ref.dtype)
        for row in range(part):
            out_ref[:, at * part + row] = traces[row * lanes : (row + 1) * lanes].reshape(
                high, rhs, length
            )
        rows = pl.ds(at * part, part)
        copies.append(
            pltpu.make_async_copy(out_ref.at[:, rows], out_hbm.at[:, rows], out_sems.at[at])
        )
        copies[-1].start()
    for copy in copies:
        copy.wait()


def gradient_of(parts, table, rhs):
    freqs, _, low, lanes = parts[0].shape
    bins, length = table.shape
    high = lanes // rhs
    chunks = math.gcd(low, 4)
    shape = (high, low, rhs, length)
    out = pl.pallas_call(
        gradient_kernel,
        in_specs=[pl.BlockSpec(memory_space=pltpu.VMEM)] * (1 + len(parts)),
        out_specs=pl.BlockSpec(memory_space=pltpu.HBM),
        out_shape=jax.ShapeDtypeStruct(shape, jnp.bfloat16),
        scratch_shapes=[
            pltpu.VMEM(shape, jnp.bfloat16),
            pltpu.VMEM((low * bins, lanes), jnp.float32),
            pltpu.SemaphoreType.DMA((chunks,)),
        ],
        compiler_params=pltpu.CompilerParams(vmem_limit_bytes=VMEM_LIMIT),
        name="gradient",
    )(table, *parts)
    return out.reshape(1, high * low, rhs, length)


def shards(model, green_left, green_right, ranks, data):
    freq_count = lax.axis_size("freq")
    tile_count = lax.axis_size("rtile")
    rep_count = lax.axis_size("rep")
    freq_local = ranks.shape[0]
    rhs_count = model.shape[2]
    table, spectrum = spectrum_of(model[0], freq_count, freq_local)
    spectrum = exchange(spectrum, "freq")
    predicted = predict(ranks, spectrum, green_right, green_left, tile_count)
    arrived = exchange(predicted, "rtile")
    residual = sum(block.astype(jnp.float32) for block in arrived) - data
    misfit = exchange([residual.astype(jnp.bfloat16)] * tile_count, "rtile")
    partial = back_project(ranks, misfit, green_right, green_left, freq_count, rep_count)
    arrived = exchange(gather(exchange(partial, "rep")), "freq")
    return (residual, gradient_of(arrived, table, rhs_count))


def solution(mesh):
    return jax.shard_map(
        shards,
        mesh=mesh,
        in_specs=(
            P("rtile", "freq", None, None),
            P(None, "freq", "rep", "rtile", None, None),
            P(None, "freq", "rep", "rtile", None, None),
            P("freq", "rep", "rtile"),
            P(None, ("freq", "rtile"), "rep"),
        ),
        out_specs=(P(None, ("freq", "rtile"), "rep"), P("rtile", ("freq", "rep"), None, None)),
        check_vma=False,
    )
```

```python
import functools
import math

import jax
import jax.numpy as jnp
from jax import lax
from jax.experimental import pallas as pl
from jax.experimental.pallas import tpu as pltpu
from jax.sharding import PartitionSpec as P

LANES = 128
VMEM_LIMIT = 48 * 1024 * 1024


def tables(bins, length):
    row = lax.broadcasted_iota(jnp.int32, (bins, length), 0)
    sample = lax.broadcasted_iota(jnp.int32, (bins, length), 1)
    is_sine = row >= bins // 2
    freq_bin = jnp.where(is_sine, row - bins // 2, row) + 1
    phase = lax.rem(freq_bin * sample, length) + jnp.where(is_sine, length // 4, 0)
    quarter = lax.div(phase + length // 8, length // 4)
    angle = (phase - quarter * (length // 4)).astype(jnp.float32) * (2.0 * math.pi / length)
    square = angle * angle
    even = 1.0
    odd = 1.0
    for order in (8, 6, 4, 2):
        even = 1.0 - square * even * (1.0 / (order * (order - 1)))
        odd = 1.0 - square * odd * (1.0 / (order * (order + 1)))
    odd = odd * angle
    quarter = quarter & 3
    value = jnp.where((quarter & 1) == 0, even, odd)
    return jnp.where((quarter == 1) | (quarter == 2), -value, value).astype(jnp.bfloat16)


def dot(first, second, first_dim, second_dim):
    return lax.dot_general(
        first,
        second,
        (((first_dim,), (second_dim,)), ((), ())),
        preferred_element_type=jnp.float32,
    )


def turned(pair):
    half = pair.shape[1] // 2
    return jnp.concatenate([-pair[:, half:], pair[:, :half]], axis=1)


def target(me, step, count):
    return me ^ step if count & (count - 1) == 0 else lax.rem(me + step, count)


def origin(me, step, count):
    return me ^ step if count & (count - 1) == 0 else lax.rem(me + count - step, count)


def exchange(blocks, axis):
    count = len(blocks)
    arrived = [blocks[0]]
    for step in range(1, count):
        pairs = [(me, me ^ step if count & (count - 1) == 0 else (me + step) % count) for me in range(count)]
        arrived.append(lax.ppermute(blocks[step], axis, pairs))
    return arrived


def spectrum_kernel(model_hbm, table_out_ref, *refs):
    out_refs = refs[:-3]
    model_ref, rows_ref, model_sems = refs[-3:]
    high, low, rhs, length = model_ref.shape
    dests = len(out_refs)
    freqs = out_refs[0].shape[0]
    bins = 2 * dests * freqs
    chunks = model_sems.shape[0]
    part = low // chunks
    own = model_hbm.at[lax.axis_index("rep")]
    copies = []
    for at in range(chunks):
        rows = pl.ds(at * part, part)
        copies.append(
            pltpu.make_async_copy(own.at[:, rows], model_ref.at[:, rows], model_sems.at[at])
        )
        copies[-1].start()
    table = tables(bins, length)
    table_out_ref[...] = table
    for at in range(chunks):
        copies[at].wait()
        block = model_ref[:, at * part : (at + 1) * part].reshape(high * part * rhs, length)
        sums = dot(block, table, 1, 1)
        for row in range(part):
            mine = jnp.concatenate(
                [sums[(h * part + row) * rhs : (h * part + row + 1) * rhs] for h in range(high)]
            )
            place = (at * part + row) * bins
            rows_ref[place : place + bins] = mine.T
    me = lax.axis_index("freq")
    for at, out_ref in enumerate(out_refs):
        dest = target(me, at, dests)
        for f in range(freqs):
            for c in range(2):
                q = c * dests * freqs + dest * freqs + f
                out_ref[f, c] = rows_ref[pl.ds(q, low, stride=bins), :].astype(out_ref.dtype)


def spectrum_of(model, dests, freqs, reps):
    traces, rhs, length = model.shape
    high = LANES // rhs
    low = traces // (reps * high)
    chunks = math.gcd(low, 4)
    bins = 2 * dests * freqs
    table, *blocks = pl.pallas_call(
        spectrum_kernel,
        in_specs=[pl.BlockSpec(memory_space=pltpu.HBM)],
        out_specs=[pl.BlockSpec(memory_space=pltpu.VMEM)] * (1 + dests),
        out_shape=[jax.ShapeDtypeStruct((bins, length), jnp.bfloat16)]
        + [jax.ShapeDtypeStruct((freqs, 2, low, LANES), jnp.bfloat16)] * dests,
        scratch_shapes=[
            pltpu.VMEM((high, low, rhs, length), model.dtype),
            pltpu.VMEM((low * bins, LANES), jnp.float32),
            pltpu.SemaphoreType.DMA((chunks,)),
        ],
        compiler_params=pltpu.CompilerParams(vmem_limit_bytes=VMEM_LIMIT),
        name="spectrum",
    )(model.reshape(reps, high, low, rhs, length))
    return table, blocks


def pack_kernel(*refs):
    block_refs, out_ref = refs[:-1], refs[-1]
    me = lax.axis_index("freq")
    for at, block_ref in enumerate(block_refs):
        out_ref[origin(me, at, len(block_refs))] = block_ref[...]


def pack(blocks):
    shape = (len(blocks),) + blocks[0].shape
    return pl.pallas_call(
        pack_kernel,
        in_specs=[pl.BlockSpec(memory_space=pltpu.VMEM)] * len(blocks),
        out_specs=pl.BlockSpec(memory_space=pltpu.VMEM),
        out_shape=jax.ShapeDtypeStruct(shape, blocks[0].dtype),
        compiler_params=pltpu.CompilerParams(vmem_limit_bytes=VMEM_LIMIT),
        name="pack",
    )(*blocks)


def tile_cost(count, size, tile, rhs):
    return pl.CostEstimate(
        flops=count * 2 * 8 * size * tile * rhs,
        bytes_accessed=count * 2 * 4 * size * tile,
        transcendentals=0,
    )


def masked(product, ranks_ref, places, size):
    row = lax.broadcasted_iota(jnp.int32, (size, product.shape[1]), 0)
    kept = [
        jnp.where(row < ranks_ref[place], product[at * size : (at + 1) * size], 0.0)
        for at, place in enumerate(places)
    ]
    return [part.astype(jnp.bfloat16) for part in kept]


def spans(first, count, size):
    found = []
    at = first
    while at < first + count:
        length = min(size - at % size, first + count - at)
        found.append((at // size, at % size, length))
        at += length
    return found


def predict_kernel(reps, parts, tiles, ranks_ref, right_ref, left_ref, *refs):
    arrived_refs, out_refs = refs[:reps], refs[reps : reps + parts]
    spec_ref, sum_ref = refs[reps + parts :]
    _, groups, freqs, _, low, lanes = spec_ref.shape
    col_tiles, size, tile = left_ref.shape[3:]
    first, last = tiles
    row_tiles = last - first
    _, pairs, _ = out_refs[0].shape
    own = lax.axis_index("rep")
    for at, arrived_ref in enumerate(arrived_refs):
        spec_ref[origin(own, at, reps)] = arrived_ref[...]
    rhs = parts * pairs // freqs
    high = lanes // rhs
    per_tile = groups // col_tiles
    for f in range(freqs):
        projected = []
        for j in range(col_tiles):
            halves = []
            for c in range(2):
                blocks = []
                for g in range(j * per_tile, (j + 1) * per_tile):
                    for rep in range(reps):
                        got = spec_ref[rep, g, f, c].astype(jnp.float32)
                        blocks += [got[:, h * rhs : (h + 1) * rhs] for h in range(high)]
                halves.append(jnp.concatenate(blocks))
            straight = jnp.concatenate(halves, axis=1).astype(jnp.bfloat16)
            crossed = jnp.concatenate([halves[1], -halves[0]], axis=1).astype(jnp.bfloat16)
            right = [
                right_ref[c, f, first:last, j].reshape(row_tiles * size, tile) for c in range(2)
            ]
            product = dot(right[0], straight, 1, 0) + dot(right[1], crossed, 1, 0)
            places = [(f, i, j) for i in range(first, last)]
            projected.append(masked(product, ranks_ref, places, size))
        for i in range(row_tiles):
            straight = [projected[j][i] for j in range(col_tiles)]
            factors = jnp.concatenate(straight + [turned(part) for part in straight])
            left = left_ref[:, f, first + i].reshape(2 * col_tiles * size, tile)
            predicted = dot(factors, left, 0, 0)
            for c in range(2):
                row = c * rhs
                for part, start, length in spans(f * rhs, rhs, pairs):
                    sum_ref[part, c, start : start + length, i * tile : (i + 1) * tile] = predicted[
                        row : row + length
                    ]
                    row += length
    me = lax.axis_index("rtile")
    for at, out_ref in enumerate(out_refs):
        out_ref[...] = sum_ref[target(me, at, parts)].astype(out_ref.dtype)


def predict(ranks, spectrum, green_right, green_left, parts, tiles):
    freqs = ranks.shape[0]
    row_tiles = tiles[1] - tiles[0]
    col_tiles, size, tile = green_left.shape[3:]
    reps = len(spectrum)
    groups, _, _, low, _ = spectrum[0].shape
    rhs = LANES * reps * groups * low // (col_tiles * tile)
    pairs = freqs * rhs
    sources = row_tiles * tile
    return pl.pallas_call(
        functools.partial(predict_kernel, reps, parts, tiles),
        in_specs=[pl.BlockSpec(memory_space=pltpu.SMEM)]
        + [pl.BlockSpec(memory_space=pltpu.VMEM)] * (2 + reps),
        out_specs=[pl.BlockSpec(memory_space=pltpu.VMEM)] * parts,
        out_shape=[jax.ShapeDtypeStruct((2, pairs // parts, sources), jnp.bfloat16)] * parts,
        scratch_shapes=[
            pltpu.VMEM((reps,) + spectrum[0].shape, jnp.bfloat16),
            pltpu.VMEM((parts, 2, pairs // parts, sources), jnp.float32),
        ],
        compiler_params=pltpu.CompilerParams(vmem_limit_bytes=VMEM_LIMIT),
        cost_estimate=tile_cost(freqs * row_tiles * col_tiles, size, tile, rhs),
        name="predict",
    )(ranks, green_right, green_left, *spectrum)


def residual_kernel(column, data_ref, *refs):
    block_refs, (misfit_ref, residual_ref) = refs[:-2], refs[-2:]
    observed = data_ref[:, :, column : column + residual_ref.shape[2]]
    residual = sum(block_ref[...].astype(jnp.float32) for block_ref in block_refs) - observed
    residual_ref[...] = residual
    misfit_ref[...] = residual.astype(misfit_ref.dtype)


def residual_of(blocks, data, column):
    shape = blocks[0].shape
    return pl.pallas_call(
        functools.partial(residual_kernel, column),
        in_specs=[pl.BlockSpec(memory_space=pltpu.VMEM)] * (1 + len(blocks)),
        out_specs=[pl.BlockSpec(memory_space=pltpu.VMEM)] * 2,
        out_shape=[
            jax.ShapeDtypeStruct(shape, jnp.bfloat16),
            jax.ShapeDtypeStruct(shape, jnp.float32),
        ],
        compiler_params=pltpu.CompilerParams(vmem_limit_bytes=VMEM_LIMIT),
        name="residual",
    )(data, *blocks)


def back_kernel(parts, groups, reps, tiles, ranks_ref, right_ref, left_ref, *refs):
    first, last = tiles
    _, freqs, row_tiles, col_tiles, size, tile = left_ref.shape
    carried, final = first > 0, last == row_tiles
    misfit_refs, refs = refs[:parts], refs[parts:]
    if carried:
        carried_ref, refs = refs[0], refs[1:]
    dests = groups * reps
    _, pairs, _ = misfit_refs[0].shape
    rhs = parts * pairs // freqs
    if final:
        out_refs, (misfit_all_ref, grad_ref) = refs[:reps], refs[reps:]
        _, _, _, low, lanes = out_refs[0].shape
        high = lanes // rhs
        per_tile = dests // col_tiles
    else:
        carry_ref, misfit_all_ref = refs
    me = lax.axis_index("rtile")
    for at, misfit_ref in enumerate(misfit_refs):
        misfit_all_ref[origin(me, at, parts)] = misfit_ref[...].astype(jnp.float32)
    for f in range(freqs):
        back = []
        for i in range(last - first):
            rows = [
                jnp.concatenate(
                    [
                        misfit_all_ref[part, c, start : start + length, i * tile : (i + 1) * tile]
                        for part, start, length in spans(f * rhs, rhs, pairs)
                    ]
                )
                for c in range(2)
            ]
            straight = jnp.concatenate(rows).astype(jnp.bfloat16)
            crossed = jnp.concatenate([rows[1], -rows[0]]).astype(jnp.bfloat16)
            left = [left_ref[c, f, first + i].reshape(col_tiles * size, tile) for c in range(2)]
            product = dot(left[0], straight, 1, 1) + dot(left[1], crossed, 1, 1)
            places = [(f, first + i, j) for j in range(col_tiles)]
            back.append(masked(product, ranks_ref, places, size))
        for j in range(col_tiles):
            straight = [part[j] for part in back]
            factors = jnp.concatenate(straight + [turned(part) for part in straight])
            right = jnp.concatenate(
                [
                    right_ref[c, f, first:last, j].reshape((last - first) * size, tile)
                    for c in range(2)
                ]
            )
            grad = dot(factors, right, 0, 0)
            if carried:
                grad = grad + carried_ref[f, j]
            if not final:
                carry_ref[f, j] = grad
                continue
            grad = grad.T
            for at in range(per_tile):
                rows = at * high * low
                for c in range(2):
                    blocks = [
                        grad[rows + h * low : rows + (h + 1) * low, c * rhs : (c + 1) * rhs]
                        for h in range(high)
                    ]
                    grad_ref[j * per_tile + at, f, c] = jnp.concatenate(blocks, axis=1).astype(
                        grad_ref.dtype
                    )
    if not final:
        return
    me, own = lax.axis_index("freq"), lax.axis_index("rep")
    for at, out_ref in enumerate(out_refs):
        rep = target(own, at, reps)
        for step in range(groups):
            out_ref[step] = grad_ref[target(me, step, groups) * reps + rep]


def back_project(ranks, misfit, green_right, green_left, groups, reps, tiles, carried):
    freqs = ranks.shape[0]
    parts = len(misfit)
    _, pairs, sources = misfit[0].shape
    row_tiles, col_tiles, size, tile = green_left.shape[2:]
    rhs = parts * pairs // freqs
    final = tiles[1] == row_tiles
    scratch = [pltpu.VMEM((parts, 2, pairs, sources), jnp.float32)]
    if final:
        low = col_tiles * tile * rhs // (groups * reps * LANES)
        block = (freqs, 2, low, LANES)
        out_shape = [jax.ShapeDtypeStruct((groups,) + block, jnp.bfloat16)] * reps
        scratch.append(pltpu.VMEM((groups * reps,) + block, jnp.bfloat16))
    else:
        out_shape = [jax.ShapeDtypeStruct((freqs, col_tiles, 2 * rhs, tile), jnp.float32)]
    return pl.pallas_call(
        functools.partial(back_kernel, parts, groups, reps, tiles),
        in_specs=[pl.BlockSpec(memory_space=pltpu.SMEM)]
        + [pl.BlockSpec(memory_space=pltpu.VMEM)] * (2 + parts + len(carried)),
        out_specs=[pl.BlockSpec(memory_space=pltpu.VMEM)] * len(out_shape),
        out_shape=out_shape,
        scratch_shapes=scratch,
        compiler_params=pltpu.CompilerParams(vmem_limit_bytes=VMEM_LIMIT),
        cost_estimate=tile_cost(freqs * (tiles[1] - tiles[0]) * col_tiles, size, tile, rhs),
        name="back_project",
    )(ranks, green_right, green_left, *misfit, *carried)


def gather_kernel(reps, *refs):
    part_refs, out_refs = refs[:reps], refs[reps:]
    for step, out_ref in enumerate(out_refs):
        total = sum(part_ref[step].astype(jnp.float32) for part_ref in part_refs)
        out_ref[...] = total.astype(out_ref.dtype)


def gather(parts):
    shape = parts[0].shape
    return pl.pallas_call(
        functools.partial(gather_kernel, len(parts)),
        in_specs=[pl.BlockSpec(memory_space=pltpu.VMEM)] * len(parts),
        out_specs=[pl.BlockSpec(memory_space=pltpu.VMEM)] * shape[0],
        out_shape=[jax.ShapeDtypeStruct(shape[1:], jnp.bfloat16)] * shape[0],
        compiler_params=pltpu.CompilerParams(vmem_limit_bytes=VMEM_LIMIT),
        name="gather",
    )(*parts)


def gradient_kernel(table_ref, *refs):
    part_refs = refs[:-4]
    out_hbm, out_ref, rows_ref, out_sems = refs[-4:]
    groups = len(part_refs)
    freqs, _, low, lanes = part_refs[0].shape
    high, _, rhs, length = out_ref.shape
    bins = table_ref.shape[0]
    chunks = out_sems.shape[0]
    part = low // chunks
    me = lax.axis_index("freq")
    for at, part_ref in enumerate(part_refs):
        g = origin(me, at, groups)
        for f in range(freqs):
            for c in range(2):
                rows = pl.ds(c * groups * freqs + g * freqs + f, low, stride=bins)
                rows_ref[rows, :] = part_ref[f, c].astype(jnp.float32)
    table = table_ref[...]
    copies = []
    for at in range(chunks):
        coefficients = jnp.concatenate(
            [rows_ref[row * bins : (row + 1) * bins] for row in range(at * part, (at + 1) * part)],
            axis=1,
        ).astype(jnp.bfloat16)
        traces = dot(coefficients, table, 0, 0).astype(out_ref.dtype)
        for row in range(part):
            out_ref[:, at * part + row] = traces[row * lanes : (row + 1) * lanes].reshape(
                high, rhs, length
            )
        rows = pl.ds(at * part, part)
        copies.append(
            pltpu.make_async_copy(out_ref.at[:, rows], out_hbm.at[:, rows], out_sems.at[at])
        )
        copies[-1].start()
    for copy in copies:
        copy.wait()


def gradient_of(parts, table, rhs):
    freqs, _, low, lanes = parts[0].shape
    bins, length = table.shape
    high = lanes // rhs
    chunks = math.gcd(low, 4)
    shape = (high, low, rhs, length)
    out = pl.pallas_call(
        gradient_kernel,
        in_specs=[pl.BlockSpec(memory_space=pltpu.VMEM)] * (1 + len(parts)),
        out_specs=pl.BlockSpec(memory_space=pltpu.HBM),
        out_shape=jax.ShapeDtypeStruct(shape, jnp.bfloat16),
        scratch_shapes=[
            pltpu.VMEM(shape, jnp.bfloat16),
            pltpu.VMEM((low * bins, lanes), jnp.float32),
            pltpu.SemaphoreType.DMA((chunks,)),
        ],
        compiler_params=pltpu.CompilerParams(vmem_limit_bytes=VMEM_LIMIT),
        name="gradient",
    )(table, *parts)
    return out.reshape(1, high * low, rhs, length)


def shards(model, green_left, green_right, ranks, data):
    freq_count = lax.axis_size("freq")
    tile_count = lax.axis_size("rtile")
    rep_count = lax.axis_size("rep")
    freq_local = ranks.shape[0]
    rhs_count = model.shape[2]
    table, spectrum = spectrum_of(model[0], freq_count, freq_local, rep_count)
    spectrum = pack(exchange(spectrum, "freq"))
    spectrum = exchange([spectrum] * rep_count, "rep")
    row_tiles, _, _, tile = green_left.shape[2:]
    halves = [(0, row_tiles // 2), (row_tiles // 2, row_tiles)]
    predicted = [
        predict(ranks, spectrum, green_right, green_left, tile_count, tiles) for tiles in halves
    ]
    arrived = [exchange(blocks, "rtile") for blocks in predicted]
    pairs = [
        residual_of(blocks, data, first * tile) for blocks, (first, _) in zip(arrived, halves)
    ]
    misfit = [exchange([half] * tile_count, "rtile") for half, _ in pairs]
    residual = [half for _, half in pairs]
    partial = []
    for blocks, tiles in zip(misfit, halves):
        partial = back_project(
            ranks, blocks, green_right, green_left, freq_count, rep_count, tiles, partial
        )
    arrived = exchange(gather(exchange(partial, "rep")), "freq")
    return (jnp.concatenate(residual, axis=2), gradient_of(arrived, table, rhs_count))


def solution(mesh):
    return jax.shard_map(
        shards,
        mesh=mesh,
        in_specs=(
            P("rtile", "freq", None, None),
            P(None, "freq", "rep", "rtile", None, None),
            P(None, "freq", "rep", "rtile", None, None),
            P("freq", "rep", "rtile"),
            P(None, ("freq", "rtile"), "rep"),
        ),
        out_specs=(P(None, ("freq", "rtile"), "rep"), P("rtile", ("freq", "rep"), None, None)),
        check_vma=False,
    )
```

```python
import functools
import math

import jax
import jax.numpy as jnp
from jax import lax
from jax.experimental import pallas as pl
from jax.experimental.pallas import tpu as pltpu
from jax.sharding import PartitionSpec as P

LANES = 128
VMEM_LIMIT = 48 * 1024 * 1024


def tables(bins, length):
    row = lax.broadcasted_iota(jnp.int32, (bins, length), 0)
    sample = lax.broadcasted_iota(jnp.int32, (bins, length), 1)
    is_sine = row >= bins // 2
    freq_bin = jnp.where(is_sine, row - bins // 2, row) + 1
    phase = lax.rem(freq_bin * sample, length) + jnp.where(is_sine, length // 4, 0)
    quarter = lax.div(phase + length // 8, length // 4)
    angle = (phase - quarter * (length // 4)).astype(jnp.float32) * (2.0 * math.pi / length)
    square = angle * angle
    even = 1.0
    odd = 1.0
    for order in (8, 6, 4, 2):
        even = 1.0 - square * even * (1.0 / (order * (order - 1)))
        odd = 1.0 - square * odd * (1.0 / (order * (order + 1)))
    odd = odd * angle
    quarter = quarter & 3
    value = jnp.where((quarter & 1) == 0, even, odd)
    return jnp.where((quarter == 1) | (quarter == 2), -value, value).astype(jnp.bfloat16)


def dot(first, second, first_dim, second_dim):
    return lax.dot_general(
        first,
        second,
        (((first_dim,), (second_dim,)), ((), ())),
        preferred_element_type=jnp.float32,
    )


def turned(pair):
    half = pair.shape[1] // 2
    return jnp.concatenate([-pair[:, half:], pair[:, :half]], axis=1)


def target(me, step, count):
    return me ^ step if count & (count - 1) == 0 else lax.rem(me + step, count)


def origin(me, step, count):
    return me ^ step if count & (count - 1) == 0 else lax.rem(me + count - step, count)


def exchange(blocks, axis):
    count = len(blocks)
    arrived = []
    for step in range(count - 1, 0, -1):
        pairs = [(me, me ^ step if count & (count - 1) == 0 else (me + step) % count) for me in range(count)]
        arrived.append(lax.ppermute(blocks[step], axis, pairs))
    return [blocks[0]] + arrived[::-1]


def spectrum_kernel(model_hbm, table_out_ref, *refs):
    out_refs = refs[:-3]
    model_ref, rows_ref, model_sems = refs[-3:]
    high, low, rhs, length = model_ref.shape
    dests = len(out_refs)
    freqs = out_refs[0].shape[0]
    bins = 2 * dests * freqs
    chunks = model_sems.shape[0]
    part = low // chunks
    own = model_hbm.at[lax.axis_index("rep")]
    copies = []
    for at in range(chunks):
        rows = pl.ds(at * part, part)
        copies.append(
            [
                pltpu.make_async_copy(
                    own.at[h, rows], model_ref.at[h, rows], model_sems.at[at, h]
                )
                for h in range(high)
            ]
        )
        for copy in copies[-1]:
            copy.start()
    table = tables(bins, length)
    table_out_ref[...] = table
    for at in range(chunks):
        for copy in copies[at]:
            copy.wait()
        block = model_ref[:, at * part : (at + 1) * part].reshape(high * part * rhs, length)
        sums = dot(block, table, 1, 1)
        for row in range(part):
            mine = jnp.concatenate(
                [sums[(h * part + row) * rhs : (h * part + row + 1) * rhs] for h in range(high)]
            )
            place = (at * part + row) * bins
            rows_ref[place : place + bins] = mine.T
    me = lax.axis_index("freq")
    for at, out_ref in enumerate(out_refs):
        dest = target(me, at, dests)
        for f in range(freqs):
            for c in range(2):
                q = c * dests * freqs + dest * freqs + f
                out_ref[f, c] = rows_ref[pl.ds(q, low, stride=bins), :].astype(out_ref.dtype)


def spectrum_of(model, dests, freqs, reps):
    traces, rhs, length = model.shape
    high = LANES // rhs
    low = traces // (reps * high)
    chunks = math.gcd(low, 4)
    bins = 2 * dests * freqs
    table, *blocks = pl.pallas_call(
        spectrum_kernel,
        in_specs=[pl.BlockSpec(memory_space=pltpu.HBM)],
        out_specs=[pl.BlockSpec(memory_space=pltpu.VMEM)] * (1 + dests),
        out_shape=[jax.ShapeDtypeStruct((bins, length), jnp.bfloat16)]
        + [jax.ShapeDtypeStruct((freqs, 2, low, LANES), jnp.bfloat16)] * dests,
        scratch_shapes=[
            pltpu.VMEM((high, low, rhs, length), model.dtype),
            pltpu.VMEM((low * bins, LANES), jnp.float32),
            pltpu.SemaphoreType.DMA((chunks, high)),
        ],
        compiler_params=pltpu.CompilerParams(vmem_limit_bytes=VMEM_LIMIT),
        name="spectrum",
    )(model.reshape(reps, high, low, rhs, length))
    return table, blocks


def pack_kernel(*refs):
    block_refs, out_ref = refs[:-1], refs[-1]
    me = lax.axis_index("freq")
    for at, block_ref in enumerate(block_refs):
        out_ref[origin(me, at, len(block_refs))] = block_ref[...]


def pack(blocks):
    shape = (len(blocks),) + blocks[0].shape
    return pl.pallas_call(
        pack_kernel,
        in_specs=[pl.BlockSpec(memory_space=pltpu.VMEM)] * len(blocks),
        out_specs=pl.BlockSpec(memory_space=pltpu.VMEM),
        out_shape=jax.ShapeDtypeStruct(shape, blocks[0].dtype),
        compiler_params=pltpu.CompilerParams(vmem_limit_bytes=VMEM_LIMIT),
        name="pack",
    )(*blocks)


def tile_cost(count, size, tile, rhs):
    return pl.CostEstimate(
        flops=count * 2 * 8 * size * tile * rhs,
        bytes_accessed=count * 2 * 4 * size * tile,
        transcendentals=0,
    )


def masked(product, limits_ref, places, size):
    columns = product.shape[1]
    row = lax.broadcasted_iota(jnp.int32, (size, columns), 0)
    kept = [
        jnp.where(row < limits_ref[place][:, :columns], product[at * size : (at + 1) * size], 0.0)
        for at, place in enumerate(places)
    ]
    return [part.astype(jnp.bfloat16) for part in kept]


def spans(first, count, size):
    found = []
    at = first
    while at < first + count:
        length = min(size - at % size, first + count - at)
        found.append((at // size, at % size, length))
        at += length
    return found


def predict_kernel(reps, parts, limits_ref, right_ref, left_ref, *refs):
    arrived_refs, out_refs = refs[:reps], refs[reps : reps + parts]
    spec_ref, sum_ref = refs[reps + parts :]
    _, groups, freqs, _, low, lanes = spec_ref.shape
    row_tiles, col_tiles, size, tile = left_ref.shape[2:]
    _, pairs, _ = out_refs[0].shape
    own = lax.axis_index("rep")
    for at, arrived_ref in enumerate(arrived_refs):
        spec_ref[origin(own, at, reps)] = arrived_ref[...]
    rhs = parts * pairs // freqs
    high = lanes // rhs
    per_tile = groups // col_tiles
    for f in range(freqs):
        projected = []
        for j in range(col_tiles):
            halves = []
            for c in range(2):
                blocks = []
                for g in range(j * per_tile, (j + 1) * per_tile):
                    for rep in range(reps):
                        got = spec_ref[rep, g, f, c].astype(jnp.float32)
                        blocks += [got[:, h * rhs : (h + 1) * rhs] for h in range(high)]
                halves.append(jnp.concatenate(blocks))
            straight = jnp.concatenate(halves, axis=1).astype(jnp.bfloat16)
            crossed = jnp.concatenate([halves[1], -halves[0]], axis=1).astype(jnp.bfloat16)
            right = [right_ref[c, f, :, j].reshape(row_tiles * size, tile) for c in range(2)]
            product = dot(right[0], straight, 1, 0) + dot(right[1], crossed, 1, 0)
            places = [(f, i, j) for i in range(row_tiles)]
            projected.append(masked(product, limits_ref, places, size))
        for i in range(row_tiles):
            straight = [projected[j][i] for j in range(col_tiles)]
            factors = jnp.concatenate(straight + [turned(part) for part in straight])
            left = left_ref[:, f, i].reshape(2 * col_tiles * size, tile)
            predicted = dot(factors, left, 0, 0)
            for c in range(2):
                row = c * rhs
                for part, start, length in spans(f * rhs, rhs, pairs):
                    sum_ref[part, c, start : start + length, i * tile : (i + 1) * tile] = predicted[
                        row : row + length
                    ]
                    row += length
    me = lax.axis_index("rtile")
    for at, out_ref in enumerate(out_refs):
        out_ref[...] = sum_ref[target(me, at, parts)].astype(out_ref.dtype)


def predict(limits, spectrum, green_right, green_left, parts):
    freqs, row_tiles, col_tiles, size, tile = green_left.shape[1:]
    reps = len(spectrum)
    groups, _, _, low, _ = spectrum[0].shape
    rhs = LANES * reps * groups * low // (col_tiles * tile)
    pairs = freqs * rhs
    sources = row_tiles * tile
    return pl.pallas_call(
        functools.partial(predict_kernel, reps, parts),
        in_specs=[pl.BlockSpec(memory_space=pltpu.VMEM)] * (3 + reps),
        out_specs=[pl.BlockSpec(memory_space=pltpu.VMEM)] * parts,
        out_shape=[jax.ShapeDtypeStruct((2, pairs // parts, sources), jnp.bfloat16)] * parts,
        scratch_shapes=[
            pltpu.VMEM((reps,) + spectrum[0].shape, jnp.bfloat16),
            pltpu.VMEM((parts, 2, pairs // parts, sources), jnp.float32),
        ],
        compiler_params=pltpu.CompilerParams(vmem_limit_bytes=VMEM_LIMIT),
        cost_estimate=tile_cost(freqs * row_tiles * col_tiles, size, tile, rhs),
        name="predict",
    )(limits, green_right, green_left, *spectrum)


def residual_kernel(data_ref, *refs):
    block_refs, (misfit_ref, residual_ref) = refs[:-2], refs[-2:]
    residual = sum(block_ref[...].astype(jnp.float32) for block_ref in block_refs) - data_ref[...]
    residual_ref[...] = residual
    misfit_ref[...] = residual.astype(misfit_ref.dtype)


def residual_of(blocks, data):
    shape = blocks[0].shape
    return pl.pallas_call(
        residual_kernel,
        in_specs=[pl.BlockSpec(memory_space=pltpu.VMEM)] * (1 + len(blocks)),
        out_specs=[pl.BlockSpec(memory_space=pltpu.VMEM)] * 2,
        out_shape=[
            jax.ShapeDtypeStruct(shape, jnp.bfloat16),
            jax.ShapeDtypeStruct(shape, jnp.float32),
        ],
        compiler_params=pltpu.CompilerParams(vmem_limit_bytes=VMEM_LIMIT),
        name="residual",
    )(data, *blocks)


def back_kernel(parts, groups, reps, limits_ref, right_ref, left_ref, *refs):
    misfit_refs, out_refs = refs[:parts], refs[parts : parts + reps]
    misfit_all_ref, grad_ref = refs[parts + reps :]
    _, freqs, row_tiles, col_tiles, size, tile = left_ref.shape
    _, pairs, _ = misfit_refs[0].shape
    rhs = parts * pairs // freqs
    _, _, _, low, lanes = out_refs[0].shape
    high = lanes // rhs
    per_tile = groups * reps // col_tiles
    me = lax.axis_index("rtile")
    for at, misfit_ref in enumerate(misfit_refs):
        misfit_all_ref[origin(me, at, parts)] = misfit_ref[...].astype(jnp.float32)
    for f in range(freqs):
        back = []
        for i in range(row_tiles):
            rows = [
                jnp.concatenate(
                    [
                        misfit_all_ref[part, c, start : start + length, i * tile : (i + 1) * tile]
                        for part, start, length in spans(f * rhs, rhs, pairs)
                    ]
                )
                for c in range(2)
            ]
            straight = jnp.concatenate(rows).astype(jnp.bfloat16)
            crossed = jnp.concatenate([rows[1], -rows[0]]).astype(jnp.bfloat16)
            left = [left_ref[c, f, i].reshape(col_tiles * size, tile) for c in range(2)]
            product = dot(left[0], straight, 1, 1) + dot(left[1], crossed, 1, 1)
            places = [(f, i, j) for j in range(col_tiles)]
            back.append(masked(product, limits_ref, places, size))
        for j in range(col_tiles):
            straight = [part[j] for part in back]
            factors = jnp.concatenate(straight + [turned(part) for part in straight])
            right = jnp.concatenate(
                [right_ref[c, f, :, j].reshape(row_tiles * size, tile) for c in range(2)]
            )
            grad = dot(factors, right, 0, 0).T
            for at in range(per_tile):
                rows = at * high * low
                for c in range(2):
                    blocks = [
                        grad[rows + h * low : rows + (h + 1) * low, c * rhs : (c + 1) * rhs]
                        for h in range(high)
                    ]
                    grad_ref[j * per_tile + at, f, c] = jnp.concatenate(blocks, axis=1).astype(
                        grad_ref.dtype
                    )
    me, own = lax.axis_index("freq"), lax.axis_index("rep")
    for at, out_ref in enumerate(out_refs):
        rep = target(own, at, reps)
        for step in range(groups):
            out_ref[step] = grad_ref[target(me, step, groups) * reps + rep]


def back_project(limits, misfit, green_right, green_left, groups, reps):
    parts = len(misfit)
    _, pairs, sources = misfit[0].shape
    freqs, row_tiles, col_tiles, size, tile = green_left.shape[1:]
    rhs = parts * pairs // freqs
    low = col_tiles * tile * rhs // (groups * reps * LANES)
    block = (freqs, 2, low, LANES)
    return pl.pallas_call(
        functools.partial(back_kernel, parts, groups, reps),
        in_specs=[pl.BlockSpec(memory_space=pltpu.VMEM)] * (3 + parts),
        out_specs=[pl.BlockSpec(memory_space=pltpu.VMEM)] * reps,
        out_shape=[jax.ShapeDtypeStruct((groups,) + block, jnp.bfloat16)] * reps,
        scratch_shapes=[
            pltpu.VMEM((parts, 2, pairs, sources), jnp.float32),
            pltpu.VMEM((groups * reps,) + block, jnp.bfloat16),
        ],
        compiler_params=pltpu.CompilerParams(vmem_limit_bytes=VMEM_LIMIT),
        cost_estimate=tile_cost(freqs * row_tiles * col_tiles, size, tile, rhs),
        name="back_project",
    )(limits, green_right, green_left, *misfit)


def gather_kernel(reps, *refs):
    part_refs, out_refs = refs[:reps], refs[reps:]
    for step, out_ref in enumerate(out_refs):
        total = sum(part_ref[step].astype(jnp.float32) for part_ref in part_refs)
        out_ref[...] = total.astype(out_ref.dtype)


def gather(parts):
    shape = parts[0].shape
    return pl.pallas_call(
        functools.partial(gather_kernel, len(parts)),
        in_specs=[pl.BlockSpec(memory_space=pltpu.VMEM)] * len(parts),
        out_specs=[pl.BlockSpec(memory_space=pltpu.VMEM)] * shape[0],
        out_shape=[jax.ShapeDtypeStruct(shape[1:], jnp.bfloat16)] * shape[0],
        compiler_params=pltpu.CompilerParams(vmem_limit_bytes=VMEM_LIMIT),
        name="gather",
    )(*parts)


def gradient_kernel(table_ref, *refs):
    part_refs = refs[:-4]
    out_hbm, out_ref, rows_ref, out_sems = refs[-4:]
    groups = len(part_refs)
    freqs, _, low, lanes = part_refs[0].shape
    high, _, rhs, length = out_ref.shape
    bins = table_ref.shape[0]
    chunks = out_sems.shape[0]
    part = low // chunks
    me = lax.axis_index("freq")
    for at, part_ref in enumerate(part_refs):
        g = origin(me, at, groups)
        for f in range(freqs):
            for c in range(2):
                rows = pl.ds(c * groups * freqs + g * freqs + f, low, stride=bins)
                rows_ref[rows, :] = part_ref[f, c].astype(jnp.float32)
    table = table_ref[...]
    copies = []
    for at in range(chunks):
        coefficients = jnp.concatenate(
            [rows_ref[row * bins : (row + 1) * bins] for row in range(at * part, (at + 1) * part)],
            axis=1,
        ).astype(jnp.bfloat16)
        traces = dot(coefficients, table, 0, 0).astype(out_ref.dtype)
        for row in range(part):
            out_ref[:, at * part + row] = traces[row * lanes : (row + 1) * lanes].reshape(
                high, rhs, length
            )
        rows = pl.ds(at * part, part)
        for h in range(high):
            copies.append(
                pltpu.make_async_copy(
                    out_ref.at[h, rows], out_hbm.at[h, rows], out_sems.at[at, h]
                )
            )
            copies[-1].start()
    for copy in copies:
        copy.wait()


def gradient_of(parts, table, rhs):
    freqs, _, low, lanes = parts[0].shape
    bins, length = table.shape
    high = lanes // rhs
    chunks = math.gcd(low, 4)
    shape = (high, low, rhs, length)
    out = pl.pallas_call(
        gradient_kernel,
        in_specs=[pl.BlockSpec(memory_space=pltpu.VMEM)] * (1 + len(parts)),
        out_specs=pl.BlockSpec(memory_space=pltpu.HBM),
        out_shape=jax.ShapeDtypeStruct(shape, jnp.bfloat16),
        scratch_shapes=[
            pltpu.VMEM(shape, jnp.bfloat16),
            pltpu.VMEM((low * bins, lanes), jnp.float32),
            pltpu.SemaphoreType.DMA((chunks, high)),
        ],
        compiler_params=pltpu.CompilerParams(vmem_limit_bytes=VMEM_LIMIT),
        name="gradient",
    )(table, *parts)
    return out.reshape(1, high * low, rhs, length)


def shards(model, green_left, green_right, ranks, data):
    freq_count = lax.axis_size("freq")
    tile_count = lax.axis_size("rtile")
    rep_count = lax.axis_size("rep")
    freq_local = ranks.shape[0]
    rhs_count = model.shape[2]
    table, spectrum = spectrum_of(model[0], freq_count, freq_local, rep_count)
    spectrum = pack(exchange(spectrum, "freq"))
    spectrum = exchange([spectrum] * rep_count, "rep")
    limits = jnp.broadcast_to(ranks[..., None, None], ranks.shape + (1, LANES))
    predicted = predict(limits, spectrum, green_right, green_left, tile_count)
    misfit, residual = residual_of(exchange(predicted, "rtile"), data)
    misfit = exchange([misfit] * tile_count, "rtile")
    partial = back_project(limits, misfit, green_right, green_left, freq_count, rep_count)
    arrived = exchange(gather(exchange(partial, "rep")), "freq")
    return (residual, gradient_of(arrived, table, rhs_count))


def solution(mesh):
    return jax.shard_map(
        shards,
        mesh=mesh,
        in_specs=(
            P("rtile", "freq", None, None),
            P(None, "freq", "rep", "rtile", None, None),
            P(None, "freq", "rep", "rtile", None, None),
            P("freq", "rep", "rtile"),
            P(None, ("freq", "rtile"), "rep"),
        ),
        out_specs=(P(None, ("freq", "rtile"), "rep"), P("rtile", ("freq", "rep"), None, None)),
        check_vma=False,
    )
```

```python
import functools
import math

import jax
import jax.numpy as jnp
from jax import lax
from jax.experimental import pallas as pl
from jax.experimental.pallas import tpu as pltpu
from jax.sharding import PartitionSpec as P

LANES = 128
VMEM_LIMIT = 48 * 1024 * 1024


def tables(bins, length):
    row = lax.broadcasted_iota(jnp.int32, (bins, length), 0)
    sample = lax.broadcasted_iota(jnp.int32, (bins, length), 1)
    is_sine = row >= bins // 2
    freq_bin = jnp.where(is_sine, row - bins // 2, row) + 1
    phase = lax.rem(freq_bin * sample, length) + jnp.where(is_sine, length // 4, 0)
    quarter = lax.div(phase + length // 8, length // 4)
    angle = (phase - quarter * (length // 4)).astype(jnp.float32) * (2.0 * math.pi / length)
    square = angle * angle
    even = 1.0
    odd = 1.0
    for order in (8, 6, 4, 2):
        even = 1.0 - square * even * (1.0 / (order * (order - 1)))
        odd = 1.0 - square * odd * (1.0 / (order * (order + 1)))
    odd = odd * angle
    quarter = quarter & 3
    value = jnp.where((quarter & 1) == 0, even, odd)
    return jnp.where((quarter == 1) | (quarter == 2), -value, value).astype(jnp.bfloat16)


def dot(first, second, first_dim, second_dim):
    return lax.dot_general(
        first,
        second,
        (((first_dim,), (second_dim,)), ((), ())),
        preferred_element_type=jnp.float32,
    )


def turned(pair):
    half = pair.shape[1] // 2
    return jnp.concatenate([-pair[:, half:], pair[:, :half]], axis=1)


def target(me, step, count):
    return me ^ step if count & (count - 1) == 0 else lax.rem(me + step, count)


def origin(me, step, count):
    return me ^ step if count & (count - 1) == 0 else lax.rem(me + count - step, count)


def exchange(blocks, axis):
    count = len(blocks)
    arrived = []
    for step in range(count - 1, 0, -1):
        pairs = [(me, me ^ step if count & (count - 1) == 0 else (me + step) % count) for me in range(count)]
        arrived.append(lax.ppermute(blocks[step], axis, pairs))
    return [blocks[0]] + arrived[::-1]


def spectrum_kernel(model_hbm, table_out_ref, *refs):
    out_refs = refs[:-3]
    model_ref, rows_ref, model_sems = refs[-3:]
    high, low, rhs, length = model_ref.shape
    dests = len(out_refs)
    freqs, _, _, lanes = out_refs[0].shape
    bins = 2 * dests * freqs
    chunks = model_sems.shape[0]
    part = low // chunks
    own = model_hbm.at[lax.axis_index("rep")]
    copies = []
    for at in range(chunks):
        rows = pl.ds(at * part, part)
        copies.append(
            [
                pltpu.make_async_copy(
                    own.at[h, rows], model_ref.at[h, rows], model_sems.at[at, h]
                )
                for h in range(high)
            ]
        )
        for copy in copies[-1]:
            copy.start()
    table = tables(bins, length)
    table_out_ref[...] = table
    for at in range(chunks):
        for copy in copies[at]:
            copy.wait()
        for start in range(at * part, (at + 1) * part, 2):
            width = min(2, (at + 1) * part - start)
            block = jnp.concatenate(
                [model_ref[:, start + row].reshape(lanes, length) for row in range(width)]
            )
            sums = dot(table, block, 1, 1)
            for row in range(width):
                place = (start + row) * bins
                rows_ref[place : place + bins] = sums[:, row * lanes : (row + 1) * lanes]
    me = lax.axis_index("freq")
    for at, out_ref in enumerate(out_refs):
        dest = target(me, at, dests)
        for f in range(freqs):
            for c in range(2):
                q = c * dests * freqs + dest * freqs + f
                out_ref[f, c] = rows_ref[pl.ds(q, low, stride=bins), :].astype(out_ref.dtype)


def spectrum_of(model, dests, freqs, reps):
    traces, rhs, length = model.shape
    high = LANES // rhs
    low = traces // (reps * high)
    chunks = math.gcd(low, 4)
    bins = 2 * dests * freqs
    table, *blocks = pl.pallas_call(
        spectrum_kernel,
        in_specs=[pl.BlockSpec(memory_space=pltpu.HBM)],
        out_specs=[pl.BlockSpec(memory_space=pltpu.VMEM)] * (1 + dests),
        out_shape=[jax.ShapeDtypeStruct((bins, length), jnp.bfloat16)]
        + [jax.ShapeDtypeStruct((freqs, 2, low, LANES), jnp.bfloat16)] * dests,
        scratch_shapes=[
            pltpu.VMEM((high, low, rhs, length), model.dtype),
            pltpu.VMEM((low * bins, LANES), jnp.float32),
            pltpu.SemaphoreType.DMA((chunks, high)),
        ],
        compiler_params=pltpu.CompilerParams(vmem_limit_bytes=VMEM_LIMIT),
        name="spectrum",
    )(model.reshape(reps, high, low, rhs, length))
    return table, blocks


def pack_kernel(*refs):
    block_refs, out_ref = refs[:-1], refs[-1]
    me = lax.axis_index("freq")
    for at, block_ref in enumerate(block_refs):
        out_ref[origin(me, at, len(block_refs))] = block_ref[...]


def pack(blocks):
    shape = (len(blocks),) + blocks[0].shape
    return pl.pallas_call(
        pack_kernel,
        in_specs=[pl.BlockSpec(memory_space=pltpu.VMEM)] * len(blocks),
        out_specs=pl.BlockSpec(memory_space=pltpu.VMEM),
        out_shape=jax.ShapeDtypeStruct(shape, blocks[0].dtype),
        compiler_params=pltpu.CompilerParams(vmem_limit_bytes=VMEM_LIMIT),
        name="pack",
    )(*blocks)


def tile_cost(count, size, tile, rhs):
    return pl.CostEstimate(
        flops=count * 2 * 8 * size * tile * rhs,
        bytes_accessed=count * 2 * 4 * size * tile,
        transcendentals=0,
    )


def masked(product, limits_ref, places, size):
    columns = product.shape[1]
    row = lax.broadcasted_iota(jnp.int32, (size, columns), 0)
    kept = [
        jnp.where(row < limits_ref[place][:, :columns], product[at * size : (at + 1) * size], 0.0)
        for at, place in enumerate(places)
    ]
    return [part.astype(jnp.bfloat16) for part in kept]


def spans(first, count, size):
    found = []
    at = first
    while at < first + count:
        length = min(size - at % size, first + count - at)
        found.append((at // size, at % size, length))
        at += length
    return found


def predict_kernel(reps, parts, limits_ref, right_ref, left_ref, *refs):
    arrived_refs, out_refs = refs[:reps], refs[reps : reps + parts]
    spec_ref, sum_ref = refs[reps + parts :]
    _, groups, freqs, _, low, lanes = spec_ref.shape
    row_tiles, col_tiles, size, tile = left_ref.shape[2:]
    _, pairs, _ = out_refs[0].shape
    own = lax.axis_index("rep")
    for at, arrived_ref in enumerate(arrived_refs):
        spec_ref[origin(own, at, reps)] = arrived_ref[...]
    rhs = parts * pairs // freqs
    high = lanes // rhs
    per_tile = groups // col_tiles
    for f in range(freqs):
        projected = []
        for j in range(col_tiles):
            halves = []
            for c in range(2):
                blocks = []
                for g in range(j * per_tile, (j + 1) * per_tile):
                    for rep in range(reps):
                        got = spec_ref[rep, g, f, c]
                        if low % 16:
                            got = got.astype(jnp.float32)
                        blocks += [got[:, h * rhs : (h + 1) * rhs] for h in range(high)]
                halves.append(jnp.concatenate(blocks))
            straight = jnp.concatenate(halves, axis=1).astype(jnp.bfloat16)
            crossed = jnp.concatenate([halves[1], -halves[0]], axis=1).astype(jnp.bfloat16)
            right = [right_ref[c, f, :, j].reshape(row_tiles * size, tile) for c in range(2)]
            product = dot(right[0], straight, 1, 0) + dot(right[1], crossed, 1, 0)
            places = [(f, i, j) for i in range(row_tiles)]
            projected.append(masked(product, limits_ref, places, size))
        for i in range(row_tiles):
            straight = [projected[j][i] for j in range(col_tiles)]
            factors = jnp.concatenate(straight + [turned(part) for part in straight])
            left = left_ref[:, f, i].reshape(2 * col_tiles * size, tile)
            predicted = dot(factors, left, 0, 0)
            for c in range(2):
                row = c * rhs
                for part, start, length in spans(f * rhs, rhs, pairs):
                    sum_ref[part, c, start : start + length, i * tile : (i + 1) * tile] = predicted[
                        row : row + length
                    ]
                    row += length
    me = lax.axis_index("rtile")
    for at, out_ref in enumerate(out_refs):
        out_ref[...] = sum_ref[target(me, at, parts)].astype(out_ref.dtype)


def predict(limits, spectrum, green_right, green_left, parts):
    freqs, row_tiles, col_tiles, size, tile = green_left.shape[1:]
    reps = len(spectrum)
    groups, _, _, low, _ = spectrum[0].shape
    rhs = LANES * reps * groups * low // (col_tiles * tile)
    pairs = freqs * rhs
    sources = row_tiles * tile
    return pl.pallas_call(
        functools.partial(predict_kernel, reps, parts),
        in_specs=[pl.BlockSpec(memory_space=pltpu.VMEM)] * (3 + reps),
        out_specs=[pl.BlockSpec(memory_space=pltpu.VMEM)] * parts,
        out_shape=[jax.ShapeDtypeStruct((2, pairs // parts, sources), jnp.bfloat16)] * parts,
        scratch_shapes=[
            pltpu.VMEM((reps,) + spectrum[0].shape, jnp.bfloat16),
            pltpu.VMEM((parts, 2, pairs // parts, sources), jnp.float32),
        ],
        compiler_params=pltpu.CompilerParams(vmem_limit_bytes=VMEM_LIMIT),
        cost_estimate=tile_cost(freqs * row_tiles * col_tiles, size, tile, rhs),
        name="predict",
    )(limits, green_right, green_left, *spectrum)


def residual_kernel(data_ref, *refs):
    block_refs, (misfit_ref, *part_refs) = refs[:-3], refs[-3:]
    residual = sum(block_ref[...].astype(jnp.float32) for block_ref in block_refs) - data_ref[...]
    for c, part_ref in enumerate(part_refs):
        part_ref[...] = residual[c]
    misfit_ref[...] = residual.astype(misfit_ref.dtype)


def residual_of(blocks, data):
    shape = blocks[0].shape
    return pl.pallas_call(
        residual_kernel,
        in_specs=[pl.BlockSpec(memory_space=pltpu.VMEM)] * (1 + len(blocks)),
        out_specs=[pl.BlockSpec(memory_space=pltpu.VMEM)] * 3,
        out_shape=[
            jax.ShapeDtypeStruct(shape, jnp.bfloat16),
            jax.ShapeDtypeStruct(shape[1:], jnp.float32),
            jax.ShapeDtypeStruct(shape[1:], jnp.float32),
        ],
        compiler_params=pltpu.CompilerParams(vmem_limit_bytes=VMEM_LIMIT),
        name="residual",
    )(data, *blocks)


def back_kernel(parts, groups, reps, limits_ref, right_ref, left_ref, *refs):
    misfit_refs, out_refs = refs[:parts], refs[parts : parts + reps]
    misfit_all_ref, grad_ref = refs[parts + reps :]
    _, freqs, row_tiles, col_tiles, size, tile = left_ref.shape
    _, pairs, _ = misfit_refs[0].shape
    rhs = parts * pairs // freqs
    _, _, _, low, lanes = out_refs[0].shape
    high = lanes // rhs
    per_tile = groups * reps // col_tiles
    me = lax.axis_index("rtile")
    for at, misfit_ref in enumerate(misfit_refs):
        misfit_all_ref[origin(me, at, parts)] = misfit_ref[...].astype(jnp.float32)
    for f in range(freqs):
        back = []
        for i in range(row_tiles):
            rows = [
                jnp.concatenate(
                    [
                        misfit_all_ref[part, c, start : start + length, i * tile : (i + 1) * tile]
                        for part, start, length in spans(f * rhs, rhs, pairs)
                    ]
                )
                for c in range(2)
            ]
            straight = jnp.concatenate(rows).astype(jnp.bfloat16)
            crossed = jnp.concatenate([rows[1], -rows[0]]).astype(jnp.bfloat16)
            left = [left_ref[c, f, i].reshape(col_tiles * size, tile) for c in range(2)]
            product = dot(left[0], straight, 1, 1) + dot(left[1], crossed, 1, 1)
            places = [(f, i, j) for j in range(col_tiles)]
            back.append(masked(product, limits_ref, places, size))
        for j in range(col_tiles):
            straight = [part[j] for part in back]
            factors = jnp.concatenate(straight + [turned(part) for part in straight])
            right = jnp.concatenate(
                [right_ref[c, f, :, j].reshape(row_tiles * size, tile) for c in range(2)]
            )
            grad = dot(factors, right, 0, 0)
            grad = (grad if low % 16 else grad.astype(out_refs[0].dtype)).T
            for at in range(per_tile):
                rows = at * high * low
                for c in range(2):
                    blocks = [
                        grad[rows + h * low : rows + (h + 1) * low, c * rhs : (c + 1) * rhs]
                        for h in range(high)
                    ]
                    grad_ref[j * per_tile + at, f, c] = jnp.concatenate(blocks, axis=1).astype(
                        grad_ref.dtype
                    )
    me, own = lax.axis_index("freq"), lax.axis_index("rep")
    for at, out_ref in enumerate(out_refs):
        rep = target(own, at, reps)
        for step in range(groups):
            out_ref[step] = grad_ref[target(me, step, groups) * reps + rep]


def back_project(limits, misfit, green_right, green_left, groups, reps):
    parts = len(misfit)
    _, pairs, sources = misfit[0].shape
    freqs, row_tiles, col_tiles, size, tile = green_left.shape[1:]
    rhs = parts * pairs // freqs
    low = col_tiles * tile * rhs // (groups * reps * LANES)
    block = (freqs, 2, low, LANES)
    return pl.pallas_call(
        functools.partial(back_kernel, parts, groups, reps),
        in_specs=[pl.BlockSpec(memory_space=pltpu.VMEM)] * (3 + parts),
        out_specs=[pl.BlockSpec(memory_space=pltpu.VMEM)] * reps,
        out_shape=[jax.ShapeDtypeStruct((groups,) + block, jnp.bfloat16)] * reps,
        scratch_shapes=[
            pltpu.VMEM((parts, 2, pairs, sources), jnp.float32),
            pltpu.VMEM((groups * reps,) + block, jnp.bfloat16),
        ],
        compiler_params=pltpu.CompilerParams(vmem_limit_bytes=VMEM_LIMIT),
        cost_estimate=tile_cost(freqs * row_tiles * col_tiles, size, tile, rhs),
        name="back_project",
    )(limits, green_right, green_left, *misfit)


def gather_kernel(picks, reps, *refs):
    part_refs, out_refs = refs[:reps], refs[reps:]
    for steps, out_ref in zip(picks, out_refs):
        for at, step in enumerate(steps):
            total = sum(part_ref[step].astype(jnp.float32) for part_ref in part_refs)
            out_ref[at] = total.astype(out_ref.dtype)


def gather(parts, picks):
    shape = parts[0].shape[1:]
    return pl.pallas_call(
        functools.partial(gather_kernel, picks, len(parts)),
        in_specs=[pl.BlockSpec(memory_space=pltpu.VMEM)] * len(parts),
        out_specs=[pl.BlockSpec(memory_space=pltpu.VMEM)] * len(picks),
        out_shape=[
            jax.ShapeDtypeStruct((len(steps),) + shape, jnp.bfloat16) for steps in picks
        ],
        compiler_params=pltpu.CompilerParams(vmem_limit_bytes=VMEM_LIMIT),
        name="gather",
    )(*parts)


def select_kernel(picks, *refs):
    *block_refs, out_ref = refs
    for at, (array, place) in enumerate(picks):
        out_ref[at] = block_refs[array][place]


def select(arrays, picks):
    shape = (len(picks),) + arrays[0].shape[1:]
    return pl.pallas_call(
        functools.partial(select_kernel, picks),
        in_specs=[pl.BlockSpec(memory_space=pltpu.VMEM)] * len(arrays),
        out_specs=pl.BlockSpec(memory_space=pltpu.VMEM),
        out_shape=jax.ShapeDtypeStruct(shape, arrays[0].dtype),
        compiler_params=pltpu.CompilerParams(vmem_limit_bytes=VMEM_LIMIT),
        name="select",
    )(*arrays)


def return_spectra(parts, axis):
    count = parts[0].shape[0]
    if count & (count - 1):
        blocks = exchange(gather(parts, [[step] for step in range(count)]), axis)
        return select(blocks, [(step, 0) for step in range(count)])
    sent, kept = [[step for step in range(count) if step & 1 == bit] for bit in (1, 0)]
    message, own = gather(parts, [sent, kept])
    arrays = [own]
    held = {(0, step): (0, at) for at, step in enumerate(kept)}
    leaving = [(0, step) for step in sent]
    bit = 1
    while bit < count:
        if bit > 1:
            leaving = sorted(key for key in held if key[1] & bit)
            message = select(arrays, [held.pop(key) for key in leaving])
        arrays.append(lax.ppermute(message, axis, [(me, me ^ bit) for me in range(count)]))
        for at, (source, step) in enumerate(leaving):
            held[source ^ bit, step ^ bit] = (len(arrays) - 1, at)
        bit *= 2
    return select(arrays, [held[source, 0] for source in range(count)])


def gradient_kernel(table_ref, parts_ref, out_hbm, out_ref, rows_ref, out_sems):
    groups, freqs, _, low, lanes = parts_ref.shape
    high, _, rhs, length = out_ref.shape
    bins = table_ref.shape[0]
    chunks = out_sems.shape[0]
    part = low // chunks
    me = lax.axis_index("freq")
    for at in range(groups):
        g = origin(me, at, groups)
        for f in range(freqs):
            for c in range(2):
                rows = pl.ds(c * groups * freqs + g * freqs + f, low, stride=bins)
                rows_ref[rows, :] = parts_ref[at, f, c].astype(jnp.float32)
    table = table_ref[...]
    copies = []
    for at in range(chunks):
        coefficients = jnp.concatenate(
            [rows_ref[row * bins : (row + 1) * bins] for row in range(at * part, (at + 1) * part)],
            axis=1,
        ).astype(jnp.bfloat16)
        traces = dot(coefficients, table, 0, 0).astype(out_ref.dtype)
        for row in range(part):
            out_ref[:, at * part + row] = traces[row * lanes : (row + 1) * lanes].reshape(
                high, rhs, length
            )
        rows = pl.ds(at * part, part)
        for h in range(high):
            copies.append(
                pltpu.make_async_copy(
                    out_ref.at[h, rows], out_hbm.at[h, rows], out_sems.at[at, h]
                )
            )
            copies[-1].start()
    for copy in copies:
        copy.wait()


def gradient_of(parts, table, rhs):
    _, _, _, low, lanes = parts.shape
    bins, length = table.shape
    high = lanes // rhs
    chunks = math.gcd(low, 4)
    shape = (high, low, rhs, length)
    out = pl.pallas_call(
        gradient_kernel,
        in_specs=[pl.BlockSpec(memory_space=pltpu.VMEM)] * 2,
        out_specs=pl.BlockSpec(memory_space=pltpu.HBM),
        out_shape=jax.ShapeDtypeStruct(shape, jnp.bfloat16),
        scratch_shapes=[
            pltpu.VMEM(shape, jnp.bfloat16),
            pltpu.VMEM((low * bins, lanes), jnp.float32),
            pltpu.SemaphoreType.DMA((chunks, high)),
        ],
        compiler_params=pltpu.CompilerParams(vmem_limit_bytes=VMEM_LIMIT),
        name="gradient",
    )(table, parts)
    return out.reshape(1, high * low, rhs, length)


def shards(model, green_left, green_right, ranks, data):
    freq_count = lax.axis_size("freq")
    tile_count = lax.axis_size("rtile")
    rep_count = lax.axis_size("rep")
    freq_local = ranks.shape[0]
    rhs_count = model.shape[2]
    table, spectrum = spectrum_of(model[0], freq_count, freq_local, rep_count)
    spectrum = pack(exchange(spectrum, "freq"))
    spectrum = exchange([spectrum] * rep_count, "rep")
    limits = jnp.broadcast_to(ranks[..., None, None], ranks.shape + (1, LANES))
    predicted = predict(limits, spectrum, green_right, green_left, tile_count)
    misfit, *residual = residual_of(exchange(predicted, "rtile")[::-1], data)
    misfit = exchange([misfit] * tile_count, "rtile")
    partial = back_project(limits, misfit, green_right, green_left, freq_count, rep_count)
    arrived = return_spectra(exchange(partial, "rep"), "freq")
    return (jnp.stack(residual), gradient_of(arrived, table, rhs_count))


def solution(mesh):
    return jax.shard_map(
        shards,
        mesh=mesh,
        in_specs=(
            P("rtile", "freq", None, None),
            P(None, "freq", "rep", "rtile", None, None),
            P(None, "freq", "rep", "rtile", None, None),
            P("freq", "rep", "rtile"),
            P(None, ("freq", "rtile"), "rep"),
        ),
        out_specs=(P(None, ("freq", "rtile"), "rep"), P("rtile", ("freq", "rep"), None, None)),
        check_vma=False,
    )
```

```python
import functools
import math

import jax
import jax.numpy as jnp
from jax import lax
from jax.experimental import pallas as pl
from jax.experimental.pallas import tpu as pltpu
from jax.sharding import PartitionSpec as P

LANES = 128
VMEM_LIMIT = 48 * 1024 * 1024


def tables(bins, length):
    row = lax.broadcasted_iota(jnp.int32, (bins, length), 0)
    sample = lax.broadcasted_iota(jnp.int32, (bins, length), 1)
    is_sine = row >= bins // 2
    freq_bin = jnp.where(is_sine, row - bins // 2, row) + 1
    phase = lax.rem(freq_bin * sample, length) + jnp.where(is_sine, length // 4, 0)
    quarter = lax.div(phase + length // 8, length // 4)
    angle = (phase - quarter * (length // 4)).astype(jnp.float32) * (2.0 * math.pi / length)
    square = angle * angle
    even = 1.0
    odd = 1.0
    for order in (8, 6, 4, 2):
        even = 1.0 - square * even * (1.0 / (order * (order - 1)))
        odd = 1.0 - square * odd * (1.0 / (order * (order + 1)))
    odd = odd * angle
    quarter = quarter & 3
    value = jnp.where((quarter & 1) == 0, even, odd)
    return jnp.where((quarter == 1) | (quarter == 2), -value, value).astype(jnp.bfloat16)


def dot(first, second, first_dim, second_dim):
    return lax.dot_general(
        first,
        second,
        (((first_dim,), (second_dim,)), ((), ())),
        preferred_element_type=jnp.float32,
    )


def turned(pair):
    half = pair.shape[1] // 2
    return jnp.concatenate([-pair[:, half:], pair[:, :half]], axis=1)


def target(me, step, count):
    return me ^ step if count & (count - 1) == 0 else lax.rem(me + step, count)


def origin(me, step, count):
    return me ^ step if count & (count - 1) == 0 else lax.rem(me + count - step, count)


def exchange(blocks, axis):
    count = len(blocks)
    arrived = []
    for step in range(count - 1, 0, -1):
        pairs = [(me, me ^ step if count & (count - 1) == 0 else (me + step) % count) for me in range(count)]
        arrived.append(lax.ppermute(blocks[step], axis, pairs))
    return [blocks[0]] + arrived[::-1]


def spectrum_kernel(model_hbm, table_out_ref, *refs):
    out_refs = refs[:-3]
    model_ref, rows_ref, model_sems = refs[-3:]
    high, low, rhs, length = model_ref.shape
    dests = len(out_refs)
    freqs, _, _, lanes = out_refs[0].shape
    bins = 2 * dests * freqs
    chunks = model_sems.shape[0]
    part = low // chunks
    copies = []
    for at in range(chunks):
        rows = pl.ds(at * part, part)
        copies.append(
            [
                pltpu.make_async_copy(
                    model_hbm.at[h, rows], model_ref.at[h, rows], model_sems.at[at, h]
                )
                for h in range(high)
            ]
        )
        for copy in copies[-1]:
            copy.start()
    table = tables(bins, length)
    table_out_ref[...] = table
    for at in range(chunks):
        for copy in copies[at]:
            copy.wait()
        for start in range(at * part, (at + 1) * part, 2):
            width = min(2, (at + 1) * part - start)
            block = jnp.concatenate(
                [model_ref[:, start + row].reshape(lanes, length) for row in range(width)]
            )
            sums = dot(table, block, 1, 1)
            for row in range(width):
                place = (start + row) * bins
                rows_ref[place : place + bins] = sums[:, row * lanes : (row + 1) * lanes]
    me = lax.axis_index("freq")
    for at, out_ref in enumerate(out_refs):
        dest = target(me, at, dests)
        for f in range(freqs):
            for c in range(2):
                q = c * dests * freqs + dest * freqs + f
                out_ref[f, c] = rows_ref[pl.ds(q, low, stride=bins), :].astype(out_ref.dtype)


def spectrum_of(model, dests, freqs):
    traces, rhs, length = model.shape
    high = LANES // rhs
    low = traces // high
    chunks = math.gcd(low, 4)
    bins = 2 * dests * freqs
    table, *blocks = pl.pallas_call(
        spectrum_kernel,
        in_specs=[pl.BlockSpec(memory_space=pltpu.HBM)],
        out_specs=[pl.BlockSpec(memory_space=pltpu.VMEM)] * (1 + dests),
        out_shape=[jax.ShapeDtypeStruct((bins, length), jnp.bfloat16)]
        + [jax.ShapeDtypeStruct((freqs, 2, low, LANES), jnp.bfloat16)] * dests,
        scratch_shapes=[
            pltpu.VMEM((high, low, rhs, length), model.dtype),
            pltpu.VMEM((low * bins, LANES), jnp.float32),
            pltpu.SemaphoreType.DMA((chunks, high)),
        ],
        compiler_params=pltpu.CompilerParams(vmem_limit_bytes=VMEM_LIMIT),
        name="spectrum",
    )(model.reshape(high, low, rhs, length))
    return table, blocks


def tile_cost(count, size, tile, rhs):
    return pl.CostEstimate(
        flops=count * 2 * 8 * size * tile * rhs,
        bytes_accessed=count * 2 * 4 * size * tile,
        transcendentals=0,
    )


def masked(product, limits_ref, places, size):
    columns = product.shape[1]
    row = lax.broadcasted_iota(jnp.int32, (size, columns), 0)
    kept = [
        jnp.where(row < limits_ref[place][:, :columns], product[at * size : (at + 1) * size], 0.0)
        for at, place in enumerate(places)
    ]
    return [part.astype(jnp.bfloat16) for part in kept]


def spans(first, count, size):
    found = []
    at = first
    while at < first + count:
        length = min(size - at % size, first + count - at)
        found.append((at // size, at % size, length))
        at += length
    return found


def predict_kernel(groups, parts, limits_ref, right_ref, left_ref, *refs):
    arrived_refs, out_refs = refs[:groups], refs[groups : groups + parts]
    spec_ref, sum_ref = refs[groups + parts :]
    _, freqs, _, low, lanes = spec_ref.shape
    row_tiles, col_tiles, size, tile = left_ref.shape[2:]
    _, pairs, _ = out_refs[0].shape
    me = lax.axis_index("freq")
    for at, arrived_ref in enumerate(arrived_refs[::-1]):
        spec_ref[origin(me, at, groups)] = arrived_ref[...]
    rhs = parts * pairs // freqs
    high = lanes // rhs
    per_tile = groups // col_tiles
    for f in range(freqs):
        projected = []
        for j in range(col_tiles):
            halves = []
            for c in range(2):
                blocks = []
                for g in range(j * per_tile, (j + 1) * per_tile):
                    got = spec_ref[g, f, c]
                    if low % 16:
                        got = got.astype(jnp.float32)
                    blocks += [got[:, h * rhs : (h + 1) * rhs] for h in range(high)]
                halves.append(jnp.concatenate(blocks))
            straight = jnp.concatenate(halves, axis=1).astype(jnp.bfloat16)
            crossed = jnp.concatenate([halves[1], -halves[0]], axis=1).astype(jnp.bfloat16)
            right = [right_ref[c, f, :, j].reshape(row_tiles * size, tile) for c in range(2)]
            product = dot(right[0], straight, 1, 0) + dot(right[1], crossed, 1, 0)
            places = [(f, i, j) for i in range(row_tiles)]
            projected.append(masked(product, limits_ref, places, size))
        for i in range(row_tiles):
            straight = [projected[j][i] for j in range(col_tiles)]
            factors = jnp.concatenate(straight + [turned(part) for part in straight])
            left = left_ref[:, f, i].reshape(2 * col_tiles * size, tile)
            predicted = dot(factors, left, 0, 0)
            for c in range(2):
                row = c * rhs
                for part, start, length in spans(f * rhs, rhs, pairs):
                    sum_ref[part, c, start : start + length, i * tile : (i + 1) * tile] = predicted[
                        row : row + length
                    ]
                    row += length
    me = lax.axis_index("rtile")
    for at, out_ref in enumerate(out_refs):
        out_ref[...] = sum_ref[target(me, at, parts)].astype(out_ref.dtype)


def predict(limits, spectrum, green_right, green_left, parts):
    freqs, row_tiles, col_tiles, size, tile = green_left.shape[1:]
    groups = len(spectrum)
    _, _, low, _ = spectrum[0].shape
    rhs = LANES * groups * low // (col_tiles * tile)
    pairs = freqs * rhs
    sources = row_tiles * tile
    return pl.pallas_call(
        functools.partial(predict_kernel, groups, parts),
        in_specs=[pl.BlockSpec(memory_space=pltpu.VMEM)] * (3 + groups),
        out_specs=[pl.BlockSpec(memory_space=pltpu.VMEM)] * parts,
        out_shape=[jax.ShapeDtypeStruct((2, pairs // parts, sources), jnp.bfloat16)] * parts,
        scratch_shapes=[
            pltpu.VMEM((groups,) + spectrum[0].shape, jnp.bfloat16),
            pltpu.VMEM((parts, 2, pairs // parts, sources), jnp.float32),
        ],
        compiler_params=pltpu.CompilerParams(vmem_limit_bytes=VMEM_LIMIT),
        cost_estimate=tile_cost(freqs * row_tiles * col_tiles, size, tile, rhs),
        name="predict",
    )(limits, green_right, green_left, *spectrum[::-1])


def residual_kernel(data_ref, *refs):
    block_refs, (misfit_ref, *part_refs) = refs[:-3], refs[-3:]
    residual = sum(block_ref[...].astype(jnp.float32) for block_ref in block_refs) - data_ref[...]
    for c, part_ref in enumerate(part_refs):
        part_ref[...] = residual[c]
    misfit_ref[...] = residual.astype(misfit_ref.dtype)


def residual_of(blocks, data):
    shape = blocks[0].shape
    return pl.pallas_call(
        residual_kernel,
        in_specs=[pl.BlockSpec(memory_space=pltpu.VMEM)] * (1 + len(blocks)),
        out_specs=[pl.BlockSpec(memory_space=pltpu.VMEM)] * 3,
        out_shape=[
            jax.ShapeDtypeStruct(shape, jnp.bfloat16),
            jax.ShapeDtypeStruct(shape[1:], jnp.float32),
            jax.ShapeDtypeStruct(shape[1:], jnp.float32),
        ],
        compiler_params=pltpu.CompilerParams(vmem_limit_bytes=VMEM_LIMIT),
        name="residual",
    )(data, *blocks)


def back_kernel(parts, groups, reps, limits_ref, right_ref, left_ref, *refs):
    misfit_refs, out_refs = refs[:parts], refs[parts : parts + reps]
    misfit_all_ref, grad_ref = refs[parts + reps :]
    _, freqs, row_tiles, col_tiles, size, tile = left_ref.shape
    _, pairs, _ = misfit_refs[0].shape
    rhs = parts * pairs // freqs
    _, _, _, low, lanes = out_refs[0].shape
    high = lanes // rhs
    per_tile = groups * reps // col_tiles
    me = lax.axis_index("rtile")
    for at, misfit_ref in enumerate(misfit_refs):
        misfit_all_ref[origin(me, at, parts)] = misfit_ref[...].astype(jnp.float32)
    for f in range(freqs):
        back = []
        for i in range(row_tiles):
            rows = [
                jnp.concatenate(
                    [
                        misfit_all_ref[part, c, start : start + length, i * tile : (i + 1) * tile]
                        for part, start, length in spans(f * rhs, rhs, pairs)
                    ]
                )
                for c in range(2)
            ]
            straight = jnp.concatenate(rows).astype(jnp.bfloat16)
            crossed = jnp.concatenate([rows[1], -rows[0]]).astype(jnp.bfloat16)
            left = [left_ref[c, f, i].reshape(col_tiles * size, tile) for c in range(2)]
            product = dot(left[0], straight, 1, 1) + dot(left[1], crossed, 1, 1)
            places = [(f, i, j) for j in range(col_tiles)]
            back.append(masked(product, limits_ref, places, size))
        for j in range(col_tiles):
            straight = [part[j] for part in back]
            factors = jnp.concatenate(straight + [turned(part) for part in straight])
            right = jnp.concatenate(
                [right_ref[c, f, :, j].reshape(row_tiles * size, tile) for c in range(2)]
            )
            grad = dot(factors, right, 0, 0)
            grad = (grad if low % 16 else grad.astype(out_refs[0].dtype)).T
            for at in range(per_tile):
                rows = at * high * low
                for c in range(2):
                    blocks = [
                        grad[rows + h * low : rows + (h + 1) * low, c * rhs : (c + 1) * rhs]
                        for h in range(high)
                    ]
                    grad_ref[j * per_tile + at, f, c] = jnp.concatenate(blocks, axis=1).astype(
                        grad_ref.dtype
                    )
    me, own = lax.axis_index("freq"), lax.axis_index("rep")
    for at, out_ref in enumerate(out_refs):
        rep = target(own, at, reps)
        for step in range(groups):
            out_ref[step] = grad_ref[target(me, step, groups) * reps + rep]


def back_project(limits, misfit, green_right, green_left, groups, reps):
    parts = len(misfit)
    _, pairs, sources = misfit[0].shape
    freqs, row_tiles, col_tiles, size, tile = green_left.shape[1:]
    rhs = parts * pairs // freqs
    low = col_tiles * tile * rhs // (groups * reps * LANES)
    block = (freqs, 2, low, LANES)
    return pl.pallas_call(
        functools.partial(back_kernel, parts, groups, reps),
        in_specs=[pl.BlockSpec(memory_space=pltpu.VMEM)] * (3 + parts),
        out_specs=[pl.BlockSpec(memory_space=pltpu.VMEM)] * reps,
        out_shape=[jax.ShapeDtypeStruct((groups,) + block, jnp.bfloat16)] * reps,
        scratch_shapes=[
            pltpu.VMEM((parts, 2, pairs, sources), jnp.float32),
            pltpu.VMEM((groups * reps,) + block, jnp.bfloat16),
        ],
        compiler_params=pltpu.CompilerParams(vmem_limit_bytes=VMEM_LIMIT),
        cost_estimate=tile_cost(freqs * row_tiles * col_tiles, size, tile, rhs),
        name="back_project",
    )(limits, green_right, green_left, *misfit)


def gather_kernel(reps, *refs):
    part_refs, out_refs = refs[:reps], refs[reps:]
    for step, out_ref in enumerate(out_refs):
        total = sum(part_ref[step].astype(jnp.float32) for part_ref in part_refs)
        out_ref[...] = total.astype(out_ref.dtype)


def gather(parts):
    shape = parts[0].shape
    return pl.pallas_call(
        functools.partial(gather_kernel, len(parts)),
        in_specs=[pl.BlockSpec(memory_space=pltpu.VMEM)] * len(parts),
        out_specs=[pl.BlockSpec(memory_space=pltpu.VMEM)] * shape[0],
        out_shape=[jax.ShapeDtypeStruct(shape[1:], jnp.bfloat16)] * shape[0],
        compiler_params=pltpu.CompilerParams(vmem_limit_bytes=VMEM_LIMIT),
        name="gather",
    )(*parts)


def gradient_kernel(table_ref, *refs):
    part_refs, (out_hbm, out_ref, rows_ref, out_sems) = refs[-5::-1], refs[-4:]
    groups = len(part_refs)
    freqs, _, low, lanes = part_refs[0].shape
    high, _, rhs, length = out_ref.shape
    bins = table_ref.shape[0]
    chunks = out_sems.shape[0]
    part = low // chunks
    me = lax.axis_index("freq")
    for at, part_ref in enumerate(part_refs):
        g = origin(me, at, groups)
        for f in range(freqs):
            for c in range(2):
                rows = pl.ds(c * groups * freqs + g * freqs + f, low, stride=bins)
                rows_ref[rows, :] = part_ref[f, c].astype(jnp.float32)
    table = table_ref[...]
    copies = []
    for at in range(chunks):
        coefficients = jnp.concatenate(
            [rows_ref[row * bins : (row + 1) * bins] for row in range(at * part, (at + 1) * part)],
            axis=1,
        ).astype(jnp.bfloat16)
        traces = dot(coefficients, table, 0, 0).astype(out_ref.dtype)
        for row in range(part):
            out_ref[:, at * part + row] = traces[row * lanes : (row + 1) * lanes].reshape(
                high, rhs, length
            )
        rows = pl.ds(at * part, part)
        for h in range(high):
            copies.append(
                pltpu.make_async_copy(
                    out_ref.at[h, rows], out_hbm.at[h, rows], out_sems.at[at, h]
                )
            )
            copies[-1].start()
    for copy in copies:
        copy.wait()


def gradient_of(parts, table, rhs):
    _, _, low, lanes = parts[0].shape
    bins, length = table.shape
    high = lanes // rhs
    chunks = math.gcd(low, 4)
    shape = (high, low, rhs, length)
    out = pl.pallas_call(
        gradient_kernel,
        in_specs=[pl.BlockSpec(memory_space=pltpu.VMEM)] * (1 + len(parts)),
        out_specs=pl.BlockSpec(memory_space=pltpu.HBM),
        out_shape=jax.ShapeDtypeStruct(shape, jnp.bfloat16),
        scratch_shapes=[
            pltpu.VMEM(shape, jnp.bfloat16),
            pltpu.VMEM((low * bins, lanes), jnp.float32),
            pltpu.SemaphoreType.DMA((chunks, high)),
        ],
        compiler_params=pltpu.CompilerParams(vmem_limit_bytes=VMEM_LIMIT),
        name="gradient",
    )(table, *parts[::-1])
    return out.reshape(1, high * low, rhs, length)


def shards(model, green_left, green_right, ranks, data):
    freq_count = lax.axis_size("freq")
    tile_count = lax.axis_size("rtile")
    rep_count = lax.axis_size("rep")
    freq_local = ranks.shape[0]
    rhs_count = model.shape[2]
    table, spectrum = spectrum_of(model[0], freq_count, freq_local)
    spectrum = exchange(spectrum, "freq")
    limits = jnp.broadcast_to(ranks[..., None, None], ranks.shape + (1, LANES))
    predicted = predict(limits, spectrum, green_right, green_left, tile_count)
    misfit, *residual = residual_of(exchange(predicted, "rtile")[::-1], data)
    misfit = exchange([misfit] * tile_count, "rtile")
    partial = back_project(limits, misfit, green_right, green_left, freq_count, rep_count)
    arrived = exchange(gather(exchange(partial, "rep")), "freq")
    return (jnp.stack(residual), gradient_of(arrived, table, rhs_count))


def solution(mesh):
    return jax.shard_map(
        shards,
        mesh=mesh,
        in_specs=(
            P("rtile", "freq", None, None),
            P(None, "freq", "rep", "rtile", None, None),
            P(None, "freq", "rep", "rtile", None, None),
            P("freq", "rep", "rtile"),
            P(None, ("freq", "rtile"), "rep"),
        ),
        out_specs=(P(None, ("freq", "rtile"), "rep"), P("rtile", ("freq", "rep"), None, None)),
        check_vma=False,
    )
```

```python
import functools
import math

import jax
import jax.numpy as jnp
from jax import lax
from jax.experimental import pallas as pl
from jax.experimental.pallas import tpu as pltpu
from jax.sharding import PartitionSpec as P

LANES = 128
VMEM_LIMIT = 48 * 1024 * 1024


def tables(bins, length):
    row = lax.broadcasted_iota(jnp.int32, (bins, length), 0)
    sample = lax.broadcasted_iota(jnp.int32, (bins, length), 1)
    is_sine = row >= bins // 2
    freq_bin = jnp.where(is_sine, row - bins // 2, row) + 1
    phase = lax.rem(freq_bin * sample, length) + jnp.where(is_sine, length // 4, 0)
    quarter = lax.div(phase + length // 8, length // 4)
    angle = (phase - quarter * (length // 4)).astype(jnp.float32) * (2.0 * math.pi / length)
    square = angle * angle
    even = 1.0
    odd = 1.0
    for order in (8, 6, 4, 2):
        even = 1.0 - square * even * (1.0 / (order * (order - 1)))
        odd = 1.0 - square * odd * (1.0 / (order * (order + 1)))
    odd = odd * angle
    quarter = quarter & 3
    value = jnp.where((quarter & 1) == 0, even, odd)
    return jnp.where((quarter == 1) | (quarter == 2), -value, value).astype(jnp.bfloat16)


def dot(first, second, first_dim, second_dim):
    return lax.dot_general(
        first,
        second,
        (((first_dim,), (second_dim,)), ((), ())),
        preferred_element_type=jnp.float32,
    )


def turned(pair):
    half = pair.shape[1] // 2
    return jnp.concatenate([-pair[:, half:], pair[:, :half]], axis=1)


def target(me, step, count):
    return me ^ step if count & (count - 1) == 0 else lax.rem(me + step, count)


def origin(me, step, count):
    return me ^ step if count & (count - 1) == 0 else lax.rem(me + count - step, count)


def exchange(blocks, axis):
    count = len(blocks)
    arrived = []
    for step in range(count - 1, 0, -1):
        pairs = [(me, me ^ step if count & (count - 1) == 0 else (me + step) % count) for me in range(count)]
        arrived.append(lax.ppermute(blocks[step], axis, pairs))
    return [blocks[0]] + arrived[::-1]


def spectrum_kernel(model_hbm, table_out_ref, *refs):
    out_refs = refs[:-3]
    model_ref, rows_ref, model_sems = refs[-3:]
    high, low, rhs, length = model_ref.shape
    dests = len(out_refs)
    freqs, _, _, lanes = out_refs[0].shape
    bins = 2 * dests * freqs
    chunks = model_sems.shape[0]
    part = low // chunks
    copies = []
    for at in range(chunks):
        rows = pl.ds(at * part, part)
        copies.append(
            [
                pltpu.make_async_copy(
                    model_hbm.at[h, rows], model_ref.at[h, rows], model_sems.at[at, h]
                )
                for h in range(high)
            ]
        )
        for copy in copies[-1]:
            copy.start()
    table = tables(bins, length)
    table_out_ref[...] = table
    for at in range(chunks):
        for copy in copies[at]:
            copy.wait()
        for start in range(at * part, (at + 1) * part, 2):
            width = min(2, (at + 1) * part - start)
            block = jnp.concatenate(
                [model_ref[:, start + row].reshape(lanes, length) for row in range(width)]
            )
            sums = dot(table, block, 1, 1)
            for row in range(width):
                place = (start + row) * bins
                rows_ref[place : place + bins] = sums[:, row * lanes : (row + 1) * lanes]
    me = lax.axis_index("freq")
    for at, out_ref in enumerate(out_refs):
        dest = target(me, at, dests)
        for f in range(freqs):
            for c in range(2):
                q = c * dests * freqs + dest * freqs + f
                out_ref[f, c] = rows_ref[pl.ds(q, low, stride=bins), :].astype(out_ref.dtype)


def spectrum_of(model, dests, freqs):
    traces, rhs, length = model.shape
    high = LANES // rhs
    low = traces // high
    chunks = math.gcd(low, 8)
    bins = 2 * dests * freqs
    table, *blocks = pl.pallas_call(
        spectrum_kernel,
        in_specs=[pl.BlockSpec(memory_space=pltpu.HBM)],
        out_specs=[pl.BlockSpec(memory_space=pltpu.VMEM)] * (1 + dests),
        out_shape=[jax.ShapeDtypeStruct((bins, length), jnp.bfloat16)]
        + [jax.ShapeDtypeStruct((freqs, 2, low, LANES), jnp.bfloat16)] * dests,
        scratch_shapes=[
            pltpu.VMEM((high, low, rhs, length), model.dtype),
            pltpu.VMEM((low * bins, LANES), jnp.float32),
            pltpu.SemaphoreType.DMA((chunks, high)),
        ],
        compiler_params=pltpu.CompilerParams(vmem_limit_bytes=VMEM_LIMIT),
        name="spectrum",
    )(model.reshape(high, low, rhs, length))
    return table, blocks


def tile_cost(count, size, tile, rhs):
    return pl.CostEstimate(
        flops=count * 2 * 8 * size * tile * rhs,
        bytes_accessed=count * 2 * 4 * size * tile,
        transcendentals=0,
    )


def masked(product, limits_ref, places, size):
    columns = product.shape[1]
    row = lax.broadcasted_iota(jnp.int32, (size, columns), 0)
    kept = [
        jnp.where(row < limits_ref[place][:, :columns], product[at * size : (at + 1) * size], 0.0)
        for at, place in enumerate(places)
    ]
    return [part.astype(jnp.bfloat16) for part in kept]


def spans(first, count, size):
    found = []
    at = first
    while at < first + count:
        length = min(size - at % size, first + count - at)
        found.append((at // size, at % size, length))
        at += length
    return found


def predict_kernel(groups, parts, tiles, limits_ref, right_ref, left_ref, *refs):
    arrived_refs, out_refs = refs[:groups], refs[groups : groups + parts]
    spec_ref, sum_ref = refs[groups + parts :]
    _, freqs, _, low, lanes = spec_ref.shape
    col_tiles, size, tile = left_ref.shape[3:]
    begin, end = tiles
    row_tiles = end - begin
    _, pairs, _ = out_refs[0].shape
    me = lax.axis_index("freq")
    for at, arrived_ref in enumerate(arrived_refs[::-1]):
        spec_ref[origin(me, at, groups)] = arrived_ref[...]
    rhs = parts * pairs // freqs
    high = lanes // rhs
    per_tile = groups // col_tiles
    for f in range(freqs):
        projected = []
        for j in range(col_tiles):
            halves = []
            for c in range(2):
                blocks = []
                for g in range(j * per_tile, (j + 1) * per_tile):
                    got = spec_ref[g, f, c]
                    if low % 16:
                        got = got.astype(jnp.float32)
                    blocks += [got[:, h * rhs : (h + 1) * rhs] for h in range(high)]
                halves.append(jnp.concatenate(blocks))
            straight = jnp.concatenate(halves, axis=1).astype(jnp.bfloat16)
            crossed = jnp.concatenate([halves[1], -halves[0]], axis=1).astype(jnp.bfloat16)
            right = [
                right_ref[c, f, begin:end, j].reshape(row_tiles * size, tile) for c in range(2)
            ]
            product = dot(right[0], straight, 1, 0) + dot(right[1], crossed, 1, 0)
            places = [(f, i, j) for i in range(begin, end)]
            projected.append(masked(product, limits_ref, places, size))
        for i in range(row_tiles):
            straight = [projected[j][i] for j in range(col_tiles)]
            factors = jnp.concatenate(straight + [turned(part) for part in straight])
            left = left_ref[:, f, begin + i].reshape(2 * col_tiles * size, tile)
            predicted = dot(factors, left, 0, 0)
            for c in range(2):
                row = c * rhs
                for part, start, length in spans(f * rhs, rhs, pairs):
                    sum_ref[part, c, start : start + length, i * tile : (i + 1) * tile] = predicted[
                        row : row + length
                    ]
                    row += length
    me = lax.axis_index("rtile")
    for at, out_ref in enumerate(out_refs):
        out_ref[...] = sum_ref[target(me, at, parts)].astype(out_ref.dtype)


def predict(limits, spectrum, green_right, green_left, parts, tiles):
    freqs, _, col_tiles, size, tile = green_left.shape[1:]
    row_tiles = tiles[1] - tiles[0]
    groups = len(spectrum)
    _, _, low, _ = spectrum[0].shape
    rhs = LANES * groups * low // (col_tiles * tile)
    pairs = freqs * rhs
    sources = row_tiles * tile
    return pl.pallas_call(
        functools.partial(predict_kernel, groups, parts, tiles),
        in_specs=[pl.BlockSpec(memory_space=pltpu.VMEM)] * (3 + groups),
        out_specs=[pl.BlockSpec(memory_space=pltpu.VMEM)] * parts,
        out_shape=[jax.ShapeDtypeStruct((2, pairs // parts, sources), jnp.bfloat16)] * parts,
        scratch_shapes=[
            pltpu.VMEM((groups,) + spectrum[0].shape, jnp.bfloat16),
            pltpu.VMEM((parts, 2, pairs // parts, sources), jnp.float32),
        ],
        compiler_params=pltpu.CompilerParams(vmem_limit_bytes=VMEM_LIMIT),
        cost_estimate=tile_cost(freqs * row_tiles * col_tiles, size, tile, rhs),
        name="predict",
    )(limits, green_right, green_left, *spectrum[::-1])


def residual_kernel(column, data_ref, *refs):
    block_refs, (misfit_ref, residual_ref) = refs[:-2], refs[-2:]
    observed = data_ref[:, :, column : column + residual_ref.shape[2]]
    residual = sum(block_ref[...].astype(jnp.float32) for block_ref in block_refs) - observed
    residual_ref[...] = residual
    misfit_ref[...] = residual.astype(misfit_ref.dtype)


def residual_of(blocks, data, column):
    shape = blocks[0].shape
    return pl.pallas_call(
        functools.partial(residual_kernel, column),
        in_specs=[pl.BlockSpec(memory_space=pltpu.VMEM)] * (1 + len(blocks)),
        out_specs=[pl.BlockSpec(memory_space=pltpu.VMEM)] * 2,
        out_shape=[
            jax.ShapeDtypeStruct(shape, jnp.bfloat16),
            jax.ShapeDtypeStruct(shape, jnp.float32),
        ],
        compiler_params=pltpu.CompilerParams(vmem_limit_bytes=VMEM_LIMIT),
        name="residual",
    )(data, *blocks)


def back_kernel(parts, groups, reps, tiles, limits_ref, right_ref, left_ref, *refs):
    _, freqs, row_tiles, col_tiles, size, tile = left_ref.shape
    begin, end = tiles
    carried, final = begin > 0, end == row_tiles
    row_tiles = end - begin
    misfit_refs, refs = refs[:parts], refs[parts:]
    if carried:
        carried_ref, refs = refs[0], refs[1:]
    _, pairs, _ = misfit_refs[0].shape
    rhs = parts * pairs // freqs
    if final:
        out_refs, (misfit_all_ref, grad_ref) = refs[:reps], refs[reps:]
        _, _, _, low, lanes = out_refs[0].shape
        high = lanes // rhs
        per_tile = groups * reps // col_tiles
    else:
        carry_ref, misfit_all_ref = refs
    me = lax.axis_index("rtile")
    for at, misfit_ref in enumerate(misfit_refs):
        misfit_all_ref[origin(me, at, parts)] = misfit_ref[...].astype(jnp.float32)
    for f in range(freqs):
        back = []
        for i in range(row_tiles):
            rows = [
                jnp.concatenate(
                    [
                        misfit_all_ref[part, c, start : start + length, i * tile : (i + 1) * tile]
                        for part, start, length in spans(f * rhs, rhs, pairs)
                    ]
                )
                for c in range(2)
            ]
            straight = jnp.concatenate(rows).astype(jnp.bfloat16)
            crossed = jnp.concatenate([rows[1], -rows[0]]).astype(jnp.bfloat16)
            left = [left_ref[c, f, begin + i].reshape(col_tiles * size, tile) for c in range(2)]
            product = dot(left[0], straight, 1, 1) + dot(left[1], crossed, 1, 1)
            places = [(f, begin + i, j) for j in range(col_tiles)]
            back.append(masked(product, limits_ref, places, size))
        for j in range(col_tiles):
            straight = [part[j] for part in back]
            factors = jnp.concatenate(straight + [turned(part) for part in straight])
            right = jnp.concatenate(
                [right_ref[c, f, begin:end, j].reshape(row_tiles * size, tile) for c in range(2)]
            )
            grad = dot(factors, right, 0, 0)
            if carried:
                grad = grad + carried_ref[f, j]
            if not final:
                carry_ref[f, j] = grad
                continue
            grad = (grad if low % 16 else grad.astype(out_refs[0].dtype)).T
            for at in range(per_tile):
                rows = at * high * low
                for c in range(2):
                    blocks = [
                        grad[rows + h * low : rows + (h + 1) * low, c * rhs : (c + 1) * rhs]
                        for h in range(high)
                    ]
                    grad_ref[j * per_tile + at, f, c] = jnp.concatenate(blocks, axis=1).astype(
                        grad_ref.dtype
                    )
    if not final:
        return
    me, own = lax.axis_index("freq"), lax.axis_index("rep")
    for at, out_ref in enumerate(out_refs):
        rep = target(own, at, reps)
        for step in range(groups):
            out_ref[step] = grad_ref[target(me, step, groups) * reps + rep]


def back_project(limits, misfit, green_right, green_left, groups, reps, tiles, carried):
    parts = len(misfit)
    _, pairs, sources = misfit[0].shape
    freqs, row_tiles, col_tiles, size, tile = green_left.shape[1:]
    rhs = parts * pairs // freqs
    scratch = [pltpu.VMEM((parts, 2, pairs, sources), jnp.float32)]
    if tiles[1] == row_tiles:
        low = col_tiles * tile * rhs // (groups * reps * LANES)
        block = (freqs, 2, low, LANES)
        out_shape = [jax.ShapeDtypeStruct((groups,) + block, jnp.bfloat16)] * reps
        scratch.append(pltpu.VMEM((groups * reps,) + block, jnp.bfloat16))
    else:
        out_shape = [jax.ShapeDtypeStruct((freqs, col_tiles, 2 * rhs, tile), jnp.float32)]
    return pl.pallas_call(
        functools.partial(back_kernel, parts, groups, reps, tiles),
        in_specs=[pl.BlockSpec(memory_space=pltpu.VMEM)] * (3 + parts + len(carried)),
        out_specs=[pl.BlockSpec(memory_space=pltpu.VMEM)] * len(out_shape),
        out_shape=out_shape,
        scratch_shapes=scratch,
        compiler_params=pltpu.CompilerParams(vmem_limit_bytes=VMEM_LIMIT),
        cost_estimate=tile_cost(freqs * (tiles[1] - tiles[0]) * col_tiles, size, tile, rhs),
        name="back_project",
    )(limits, green_right, green_left, *misfit, *carried)


def gather_kernel(reps, *refs):
    part_refs, out_refs = refs[:reps], refs[reps:]
    for step, out_ref in enumerate(out_refs):
        total = sum(part_ref[step].astype(jnp.float32) for part_ref in part_refs)
        out_ref[...] = total.astype(out_ref.dtype)


def gather(parts):
    shape = parts[0].shape
    return pl.pallas_call(
        functools.partial(gather_kernel, len(parts)),
        in_specs=[pl.BlockSpec(memory_space=pltpu.VMEM)] * len(parts),
        out_specs=[pl.BlockSpec(memory_space=pltpu.VMEM)] * shape[0],
        out_shape=[jax.ShapeDtypeStruct(shape[1:], jnp.bfloat16)] * shape[0],
        compiler_params=pltpu.CompilerParams(vmem_limit_bytes=VMEM_LIMIT),
        name="gather",
    )(*parts)


def gradient_kernel(table_ref, *refs):
    part_refs, (out_hbm, out_ref, rows_ref, out_sems) = refs[-5::-1], refs[-4:]
    groups = len(part_refs)
    freqs, _, low, lanes = part_refs[0].shape
    high, _, rhs, length = out_ref.shape
    bins = table_ref.shape[0]
    chunks = out_sems.shape[0]
    part = low // chunks
    me = lax.axis_index("freq")
    for at, part_ref in enumerate(part_refs):
        g = origin(me, at, groups)
        for f in range(freqs):
            for c in range(2):
                rows = pl.ds(c * groups * freqs + g * freqs + f, low, stride=bins)
                rows_ref[rows, :] = part_ref[f, c].astype(jnp.float32)
    table = table_ref[...]
    copies = []
    for at in range(chunks):
        coefficients = jnp.concatenate(
            [rows_ref[row * bins : (row + 1) * bins] for row in range(at * part, (at + 1) * part)],
            axis=1,
        ).astype(jnp.bfloat16)
        traces = dot(coefficients, table, 0, 0).astype(out_ref.dtype)
        for row in range(part):
            out_ref[:, at * part + row] = traces[row * lanes : (row + 1) * lanes].reshape(
                high, rhs, length
            )
        rows = pl.ds(at * part, part)
        for h in range(high):
            copies.append(
                pltpu.make_async_copy(
                    out_ref.at[h, rows], out_hbm.at[h, rows], out_sems.at[at, h]
                )
            )
            copies[-1].start()
    for copy in copies:
        copy.wait()


def gradient_of(parts, table, rhs):
    _, _, low, lanes = parts[0].shape
    bins, length = table.shape
    high = lanes // rhs
    chunks = math.gcd(low, 4)
    shape = (high, low, rhs, length)
    out = pl.pallas_call(
        gradient_kernel,
        in_specs=[pl.BlockSpec(memory_space=pltpu.VMEM)] * (1 + len(parts)),
        out_specs=pl.BlockSpec(memory_space=pltpu.HBM),
        out_shape=jax.ShapeDtypeStruct(shape, jnp.bfloat16),
        scratch_shapes=[
            pltpu.VMEM(shape, jnp.bfloat16),
            pltpu.VMEM((low * bins, lanes), jnp.float32),
            pltpu.SemaphoreType.DMA((chunks, high)),
        ],
        compiler_params=pltpu.CompilerParams(vmem_limit_bytes=VMEM_LIMIT),
        name="gradient",
    )(table, *parts[::-1])
    return out.reshape(1, high * low, rhs, length)


def shards(model, green_left, green_right, ranks, data):
    freq_count = lax.axis_size("freq")
    tile_count = lax.axis_size("rtile")
    rep_count = lax.axis_size("rep")
    freq_local = ranks.shape[0]
    rhs_count = model.shape[2]
    table, spectrum = spectrum_of(model[0], freq_count, freq_local)
    spectrum = exchange(spectrum, "freq")
    limits = jnp.broadcast_to(ranks[..., None, None], ranks.shape + (1, LANES))
    row_tiles, _, _, tile = green_left.shape[2:]
    halves = [(0, row_tiles // 2), (row_tiles // 2, row_tiles)]
    predicted = [
        predict(limits, spectrum, green_right, green_left, tile_count, tiles) for tiles in halves
    ]
    residual = [
        residual_of(exchange(blocks, "rtile")[::-1], data, first * tile)
        for blocks, (first, _) in zip(predicted, halves)
    ]
    misfit = [exchange([half] * tile_count, "rtile") for half, _ in residual]
    partial = []
    for blocks, tiles in zip(misfit, halves):
        partial = back_project(
            limits, blocks, green_right, green_left, freq_count, rep_count, tiles, partial
        )
    arrived = exchange(gather(exchange(partial, "rep")), "freq")
    residual = jnp.concatenate([half for _, half in residual], axis=2)
    return (residual, gradient_of(arrived, table, rhs_count))


def solution(mesh):
    return jax.shard_map(
        shards,
        mesh=mesh,
        in_specs=(
            P("rtile", "freq", None, None),
            P(None, "freq", "rep", "rtile", None, None),
            P(None, "freq", "rep", "rtile", None, None),
            P("freq", "rep", "rtile"),
            P(None, ("freq", "rtile"), "rep"),
        ),
        out_specs=(P(None, ("freq", "rtile"), "rep"), P("rtile", ("freq", "rep"), None, None)),
        check_vma=False,
    )
```

```python
import functools
import math

import jax
import jax.numpy as jnp
from jax import lax
from jax.experimental import pallas as pl
from jax.experimental.pallas import tpu as pltpu
from jax.sharding import PartitionSpec as P

LANES = 128
VMEM_LIMIT = 48 * 1024 * 1024


def tables(bins, length):
    row = lax.broadcasted_iota(jnp.int32, (bins, length), 0)
    sample = lax.broadcasted_iota(jnp.int32, (bins, length), 1)
    is_sine = row >= bins // 2
    freq_bin = jnp.where(is_sine, row - bins // 2, row) + 1
    phase = lax.rem(freq_bin * sample, length) + jnp.where(is_sine, length // 4, 0)
    quarter = lax.div(phase + length // 8, length // 4)
    angle = (phase - quarter * (length // 4)).astype(jnp.float32) * (2.0 * math.pi / length)
    square = angle * angle
    even = 1.0
    odd = 1.0
    for order in (8, 6, 4, 2):
        even = 1.0 - square * even * (1.0 / (order * (order - 1)))
        odd = 1.0 - square * odd * (1.0 / (order * (order + 1)))
    odd = odd * angle
    quarter = quarter & 3
    value = jnp.where((quarter & 1) == 0, even, odd)
    return jnp.where((quarter == 1) | (quarter == 2), -value, value).astype(jnp.bfloat16)


def dot(first, second, first_dim, second_dim):
    return lax.dot_general(
        first,
        second,
        (((first_dim,), (second_dim,)), ((), ())),
        preferred_element_type=jnp.float32,
    )


def turned(pair):
    half = pair.shape[1] // 2
    return jnp.concatenate([-pair[:, half:], pair[:, :half]], axis=1)


def target(me, step, count):
    return me ^ step if count & (count - 1) == 0 else lax.rem(me + step, count)


def origin(me, step, count):
    return me ^ step if count & (count - 1) == 0 else lax.rem(me + count - step, count)


def exchange(blocks, axis):
    count = len(blocks)
    arrived = []
    for step in range(count - 1, 0, -1):
        pairs = [(me, me ^ step if count & (count - 1) == 0 else (me + step) % count) for me in range(count)]
        arrived.append(lax.ppermute(blocks[step], axis, pairs))
    return [blocks[0]] + arrived[::-1]


def swap(block, axis, count, step):
    return lax.ppermute(block, axis, [(me, me ^ step) for me in range(count)])


def add_kernel(first_ref, second_ref, out_ref):
    total = first_ref[...].astype(jnp.float32) + second_ref[...].astype(jnp.float32)
    out_ref[...] = total.astype(out_ref.dtype)


def add(first, second):
    return pl.pallas_call(
        add_kernel,
        in_specs=[pl.BlockSpec(memory_space=pltpu.VMEM)] * 2,
        out_specs=pl.BlockSpec(memory_space=pltpu.VMEM),
        out_shape=jax.ShapeDtypeStruct(first.shape, first.dtype),
        compiler_params=pltpu.CompilerParams(vmem_limit_bytes=VMEM_LIMIT),
        name="add",
    )(first, second)


def scatter_sums(blocks, axis):
    count = len(blocks)
    if count != 4:
        return exchange(blocks, axis)[::-1]
    far = swap(blocks[3], axis, count, 1)
    near = swap(blocks[1], axis, count, 1)
    across = swap(add(blocks[2], far), axis, count, 2)
    return [across, near, blocks[0]]


def collect(block, axis, count):
    if count != 4:
        return exchange([block] * count, axis)
    across = swap(block, axis, count, 2)
    near = swap(block, axis, count, 1)
    return [block, near, across, swap(across, axis, count, 1)]


def spectrum_kernel(model_hbm, table_out_ref, *refs):
    out_refs = refs[:-3]
    model_ref, rows_ref, model_sems = refs[-3:]
    high, low, rhs, length = model_ref.shape
    dests = len(out_refs)
    freqs, _, _, lanes = out_refs[0].shape
    bins = 2 * dests * freqs
    chunks = model_sems.shape[0]
    part = low // chunks
    copies = []
    for at in range(chunks):
        rows = pl.ds(at * part, part)
        copies.append(
            pltpu.make_async_copy(
                model_hbm.at[:, rows], model_ref.at[:, rows], model_sems.at[at]
            )
        )
        copies[-1].start()
    table = tables(bins, length)
    table_out_ref[...] = table
    for at in range(chunks):
        copies[at].wait()
        for start in range(at * part, (at + 1) * part, 2):
            width = min(2, (at + 1) * part - start)
            block = jnp.concatenate(
                [model_ref[:, start + row].reshape(lanes, length) for row in range(width)]
            )
            sums = dot(table, block, 1, 1)
            for row in range(width):
                place = (start + row) * bins
                rows_ref[place : place + bins] = sums[:, row * lanes : (row + 1) * lanes]
    me = lax.axis_index("freq")
    for at, out_ref in enumerate(out_refs):
        dest = target(me, at, dests)
        for f in range(freqs):
            for c in range(2):
                q = c * dests * freqs + dest * freqs + f
                out_ref[f, c] = rows_ref[pl.ds(q, low, stride=bins), :].astype(out_ref.dtype)


def spectrum_of(model, dests, freqs):
    traces, rhs, length = model.shape
    high = LANES // rhs
    low = traces // high
    chunks = math.gcd(low, 4)
    bins = 2 * dests * freqs
    table, *blocks = pl.pallas_call(
        spectrum_kernel,
        in_specs=[pl.BlockSpec(memory_space=pltpu.HBM)],
        out_specs=[pl.BlockSpec(memory_space=pltpu.VMEM)] * (1 + dests),
        out_shape=[jax.ShapeDtypeStruct((bins, length), jnp.bfloat16)]
        + [jax.ShapeDtypeStruct((freqs, 2, low, LANES), jnp.bfloat16)] * dests,
        scratch_shapes=[
            pltpu.VMEM((high, low, rhs, length), model.dtype),
            pltpu.VMEM((low * bins, LANES), jnp.float32),
            pltpu.SemaphoreType.DMA((chunks,)),
        ],
        compiler_params=pltpu.CompilerParams(vmem_limit_bytes=VMEM_LIMIT),
        name="spectrum",
    )(model.reshape(high, low, rhs, length))
    return table, blocks


def tile_cost(count, size, tile, rhs):
    return pl.CostEstimate(
        flops=count * 2 * 8 * size * tile * rhs,
        bytes_accessed=count * 2 * 4 * size * tile,
        transcendentals=0,
    )


def masked(product, limits_ref, places, size):
    columns = product.shape[1]
    row = lax.broadcasted_iota(jnp.int32, (size, columns), 0)
    kept = [
        jnp.where(row < limits_ref[place][:, :columns], product[at * size : (at + 1) * size], 0.0)
        for at, place in enumerate(places)
    ]
    return [part.astype(jnp.bfloat16) for part in kept]


def spans(first, count, size):
    found = []
    at = first
    while at < first + count:
        length = min(size - at % size, first + count - at)
        found.append((at // size, at % size, length))
        at += length
    return found


def predict_kernel(groups, parts, limits_ref, right_ref, left_ref, *refs):
    arrived_refs, out_refs = refs[:groups], refs[groups : groups + parts]
    spec_ref, sum_ref = refs[groups + parts :]
    _, freqs, _, low, lanes = spec_ref.shape
    row_tiles, col_tiles, size, tile = left_ref.shape[2:]
    _, pairs, _ = out_refs[0].shape
    me = lax.axis_index("freq")
    for at, arrived_ref in enumerate(arrived_refs[::-1]):
        spec_ref[origin(me, at, groups)] = arrived_ref[...]
    rhs = parts * pairs // freqs
    high = lanes // rhs
    per_tile = groups // col_tiles
    products = {}
    for f in range(freqs):
        for j in range(col_tiles):
            halves = []
            for c in range(2):
                blocks = []
                for g in range(j * per_tile, (j + 1) * per_tile):
                    got = spec_ref[g, f, c]
                    if low % 16:
                        got = got.astype(jnp.float32)
                    blocks += [got[:, h * rhs : (h + 1) * rhs] for h in range(high)]
                halves.append(jnp.concatenate(blocks))
            first = jnp.concatenate(halves, axis=1).astype(jnp.bfloat16)
            second = jnp.concatenate([halves[1], -halves[0]], axis=1).astype(jnp.bfloat16)
            right = [right_ref[c, f, :, j].reshape(row_tiles * size, tile) for c in range(2)]
            products[f, j] = dot(right[0], first, 1, 0) + dot(right[1], second, 1, 0)
    factors = {}
    for f in range(freqs):
        projected = [
            masked(products[f, j], limits_ref, [(f, i, j) for i in range(row_tiles)], size)
            for j in range(col_tiles)
        ]
        for i in range(row_tiles):
            straight = [projected[j][i] for j in range(col_tiles)]
            factors[f, i] = jnp.concatenate(straight + [turned(part) for part in straight])
    for f in range(freqs):
        for i in range(row_tiles):
            left = left_ref[:, f, i].reshape(2 * col_tiles * size, tile)
            predicted = dot(factors[f, i], left, 0, 0)
            for c in range(2):
                row = c * rhs
                for part, start, length in spans(f * rhs, rhs, pairs):
                    sum_ref[part, c, start : start + length, i * tile : (i + 1) * tile] = predicted[
                        row : row + length
                    ]
                    row += length
    me = lax.axis_index("rtile")
    for at, out_ref in enumerate(out_refs):
        out_ref[...] = sum_ref[target(me, at, parts)].astype(out_ref.dtype)


def predict(limits, spectrum, green_right, green_left, parts):
    freqs, row_tiles, col_tiles, size, tile = green_left.shape[1:]
    groups = len(spectrum)
    _, _, low, _ = spectrum[0].shape
    rhs = LANES * groups * low // (col_tiles * tile)
    pairs = freqs * rhs
    sources = row_tiles * tile
    return pl.pallas_call(
        functools.partial(predict_kernel, groups, parts),
        in_specs=[pl.BlockSpec(memory_space=pltpu.VMEM)] * (3 + groups),
        out_specs=[pl.BlockSpec(memory_space=pltpu.VMEM)] * parts,
        out_shape=[jax.ShapeDtypeStruct((2, pairs // parts, sources), jnp.bfloat16)] * parts,
        scratch_shapes=[
            pltpu.VMEM((groups,) + spectrum[0].shape, jnp.bfloat16),
            pltpu.VMEM((parts, 2, pairs // parts, sources), jnp.float32),
        ],
        compiler_params=pltpu.CompilerParams(vmem_limit_bytes=VMEM_LIMIT),
        cost_estimate=tile_cost(freqs * row_tiles * col_tiles, size, tile, rhs),
        name="predict",
    )(limits, green_right, green_left, *spectrum[::-1])


def residual_kernel(data_ref, *refs):
    block_refs, (misfit_ref, *part_refs) = refs[:-3], refs[-3:]
    residual = sum(block_ref[...].astype(jnp.float32) for block_ref in block_refs) - data_ref[...]
    for c, part_ref in enumerate(part_refs):
        part_ref[...] = residual[c]
    misfit_ref[...] = residual.astype(misfit_ref.dtype)


def residual_of(blocks, data):
    shape = blocks[0].shape
    return pl.pallas_call(
        residual_kernel,
        in_specs=[pl.BlockSpec(memory_space=pltpu.VMEM)] * (1 + len(blocks)),
        out_specs=[pl.BlockSpec(memory_space=pltpu.VMEM)] * 3,
        out_shape=[
            jax.ShapeDtypeStruct(shape, jnp.bfloat16),
            jax.ShapeDtypeStruct(shape[1:], jnp.float32),
            jax.ShapeDtypeStruct(shape[1:], jnp.float32),
        ],
        compiler_params=pltpu.CompilerParams(vmem_limit_bytes=VMEM_LIMIT),
        name="residual",
    )(data, *blocks)


def back_kernel(parts, groups, reps, limits_ref, right_ref, left_ref, *refs):
    misfit_refs, out_refs = refs[:parts], refs[parts : parts + reps]
    misfit_all_ref, grad_ref = refs[parts + reps :]
    _, freqs, row_tiles, col_tiles, size, tile = left_ref.shape
    _, pairs, _ = misfit_refs[0].shape
    rhs = parts * pairs // freqs
    _, _, _, low, lanes = out_refs[0].shape
    high = lanes // rhs
    per_tile = groups * reps // col_tiles
    me = lax.axis_index("rtile")
    for at, misfit_ref in enumerate(misfit_refs):
        misfit_all_ref[origin(me, at, parts)] = misfit_ref[...].astype(jnp.float32)
    products = {}
    for f in range(freqs):
        for i in range(row_tiles):
            rows = [
                jnp.concatenate(
                    [
                        misfit_all_ref[part, c, start : start + length, i * tile : (i + 1) * tile]
                        for part, start, length in spans(f * rhs, rhs, pairs)
                    ]
                )
                for c in range(2)
            ]
            first = jnp.concatenate(rows).astype(jnp.bfloat16)
            second = jnp.concatenate([rows[1], -rows[0]]).astype(jnp.bfloat16)
            left = [left_ref[c, f, i].reshape(col_tiles * size, tile) for c in range(2)]
            products[f, i] = dot(left[0], first, 1, 1) + dot(left[1], second, 1, 1)
    factors = {}
    for f in range(freqs):
        back = [
            masked(products[f, i], limits_ref, [(f, i, j) for j in range(col_tiles)], size)
            for i in range(row_tiles)
        ]
        for j in range(col_tiles):
            straight = [part[j] for part in back]
            factors[f, j] = jnp.concatenate(straight + [turned(part) for part in straight])
    for f in range(freqs):
        for j in range(col_tiles):
            right = jnp.concatenate(
                [right_ref[c, f, :, j].reshape(row_tiles * size, tile) for c in range(2)]
            )
            grad = dot(factors[f, j], right, 0, 0)
            grad = (grad if low % 16 else grad.astype(out_refs[0].dtype)).T
            for at in range(per_tile):
                rows = at * high * low
                for c in range(2):
                    blocks = [
                        grad[rows + h * low : rows + (h + 1) * low, c * rhs : (c + 1) * rhs]
                        for h in range(high)
                    ]
                    grad_ref[j * per_tile + at, f, c] = jnp.concatenate(blocks, axis=1).astype(
                        grad_ref.dtype
                    )
    me, own = lax.axis_index("freq"), lax.axis_index("rep")
    for at, out_ref in enumerate(out_refs):
        rep = target(own, at, reps)
        for step in range(groups):
            out_ref[step] = grad_ref[target(me, step, groups) * reps + rep]


def back_project(limits, misfit, green_right, green_left, groups, reps):
    parts = len(misfit)
    _, pairs, sources = misfit[0].shape
    freqs, row_tiles, col_tiles, size, tile = green_left.shape[1:]
    rhs = parts * pairs // freqs
    low = col_tiles * tile * rhs // (groups * reps * LANES)
    block = (freqs, 2, low, LANES)
    return pl.pallas_call(
        functools.partial(back_kernel, parts, groups, reps),
        in_specs=[pl.BlockSpec(memory_space=pltpu.VMEM)] * (3 + parts),
        out_specs=[pl.BlockSpec(memory_space=pltpu.VMEM)] * reps,
        out_shape=[jax.ShapeDtypeStruct((groups,) + block, jnp.bfloat16)] * reps,
        scratch_shapes=[
            pltpu.VMEM((parts, 2, pairs, sources), jnp.float32),
            pltpu.VMEM((groups * reps,) + block, jnp.bfloat16),
        ],
        compiler_params=pltpu.CompilerParams(vmem_limit_bytes=VMEM_LIMIT),
        cost_estimate=tile_cost(freqs * row_tiles * col_tiles, size, tile, rhs),
        name="back_project",
    )(limits, green_right, green_left, *misfit)


def gather_kernel(reps, *refs):
    part_refs, out_refs = refs[:reps], refs[reps:]
    for step, out_ref in enumerate(out_refs):
        total = sum(part_ref[step].astype(jnp.float32) for part_ref in part_refs)
        out_ref[...] = total.astype(out_ref.dtype)


def gather(parts):
    shape = parts[0].shape
    return pl.pallas_call(
        functools.partial(gather_kernel, len(parts)),
        in_specs=[pl.BlockSpec(memory_space=pltpu.VMEM)] * len(parts),
        out_specs=[pl.BlockSpec(memory_space=pltpu.VMEM)] * shape[0],
        out_shape=[jax.ShapeDtypeStruct(shape[1:], jnp.bfloat16)] * shape[0],
        compiler_params=pltpu.CompilerParams(vmem_limit_bytes=VMEM_LIMIT),
        name="gather",
    )(*parts)


def gradient_kernel(table_ref, *refs):
    part_refs, (out_hbm, out_ref, rows_ref, out_sems) = refs[-5::-1], refs[-4:]
    groups = len(part_refs)
    freqs, _, low, lanes = part_refs[0].shape
    high, _, rhs, length = out_ref.shape
    bins = table_ref.shape[0]
    chunks = out_sems.shape[0]
    part = low // chunks
    me = lax.axis_index("freq")
    for at, part_ref in enumerate(part_refs):
        g = origin(me, at, groups)
        for f in range(freqs):
            for c in range(2):
                rows = pl.ds(c * groups * freqs + g * freqs + f, low, stride=bins)
                rows_ref[rows, :] = part_ref[f, c].astype(jnp.float32)
    table = table_ref[...]
    copies = []
    for at in range(chunks):
        coefficients = jnp.concatenate(
            [rows_ref[row * bins : (row + 1) * bins] for row in range(at * part, (at + 1) * part)],
            axis=1,
        ).astype(jnp.bfloat16)
        traces = dot(coefficients, table, 0, 0).astype(out_ref.dtype)
        for row in range(part):
            out_ref[:, at * part + row] = traces[row * lanes : (row + 1) * lanes].reshape(
                high, rhs, length
            )
        rows = pl.ds(at * part, part)
        copies.append(
            pltpu.make_async_copy(out_ref.at[:, rows], out_hbm.at[:, rows], out_sems.at[at])
        )
        copies[-1].start()
    for copy in copies:
        copy.wait()


def gradient_of(parts, table, rhs):
    _, _, low, lanes = parts[0].shape
    bins, length = table.shape
    high = lanes // rhs
    chunks = math.gcd(low, 4)
    shape = (high, low, rhs, length)
    out = pl.pallas_call(
        gradient_kernel,
        in_specs=[pl.BlockSpec(memory_space=pltpu.VMEM)] * (1 + len(parts)),
        out_specs=pl.BlockSpec(memory_space=pltpu.HBM),
        out_shape=jax.ShapeDtypeStruct(shape, jnp.bfloat16),
        scratch_shapes=[
            pltpu.VMEM(shape, jnp.bfloat16),
            pltpu.VMEM((low * bins, lanes), jnp.float32),
            pltpu.SemaphoreType.DMA((chunks,)),
        ],
        compiler_params=pltpu.CompilerParams(vmem_limit_bytes=VMEM_LIMIT),
        name="gradient",
    )(table, *parts[::-1])
    return out.reshape(1, high * low, rhs, length)


def shards(model, green_left, green_right, ranks, data):
    freq_count = lax.axis_size("freq")
    tile_count = lax.axis_size("rtile")
    rep_count = lax.axis_size("rep")
    freq_local = ranks.shape[0]
    rhs_count = model.shape[2]
    table, spectrum = spectrum_of(model[0], freq_count, freq_local)
    spectrum = exchange(spectrum, "freq")
    limits = jnp.broadcast_to(ranks[..., None, None], ranks.shape + (1, LANES))
    predicted = predict(limits, spectrum, green_right, green_left, tile_count)
    misfit, *residual = residual_of(scatter_sums(predicted, "rtile"), data)
    misfit = collect(misfit, "rtile", tile_count)
    partial = back_project(limits, misfit, green_right, green_left, freq_count, rep_count)
    arrived = exchange(gather(exchange(partial, "rep")), "freq")
    return (jnp.stack(residual), gradient_of(arrived, table, rhs_count))


def solution(mesh):
    return jax.shard_map(
        shards,
        mesh=mesh,
        in_specs=(
            P("rtile", "freq", None, None),
            P(None, "freq", "rep", "rtile", None, None),
            P(None, "freq", "rep", "rtile", None, None),
            P("freq", "rep", "rtile"),
            P(None, ("freq", "rtile"), "rep"),
        ),
        out_specs=(P(None, ("freq", "rtile"), "rep"), P("rtile", ("freq", "rep"), None, None)),
        check_vma=False,
    )
```

```python
import functools
import math

import jax
import jax.numpy as jnp
from jax import lax
from jax.experimental import pallas as pl
from jax.experimental.pallas import tpu as pltpu
from jax.sharding import PartitionSpec as P

LANES = 128
VMEM_LIMIT = 48 * 1024 * 1024


def tables(bins, length):
    row = lax.broadcasted_iota(jnp.int32, (bins, length), 0)
    sample = lax.broadcasted_iota(jnp.int32, (bins, length), 1)
    is_sine = row >= bins // 2
    freq_bin = jnp.where(is_sine, row - bins // 2, row) + 1
    phase = lax.rem(freq_bin * sample, length) + jnp.where(is_sine, length // 4, 0)
    quarter = lax.div(phase + length // 8, length // 4)
    angle = (phase - quarter * (length // 4)).astype(jnp.float32) * (2.0 * math.pi / length)
    square = angle * angle
    even = 1.0
    odd = 1.0
    for order in (8, 6, 4, 2):
        even = 1.0 - square * even * (1.0 / (order * (order - 1)))
        odd = 1.0 - square * odd * (1.0 / (order * (order + 1)))
    odd = odd * angle
    quarter = quarter & 3
    value = jnp.where((quarter & 1) == 0, even, odd)
    return jnp.where((quarter == 1) | (quarter == 2), -value, value).astype(jnp.bfloat16)


def dot(first, second, first_dim, second_dim):
    return lax.dot_general(
        first,
        second,
        (((first_dim,), (second_dim,)), ((), ())),
        preferred_element_type=jnp.float32,
    )


def turned(pair):
    half = pair.shape[1] // 2
    return jnp.concatenate([-pair[:, half:], pair[:, :half]], axis=1)


def target(me, step, count):
    return me ^ step if count & (count - 1) == 0 else lax.rem(me + step, count)


def origin(me, step, count):
    return me ^ step if count & (count - 1) == 0 else lax.rem(me + count - step, count)


def exchange(blocks, axis):
    count = len(blocks)
    arrived = []
    for step in range(count - 1, 0, -1):
        pairs = [(me, me ^ step if count & (count - 1) == 0 else (me + step) % count) for me in range(count)]
        arrived.append(lax.ppermute(blocks[step], axis, pairs))
    return [blocks[0]] + arrived[::-1]


def spectrum_kernel(model_hbm, table_out_ref, *refs):
    out_refs = refs[:-3]
    model_ref, rows_ref, model_sems = refs[-3:]
    high, low, rhs, length = model_ref.shape
    dests = len(out_refs)
    freqs, _, _, lanes = out_refs[0].shape
    bins = 2 * dests * freqs
    chunks = model_sems.shape[0]
    part = low // chunks
    copies = []
    for at in range(chunks):
        rows = pl.ds(at * part, part)
        copies.append(
            pltpu.make_async_copy(
                model_hbm.at[:, rows], model_ref.at[:, rows], model_sems.at[at]
            )
        )
        copies[-1].start()
    table = tables(bins, length)
    table_out_ref[...] = table
    for at in range(chunks):
        copies[at].wait()
        for start in range(at * part, (at + 1) * part, 2):
            width = min(2, (at + 1) * part - start)
            block = jnp.concatenate(
                [model_ref[:, start + row].reshape(lanes, length) for row in range(width)]
            )
            sums = dot(table, block, 1, 1)
            for row in range(width):
                place = (start + row) * bins
                rows_ref[place : place + bins] = sums[:, row * lanes : (row + 1) * lanes]
    me = lax.axis_index("freq")
    for at, out_ref in enumerate(out_refs):
        dest = target(me, at, dests)
        for f in range(freqs):
            for c in range(2):
                q = c * dests * freqs + dest * freqs + f
                out_ref[f, c] = rows_ref[pl.ds(q, low, stride=bins), :].astype(out_ref.dtype)


def spectrum_of(model, dests, freqs):
    traces, rhs, length = model.shape
    high = LANES // rhs
    low = traces // high
    chunks = math.gcd(low, 4)
    bins = 2 * dests * freqs
    table, *blocks = pl.pallas_call(
        spectrum_kernel,
        in_specs=[pl.BlockSpec(memory_space=pltpu.HBM)],
        out_specs=[pl.BlockSpec(memory_space=pltpu.VMEM)] * (1 + dests),
        out_shape=[jax.ShapeDtypeStruct((bins, length), jnp.bfloat16)]
        + [jax.ShapeDtypeStruct((freqs, 2, low, LANES), jnp.bfloat16)] * dests,
        scratch_shapes=[
            pltpu.VMEM((high, low, rhs, length), model.dtype),
            pltpu.VMEM((low * bins, LANES), jnp.float32),
            pltpu.SemaphoreType.DMA((chunks,)),
        ],
        compiler_params=pltpu.CompilerParams(vmem_limit_bytes=VMEM_LIMIT),
        name="spectrum",
    )(model.reshape(high, low, rhs, length))
    return table, blocks


def tile_cost(count, size, tile, rhs):
    return pl.CostEstimate(
        flops=count * 2 * 8 * size * tile * rhs,
        bytes_accessed=count * 2 * 4 * size * tile,
        transcendentals=0,
    )


def masked(product, limits_ref, places, size):
    columns = product.shape[1]
    row = lax.broadcasted_iota(jnp.int32, (size, columns), 0)
    kept = [
        jnp.where(row < limits_ref[place][:, :columns], product[at * size : (at + 1) * size], 0.0)
        for at, place in enumerate(places)
    ]
    return [part.astype(jnp.bfloat16) for part in kept]


def spans(first, count, size):
    found = []
    at = first
    while at < first + count:
        length = min(size - at % size, first + count - at)
        found.append((at // size, at % size, length))
        at += length
    return found


def project_tile(j, block_refs, tile_ref, limits_ref, right_ref):
    freqs, _, low, lanes = block_refs[0].shape
    _, _, row_tiles, _, size, tile = right_ref.shape
    high = tile // (len(block_refs) * low)
    rhs = lanes // high
    me = lax.axis_index("freq")
    for at, block_ref in enumerate(block_refs):
        tile_ref[(me ^ at) & (len(block_refs) - 1)] = block_ref[...]
    products = []
    for f in range(freqs):
        halves = []
        for c in range(2):
            blocks = []
            for g in range(len(block_refs)):
                got = tile_ref[g, f, c]
                if low % 16:
                    got = got.astype(jnp.float32)
                blocks += [got[:, h * rhs : (h + 1) * rhs] for h in range(high)]
            halves.append(jnp.concatenate(blocks))
        first = jnp.concatenate(halves, axis=1).astype(jnp.bfloat16)
        second = jnp.concatenate([halves[1], -halves[0]], axis=1).astype(jnp.bfloat16)
        right = [right_ref[c, f, :, j].reshape(row_tiles * size, tile) for c in range(2)]
        products.append(dot(right[0], first, 1, 0) + dot(right[1], second, 1, 0))
    return [
        masked(product, limits_ref, [(f, i, j) for i in range(row_tiles)], size)
        for f, product in enumerate(products)
    ]


def project_kernel(count, limits_ref, right_ref, *refs):
    block_refs, (out_ref, tile_ref) = refs[:count], refs[count:]
    j = lax.div(lax.axis_index("freq"), count)
    for f, parts in enumerate(project_tile(j, block_refs, tile_ref, limits_ref, right_ref)):
        for i, part in enumerate(parts):
            out_ref[f, i] = part


def project(limits, blocks, green_right):
    _, freqs, row_tiles, _, size, tile = green_right.shape
    _, _, low, _ = blocks[0].shape
    columns = 2 * LANES * len(blocks) * low // tile
    return pl.pallas_call(
        functools.partial(project_kernel, len(blocks)),
        in_specs=[pl.BlockSpec(memory_space=pltpu.VMEM)] * (2 + len(blocks)),
        out_specs=pl.BlockSpec(memory_space=pltpu.VMEM),
        out_shape=jax.ShapeDtypeStruct((freqs, row_tiles, size, columns), jnp.bfloat16),
        scratch_shapes=[pltpu.VMEM((len(blocks),) + blocks[0].shape, jnp.bfloat16)],
        compiler_params=pltpu.CompilerParams(vmem_limit_bytes=VMEM_LIMIT),
        cost_estimate=tile_cost(freqs * row_tiles, size, tile, columns // 4),
        name="project",
    )(limits, green_right, *blocks)


def predict_kernel(groups, parts, limits_ref, right_ref, left_ref, own_ref, *refs):
    _, freqs, row_tiles, col_tiles, size, tile = left_ref.shape
    per_tile = groups // col_tiles
    others = groups - per_tile
    block_refs, out_refs, (tile_ref, sum_ref) = (
        refs[:others][::-1],
        refs[others : others + parts],
        refs[others + parts :],
    )
    _, pairs, _ = out_refs[0].shape
    rhs = parts * pairs // freqs
    own = lax.div(lax.axis_index("freq"), per_tile)
    tiles = [own]
    projected = [[[own_ref[f, i] for i in range(row_tiles)] for f in range(freqs)]]
    for step in range(1, col_tiles):
        blocks = block_refs[(step - 1) * per_tile : step * per_tile]
        tiles.append(own ^ step)
        projected.append(project_tile(own ^ step, blocks, tile_ref, limits_ref, right_ref))
    factors = {}
    for f in range(freqs):
        for i in range(row_tiles):
            straight = [part[f][i] for part in projected]
            factors[f, i] = jnp.concatenate(straight + [turned(part) for part in straight])
    for f in range(freqs):
        for i in range(row_tiles):
            left = jnp.concatenate([left_ref[c, f, i, j] for c in range(2) for j in tiles])
            predicted = dot(factors[f, i], left, 0, 0)
            for c in range(2):
                row = c * rhs
                for part, start, length in spans(f * rhs, rhs, pairs):
                    sum_ref[part, c, start : start + length, i * tile : (i + 1) * tile] = predicted[
                        row : row + length
                    ]
                    row += length
    me = lax.axis_index("rtile")
    for at, out_ref in enumerate(out_refs):
        out_ref[...] = sum_ref[target(me, at, parts)].astype(out_ref.dtype)


def predict(limits, own, blocks, green_right, green_left, parts):
    freqs, row_tiles, col_tiles, size, tile = green_left.shape[1:]
    groups = len(blocks) * col_tiles // (col_tiles - 1)
    pairs = freqs * own.shape[3] // 2
    sources = row_tiles * tile
    return pl.pallas_call(
        functools.partial(predict_kernel, groups, parts),
        in_specs=[pl.BlockSpec(memory_space=pltpu.VMEM)] * (4 + len(blocks)),
        out_specs=[pl.BlockSpec(memory_space=pltpu.VMEM)] * parts,
        out_shape=[jax.ShapeDtypeStruct((2, pairs // parts, sources), jnp.bfloat16)] * parts,
        scratch_shapes=[
            pltpu.VMEM((groups // col_tiles,) + blocks[0].shape, jnp.bfloat16),
            pltpu.VMEM((parts, 2, pairs // parts, sources), jnp.float32),
        ],
        compiler_params=pltpu.CompilerParams(vmem_limit_bytes=VMEM_LIMIT),
        cost_estimate=tile_cost(freqs * row_tiles * col_tiles, size, tile, pairs // freqs),
        name="predict",
    )(limits, green_right, green_left, own, *blocks[::-1])


def residual_kernel(data_ref, *refs):
    block_refs, (misfit_ref, *part_refs) = refs[:-3], refs[-3:]
    residual = sum(block_ref[...].astype(jnp.float32) for block_ref in block_refs) - data_ref[...]
    for c, part_ref in enumerate(part_refs):
        part_ref[...] = residual[c]
    misfit_ref[...] = residual.astype(misfit_ref.dtype)


def residual_of(blocks, data):
    shape = blocks[0].shape
    return pl.pallas_call(
        residual_kernel,
        in_specs=[pl.BlockSpec(memory_space=pltpu.VMEM)] * (1 + len(blocks)),
        out_specs=[pl.BlockSpec(memory_space=pltpu.VMEM)] * 3,
        out_shape=[
            jax.ShapeDtypeStruct(shape, jnp.bfloat16),
            jax.ShapeDtypeStruct(shape[1:], jnp.float32),
            jax.ShapeDtypeStruct(shape[1:], jnp.float32),
        ],
        compiler_params=pltpu.CompilerParams(vmem_limit_bytes=VMEM_LIMIT),
        name="residual",
    )(data, *blocks)


def back_kernel(parts, groups, reps, limits_ref, right_ref, left_ref, *refs):
    misfit_refs, out_refs = refs[:parts], refs[parts : parts + reps]
    misfit_all_ref, grad_ref = refs[parts + reps :]
    _, freqs, row_tiles, col_tiles, size, tile = left_ref.shape
    _, pairs, _ = misfit_refs[0].shape
    rhs = parts * pairs // freqs
    _, _, _, low, lanes = out_refs[0].shape
    high = lanes // rhs
    per_tile = groups * reps // col_tiles
    me = lax.axis_index("rtile")
    for at, misfit_ref in enumerate(misfit_refs):
        misfit_all_ref[origin(me, at, parts)] = misfit_ref[...].astype(jnp.float32)
    products = {}
    for f in range(freqs):
        for i in range(row_tiles):
            rows = [
                jnp.concatenate(
                    [
                        misfit_all_ref[part, c, start : start + length, i * tile : (i + 1) * tile]
                        for part, start, length in spans(f * rhs, rhs, pairs)
                    ]
                )
                for c in range(2)
            ]
            first = jnp.concatenate(rows).astype(jnp.bfloat16)
            second = jnp.concatenate([rows[1], -rows[0]]).astype(jnp.bfloat16)
            left = [left_ref[c, f, i].reshape(col_tiles * size, tile) for c in range(2)]
            products[f, i] = dot(left[0], first, 1, 1) + dot(left[1], second, 1, 1)
    factors = {}
    for f in range(freqs):
        back = [
            masked(products[f, i], limits_ref, [(f, i, j) for j in range(col_tiles)], size)
            for i in range(row_tiles)
        ]
        for j in range(col_tiles):
            straight = [part[j] for part in back]
            factors[f, j] = jnp.concatenate(straight + [turned(part) for part in straight])
    for f in range(freqs):
        for j in range(col_tiles):
            right = jnp.concatenate(
                [right_ref[c, f, :, j].reshape(row_tiles * size, tile) for c in range(2)]
            )
            grad = dot(factors[f, j], right, 0, 0)
            grad = (grad if low % 16 else grad.astype(out_refs[0].dtype)).T
            for at in range(per_tile):
                rows = at * high * low
                for c in range(2):
                    blocks = [
                        grad[rows + h * low : rows + (h + 1) * low, c * rhs : (c + 1) * rhs]
                        for h in range(high)
                    ]
                    grad_ref[j * per_tile + at, f, c] = jnp.concatenate(blocks, axis=1).astype(
                        grad_ref.dtype
                    )
    me, own = lax.axis_index("freq"), lax.axis_index("rep")
    for at, out_ref in enumerate(out_refs):
        rep = target(own, at, reps)
        for step in range(groups):
            out_ref[step] = grad_ref[target(me, step, groups) * reps + rep]


def back_project(limits, misfit, green_right, green_left, groups, reps):
    parts = len(misfit)
    _, pairs, sources = misfit[0].shape
    freqs, row_tiles, col_tiles, size, tile = green_left.shape[1:]
    rhs = parts * pairs // freqs
    low = col_tiles * tile * rhs // (groups * reps * LANES)
    block = (freqs, 2, low, LANES)
    return pl.pallas_call(
        functools.partial(back_kernel, parts, groups, reps),
        in_specs=[pl.BlockSpec(memory_space=pltpu.VMEM)] * (3 + parts),
        out_specs=[pl.BlockSpec(memory_space=pltpu.VMEM)] * reps,
        out_shape=[jax.ShapeDtypeStruct((groups,) + block, jnp.bfloat16)] * reps,
        scratch_shapes=[
            pltpu.VMEM((parts, 2, pairs, sources), jnp.float32),
            pltpu.VMEM((groups * reps,) + block, jnp.bfloat16),
        ],
        compiler_params=pltpu.CompilerParams(vmem_limit_bytes=VMEM_LIMIT),
        cost_estimate=tile_cost(freqs * row_tiles * col_tiles, size, tile, rhs),
        name="back_project",
    )(limits, green_right, green_left, *misfit)


def gather_kernel(reps, *refs):
    part_refs, out_refs = refs[:reps], refs[reps:]
    for step, out_ref in enumerate(out_refs):
        total = sum(part_ref[step].astype(jnp.float32) for part_ref in part_refs)
        out_ref[...] = total.astype(out_ref.dtype)


def gather(parts):
    shape = parts[0].shape
    return pl.pallas_call(
        functools.partial(gather_kernel, len(parts)),
        in_specs=[pl.BlockSpec(memory_space=pltpu.VMEM)] * len(parts),
        out_specs=[pl.BlockSpec(memory_space=pltpu.VMEM)] * shape[0],
        out_shape=[jax.ShapeDtypeStruct(shape[1:], jnp.bfloat16)] * shape[0],
        compiler_params=pltpu.CompilerParams(vmem_limit_bytes=VMEM_LIMIT),
        name="gather",
    )(*parts)


def gradient_kernel(table_ref, *refs):
    part_refs, (out_hbm, out_ref, rows_ref, out_sems) = refs[-5::-1], refs[-4:]
    groups = len(part_refs)
    freqs, _, low, lanes = part_refs[0].shape
    high, _, rhs, length = out_ref.shape
    bins = table_ref.shape[0]
    chunks = out_sems.shape[0]
    part = low // chunks
    me = lax.axis_index("freq")
    for at, part_ref in enumerate(part_refs):
        g = origin(me, at, groups)
        for f in range(freqs):
            for c in range(2):
                rows = pl.ds(c * groups * freqs + g * freqs + f, low, stride=bins)
                rows_ref[rows, :] = part_ref[f, c].astype(jnp.float32)
    table = table_ref[...]
    width = math.gcd(length, 256)
    copies = []
    for at in range(chunks):
        coefficients = jnp.concatenate(
            [rows_ref[row * bins : (row + 1) * bins] for row in range(at * part, (at + 1) * part)],
            axis=1,
        ).astype(jnp.bfloat16)
        for column in range(0, length, width):
            columns = slice(column, column + width)
            traces = dot(coefficients, table[:, columns], 0, 0).astype(out_ref.dtype)
            for row in range(part):
                out_ref[:, at * part + row, :, columns] = traces[
                    row * lanes : (row + 1) * lanes
                ].reshape(high, rhs, width)
        rows = pl.ds(at * part, part)
        copies.append(
            pltpu.make_async_copy(out_ref.at[:, rows], out_hbm.at[:, rows], out_sems.at[at])
        )
        copies[-1].start()
    for copy in copies:
        copy.wait()


def gradient_of(parts, table, rhs):
    _, _, low, lanes = parts[0].shape
    bins, length = table.shape
    high = lanes // rhs
    chunks = math.gcd(low, 4)
    shape = (high, low, rhs, length)
    out = pl.pallas_call(
        gradient_kernel,
        in_specs=[pl.BlockSpec(memory_space=pltpu.VMEM)] * (1 + len(parts)),
        out_specs=pl.BlockSpec(memory_space=pltpu.HBM),
        out_shape=jax.ShapeDtypeStruct(shape, jnp.bfloat16),
        scratch_shapes=[
            pltpu.VMEM(shape, jnp.bfloat16),
            pltpu.VMEM((low * bins, lanes), jnp.float32),
            pltpu.SemaphoreType.DMA((chunks,)),
        ],
        compiler_params=pltpu.CompilerParams(vmem_limit_bytes=VMEM_LIMIT),
        name="gradient",
    )(table, *parts[::-1])
    return out.reshape(1, high * low, rhs, length)


def shards(model, green_left, green_right, ranks, data):
    freq_count = lax.axis_size("freq")
    tile_count = lax.axis_size("rtile")
    rep_count = lax.axis_size("rep")
    freq_local = ranks.shape[0]
    rhs_count = model.shape[2]
    table, spectrum = spectrum_of(model[0], freq_count, freq_local)
    spectrum = exchange(spectrum, "freq")
    limits = jnp.broadcast_to(ranks[..., None, None], ranks.shape + (1, LANES))
    per_tile = freq_count // green_right.shape[3]
    own = project(limits, spectrum[:per_tile], green_right)
    predicted = predict(limits, own, spectrum[per_tile:], green_right, green_left, tile_count)
    misfit, *residual = residual_of(exchange(predicted, "rtile")[::-1], data)
    misfit = exchange([misfit] * tile_count, "rtile")
    partial = back_project(limits, misfit, green_right, green_left, freq_count, rep_count)
    arrived = exchange(gather(exchange(partial, "rep")), "freq")
    return (jnp.stack(residual), gradient_of(arrived, table, rhs_count))


def solution(mesh):
    return jax.shard_map(
        shards,
        mesh=mesh,
        in_specs=(
            P("rtile", "freq", None, None),
            P(None, "freq", "rep", "rtile", None, None),
            P(None, "freq", "rep", "rtile", None, None),
            P("freq", "rep", "rtile"),
            P(None, ("freq", "rtile"), "rep"),
        ),
        out_specs=(P(None, ("freq", "rtile"), "rep"), P("rtile", ("freq", "rep"), None, None)),
        check_vma=False,
    )
```

```python
import functools
import math

import jax
import jax.numpy as jnp
from jax import lax
from jax.experimental import pallas as pl
from jax.experimental.pallas import tpu as pltpu
from jax.sharding import PartitionSpec as P

LANES = 128
VMEM_LIMIT = 48 * 1024 * 1024


def tables(bins, length):
    row = lax.broadcasted_iota(jnp.int32, (bins, length), 0)
    sample = lax.broadcasted_iota(jnp.int32, (bins, length), 1)
    is_sine = row >= bins // 2
    freq_bin = jnp.where(is_sine, row - bins // 2, row) + 1
    phase = lax.rem(freq_bin * sample, length) + jnp.where(is_sine, length // 4, 0)
    quarter = lax.div(phase + length // 8, length // 4)
    angle = (phase - quarter * (length // 4)).astype(jnp.float32) * (2.0 * math.pi / length)
    square = angle * angle
    even = 1.0
    odd = 1.0
    for order in (8, 6, 4, 2):
        even = 1.0 - square * even * (1.0 / (order * (order - 1)))
        odd = 1.0 - square * odd * (1.0 / (order * (order + 1)))
    odd = odd * angle
    quarter = quarter & 3
    value = jnp.where((quarter & 1) == 0, even, odd)
    return jnp.where((quarter == 1) | (quarter == 2), -value, value).astype(jnp.bfloat16)


def dot(first, second, first_dim, second_dim):
    return lax.dot_general(
        first,
        second,
        (((first_dim,), (second_dim,)), ((), ())),
        preferred_element_type=jnp.float32,
    )


def turned(pair):
    half = pair.shape[1] // 2
    return jnp.concatenate([-pair[:, half:], pair[:, :half]], axis=1)


def target(me, step, count):
    return me ^ step if count & (count - 1) == 0 else lax.rem(me + step, count)


def origin(me, step, count):
    return me ^ step if count & (count - 1) == 0 else lax.rem(me + count - step, count)


def exchange(blocks, axis):
    count = len(blocks)
    arrived = []
    for step in range(count - 1, 0, -1):
        pairs = [(me, me ^ step if count & (count - 1) == 0 else (me + step) % count) for me in range(count)]
        arrived.append(lax.ppermute(blocks[step], axis, pairs))
    return [blocks[0]] + arrived[::-1]


def shared_steps(groups, reps):
    return groups == 4 and reps == 2


def spectrum_kernel(model_hbm, table_out_ref, *refs):
    out_refs = refs[:-3]
    model_ref, rows_ref, model_sems = refs[-3:]
    high, low, rhs, length = model_ref.shape
    dests = len(out_refs)
    freqs, _, _, lanes = out_refs[0].shape
    bins = 2 * dests * freqs
    chunks = model_sems.shape[0]
    part = low // chunks
    copies = []
    for at in range(chunks):
        rows = pl.ds(at * part, part)
        copies.append(
            pltpu.make_async_copy(
                model_hbm.at[:, rows], model_ref.at[:, rows], model_sems.at[at]
            )
        )
        copies[-1].start()
    table = tables(bins, length)
    table_out_ref[...] = table
    for at in range(chunks):
        copies[at].wait()
        for start in range(at * part, (at + 1) * part, 2):
            width = min(2, (at + 1) * part - start)
            block = jnp.concatenate(
                [model_ref[:, start + row].reshape(lanes, length) for row in range(width)]
            )
            sums = dot(table, block, 1, 1)
            for row in range(width):
                place = (start + row) * bins
                rows_ref[place : place + bins] = sums[:, row * lanes : (row + 1) * lanes]
    me = lax.axis_index("freq")
    for at, out_ref in enumerate(out_refs):
        dest = target(me, at, dests)
        for f in range(freqs):
            for c in range(2):
                q = c * dests * freqs + dest * freqs + f
                out_ref[f, c] = rows_ref[pl.ds(q, low, stride=bins), :].astype(out_ref.dtype)


def spectrum_of(model, dests, freqs):
    traces, rhs, length = model.shape
    high = LANES // rhs
    low = traces // high
    chunks = math.gcd(low, 4)
    bins = 2 * dests * freqs
    table, *blocks = pl.pallas_call(
        spectrum_kernel,
        in_specs=[pl.BlockSpec(memory_space=pltpu.HBM)],
        out_specs=[pl.BlockSpec(memory_space=pltpu.VMEM)] * (1 + dests),
        out_shape=[jax.ShapeDtypeStruct((bins, length), jnp.bfloat16)]
        + [jax.ShapeDtypeStruct((freqs, 2, low, LANES), jnp.bfloat16)] * dests,
        scratch_shapes=[
            pltpu.VMEM((high, low, rhs, length), model.dtype),
            pltpu.VMEM((low * bins, LANES), jnp.float32),
            pltpu.SemaphoreType.DMA((chunks,)),
        ],
        compiler_params=pltpu.CompilerParams(vmem_limit_bytes=VMEM_LIMIT),
        name="spectrum",
    )(model.reshape(high, low, rhs, length))
    return table, blocks


def tile_cost(count, size, tile, rhs):
    return pl.CostEstimate(
        flops=count * 2 * 8 * size * tile * rhs,
        bytes_accessed=count * 2 * 4 * size * tile,
        transcendentals=0,
    )


def masked(product, limits_ref, places, size):
    columns = product.shape[1]
    row = lax.broadcasted_iota(jnp.int32, (size, columns), 0)
    kept = [
        jnp.where(row < limits_ref[place][:, :columns], product[at * size : (at + 1) * size], 0.0)
        for at, place in enumerate(places)
    ]
    return [part.astype(jnp.bfloat16) for part in kept]


def spans(first, count, size):
    found = []
    at = first
    while at < first + count:
        length = min(size - at % size, first + count - at)
        found.append((at // size, at % size, length))
        at += length
    return found


def project_tile(j, block_refs, tile_ref, limits_ref, right_ref):
    freqs, _, low, lanes = block_refs[0].shape
    _, _, row_tiles, _, size, tile = right_ref.shape
    high = tile // (len(block_refs) * low)
    rhs = lanes // high
    me = lax.axis_index("freq")
    for at, block_ref in enumerate(block_refs):
        tile_ref[(me ^ at) & (len(block_refs) - 1)] = block_ref[...]
    products = []
    for f in range(freqs):
        halves = []
        for c in range(2):
            blocks = []
            for g in range(len(block_refs)):
                got = tile_ref[g, f, c]
                if low % 16:
                    got = got.astype(jnp.float32)
                blocks += [got[:, h * rhs : (h + 1) * rhs] for h in range(high)]
            halves.append(jnp.concatenate(blocks))
        first = jnp.concatenate(halves, axis=1).astype(jnp.bfloat16)
        second = jnp.concatenate([halves[1], -halves[0]], axis=1).astype(jnp.bfloat16)
        right = [right_ref[c, f, :, j].reshape(row_tiles * size, tile) for c in range(2)]
        products.append(dot(right[0], first, 1, 0) + dot(right[1], second, 1, 0))
    return [
        masked(product, limits_ref, [(f, i, j) for i in range(row_tiles)], size)
        for f, product in enumerate(products)
    ]


def project_kernel(count, limits_ref, right_ref, *refs):
    block_refs, (out_ref, tile_ref) = refs[:count], refs[count:]
    j = lax.div(lax.axis_index("freq"), count)
    for f, parts in enumerate(project_tile(j, block_refs, tile_ref, limits_ref, right_ref)):
        for i, part in enumerate(parts):
            out_ref[f, i] = part


def project(limits, blocks, green_right):
    _, freqs, row_tiles, _, size, tile = green_right.shape
    _, _, low, _ = blocks[0].shape
    columns = 2 * LANES * len(blocks) * low // tile
    return pl.pallas_call(
        functools.partial(project_kernel, len(blocks)),
        in_specs=[pl.BlockSpec(memory_space=pltpu.VMEM)] * (2 + len(blocks)),
        out_specs=pl.BlockSpec(memory_space=pltpu.VMEM),
        out_shape=jax.ShapeDtypeStruct((freqs, row_tiles, size, columns), jnp.bfloat16),
        scratch_shapes=[pltpu.VMEM((len(blocks),) + blocks[0].shape, jnp.bfloat16)],
        compiler_params=pltpu.CompilerParams(vmem_limit_bytes=VMEM_LIMIT),
        cost_estimate=tile_cost(freqs * row_tiles, size, tile, columns // 4),
        name="project",
    )(limits, green_right, *blocks)


def predict_kernel(groups, parts, limits_ref, right_ref, left_ref, own_ref, *refs):
    _, freqs, row_tiles, col_tiles, size, tile = left_ref.shape
    per_tile = groups // col_tiles
    others = groups - per_tile
    block_refs, out_refs, (tile_ref, sum_ref) = (
        refs[:others][::-1],
        refs[others : others + parts],
        refs[others + parts :],
    )
    _, pairs, _ = out_refs[0].shape
    rhs = parts * pairs // freqs
    own = lax.div(lax.axis_index("freq"), per_tile)
    tiles = [own]
    projected = [[[own_ref[f, i] for i in range(row_tiles)] for f in range(freqs)]]
    for step in range(1, col_tiles):
        blocks = block_refs[(step - 1) * per_tile : step * per_tile]
        tiles.append(own ^ step)
        projected.append(project_tile(own ^ step, blocks, tile_ref, limits_ref, right_ref))
    factors = {}
    for f in range(freqs):
        for i in range(row_tiles):
            straight = [part[f][i] for part in projected]
            factors[f, i] = jnp.concatenate(straight + [turned(part) for part in straight])
    for f in range(freqs):
        for i in range(row_tiles):
            left = jnp.concatenate([left_ref[c, f, i, j] for c in range(2) for j in tiles])
            predicted = dot(factors[f, i], left, 0, 0)
            for c in range(2):
                row = c * rhs
                for part, start, length in spans(f * rhs, rhs, pairs):
                    sum_ref[part, c, start : start + length, i * tile : (i + 1) * tile] = predicted[
                        row : row + length
                    ]
                    row += length
    me = lax.axis_index("rtile")
    for at, out_ref in enumerate(out_refs):
        out_ref[...] = sum_ref[target(me, at, parts)].astype(out_ref.dtype)


def predict(limits, own, blocks, green_right, green_left, parts):
    freqs, row_tiles, col_tiles, size, tile = green_left.shape[1:]
    groups = len(blocks) * col_tiles // (col_tiles - 1)
    pairs = freqs * own.shape[3] // 2
    sources = row_tiles * tile
    return pl.pallas_call(
        functools.partial(predict_kernel, groups, parts),
        in_specs=[pl.BlockSpec(memory_space=pltpu.VMEM)] * (4 + len(blocks)),
        out_specs=[pl.BlockSpec(memory_space=pltpu.VMEM)] * parts,
        out_shape=[jax.ShapeDtypeStruct((2, pairs // parts, sources), jnp.bfloat16)] * parts,
        scratch_shapes=[
            pltpu.VMEM((groups // col_tiles,) + blocks[0].shape, jnp.bfloat16),
            pltpu.VMEM((parts, 2, pairs // parts, sources), jnp.float32),
        ],
        compiler_params=pltpu.CompilerParams(vmem_limit_bytes=VMEM_LIMIT),
        cost_estimate=tile_cost(freqs * row_tiles * col_tiles, size, tile, pairs // freqs),
        name="predict",
    )(limits, green_right, green_left, own, *blocks[::-1])


def residual_kernel(data_ref, *refs):
    block_refs, (misfit_ref, *part_refs) = refs[:-3], refs[-3:]
    residual = sum(block_ref[...].astype(jnp.float32) for block_ref in block_refs) - data_ref[...]
    for c, part_ref in enumerate(part_refs):
        part_ref[...] = residual[c]
    misfit_ref[...] = residual.astype(misfit_ref.dtype)


def residual_of(blocks, data):
    shape = blocks[0].shape
    return pl.pallas_call(
        residual_kernel,
        in_specs=[pl.BlockSpec(memory_space=pltpu.VMEM)] * (1 + len(blocks)),
        out_specs=[pl.BlockSpec(memory_space=pltpu.VMEM)] * 3,
        out_shape=[
            jax.ShapeDtypeStruct(shape, jnp.bfloat16),
            jax.ShapeDtypeStruct(shape[1:], jnp.float32),
            jax.ShapeDtypeStruct(shape[1:], jnp.float32),
        ],
        compiler_params=pltpu.CompilerParams(vmem_limit_bytes=VMEM_LIMIT),
        name="residual",
    )(data, *blocks)


def back_kernel(parts, groups, reps, limits_ref, right_ref, left_ref, *refs):
    misfit_refs, out_refs = refs[:parts], refs[parts : parts + reps]
    misfit_all_ref, grad_ref = refs[parts + reps :]
    _, freqs, row_tiles, col_tiles, size, tile = left_ref.shape
    _, pairs, _ = misfit_refs[0].shape
    rhs = parts * pairs // freqs
    _, _, _, low, lanes = out_refs[0].shape
    high = lanes // rhs
    per_tile = groups * reps // col_tiles
    me = lax.axis_index("rtile")
    for at, misfit_ref in enumerate(misfit_refs):
        misfit_all_ref[origin(me, at, parts)] = misfit_ref[...].astype(jnp.float32)
    products = {}
    for f in range(freqs):
        for i in range(row_tiles):
            rows = [
                jnp.concatenate(
                    [
                        misfit_all_ref[part, c, start : start + length, i * tile : (i + 1) * tile]
                        for part, start, length in spans(f * rhs, rhs, pairs)
                    ]
                )
                for c in range(2)
            ]
            first = jnp.concatenate(rows).astype(jnp.bfloat16)
            second = jnp.concatenate([rows[1], -rows[0]]).astype(jnp.bfloat16)
            left = [left_ref[c, f, i].reshape(col_tiles * size, tile) for c in range(2)]
            products[f, i] = dot(left[0], first, 1, 1) + dot(left[1], second, 1, 1)
    factors = {}
    for f in range(freqs):
        back = [
            masked(products[f, i], limits_ref, [(f, i, j) for j in range(col_tiles)], size)
            for i in range(row_tiles)
        ]
        for j in range(col_tiles):
            straight = [part[j] for part in back]
            factors[f, j] = jnp.concatenate(straight + [turned(part) for part in straight])
    for f in range(freqs):
        for j in range(col_tiles):
            right = jnp.concatenate(
                [right_ref[c, f, :, j].reshape(row_tiles * size, tile) for c in range(2)]
            )
            grad = dot(factors[f, j], right, 0, 0)
            grad = (grad if low % 16 else grad.astype(out_refs[0].dtype)).T
            for at in range(per_tile):
                rows = at * high * low
                for c in range(2):
                    blocks = [
                        grad[rows + h * low : rows + (h + 1) * low, c * rhs : (c + 1) * rhs]
                        for h in range(high)
                    ]
                    grad_ref[j * per_tile + at, f, c] = jnp.concatenate(blocks, axis=1).astype(
                        grad_ref.dtype
                    )
    me, own = lax.axis_index("freq"), lax.axis_index("rep")
    for at, out_ref in enumerate(out_refs):
        rep = target(own, at, reps)
        if shared_steps(groups, reps):
            places = [((1 + rep), 0), ((1 + rep), 1), (3, rep), (0, rep)]
        else:
            places = [(step, rep) for step in range(groups)]
        for slot, (step, core) in enumerate(places):
            out_ref[slot] = grad_ref[target(me, step, groups) * reps + core]


def back_project(limits, misfit, green_right, green_left, groups, reps):
    parts = len(misfit)
    _, pairs, sources = misfit[0].shape
    freqs, row_tiles, col_tiles, size, tile = green_left.shape[1:]
    rhs = parts * pairs // freqs
    low = col_tiles * tile * rhs // (groups * reps * LANES)
    block = (freqs, 2, low, LANES)
    return pl.pallas_call(
        functools.partial(back_kernel, parts, groups, reps),
        in_specs=[pl.BlockSpec(memory_space=pltpu.VMEM)] * (3 + parts),
        out_specs=[pl.BlockSpec(memory_space=pltpu.VMEM)] * reps,
        out_shape=[jax.ShapeDtypeStruct((groups,) + block, jnp.bfloat16)] * reps,
        scratch_shapes=[
            pltpu.VMEM((parts, 2, pairs, sources), jnp.float32),
            pltpu.VMEM((groups * reps,) + block, jnp.bfloat16),
        ],
        compiler_params=pltpu.CompilerParams(vmem_limit_bytes=VMEM_LIMIT),
        cost_estimate=tile_cost(freqs * row_tiles * col_tiles, size, tile, rhs),
        name="back_project",
    )(limits, green_right, green_left, *misfit)


def gather_kernel(reps, *refs):
    part_refs, out_refs = refs[:reps], refs[reps:]
    slot = 0
    for out_ref in out_refs:
        for at in range(out_ref.shape[0]):
            total = sum(part_ref[slot].astype(jnp.float32) for part_ref in part_refs)
            out_ref[at] = total.astype(out_ref.dtype)
            slot += 1


def gather(parts, counts):
    shape = parts[0].shape[1:]
    return pl.pallas_call(
        functools.partial(gather_kernel, len(parts)),
        in_specs=[pl.BlockSpec(memory_space=pltpu.VMEM)] * len(parts),
        out_specs=[pl.BlockSpec(memory_space=pltpu.VMEM)] * len(counts),
        out_shape=[jax.ShapeDtypeStruct((count,) + shape, jnp.bfloat16) for count in counts],
        compiler_params=pltpu.CompilerParams(vmem_limit_bytes=VMEM_LIMIT),
        name="gather",
    )(*parts)


def other_kernel(pair_ref, out_ref):
    out_ref[0] = pair_ref[1 - lax.axis_index("rep")]


def other(pair):
    return pl.pallas_call(
        other_kernel,
        in_specs=[pl.BlockSpec(memory_space=pltpu.VMEM)],
        out_specs=pl.BlockSpec(memory_space=pltpu.VMEM),
        out_shape=jax.ShapeDtypeStruct((1,) + pair.shape[1:], pair.dtype),
        compiler_params=pltpu.CompilerParams(vmem_limit_bytes=VMEM_LIMIT),
        name="other",
    )(pair)


def return_spectra(parts):
    groups, reps = parts[0].shape[0], len(parts)
    parts = exchange(parts, "rep")
    if not shared_steps(groups, reps):
        return exchange(gather(parts, [1] * groups), "freq")
    pair, last, own = gather(parts, [2, 1, 1])
    devices = [(chip, core) for chip in range(groups) for core in range(reps)]
    near = [(chip * reps + core, (chip ^ (1 + core)) * reps + core) for chip, core in devices]
    far = [(chip * reps + core, (chip ^ 3) * reps + core) for chip, core in devices]
    pair = lax.ppermute(pair, ("freq", "rep"), near)
    last = lax.ppermute(last, ("freq", "rep"), far)
    swapped = lax.ppermute(other(pair), "rep", [(0, 1), (1, 0)])
    return [own, pair, swapped, last]


def gradient_kernel(reps, table_ref, *refs):
    part_refs, (out_hbm, out_ref, rows_ref, out_sems) = refs[-5::-1], refs[-4:]
    groups = len(part_refs)
    _, freqs, _, low, lanes = part_refs[0].shape
    high, _, rhs, length = out_ref.shape
    bins = table_ref.shape[0]
    chunks = out_sems.shape[0]
    part = low // chunks
    me = lax.axis_index("freq")
    if shared_steps(groups, reps):
        core = lax.axis_index("rep")
        places = [(0, 0), (1 + core, core), (2 - core, 0), (3, 0)]
    else:
        places = [(step, 0) for step in range(groups)]
    for part_ref, (step, place) in zip(part_refs, places):
        g = origin(me, step, groups)
        for f in range(freqs):
            for c in range(2):
                rows = pl.ds(c * groups * freqs + g * freqs + f, low, stride=bins)
                rows_ref[rows, :] = part_ref[place, f, c].astype(jnp.float32)
    table = table_ref[...]
    width = math.gcd(length, 256)
    copies = []
    for at in range(chunks):
        coefficients = jnp.concatenate(
            [rows_ref[row * bins : (row + 1) * bins] for row in range(at * part, (at + 1) * part)],
            axis=1,
        ).astype(jnp.bfloat16)
        for column in range(0, length, width):
            columns = slice(column, column + width)
            traces = dot(coefficients, table[:, columns], 0, 0).astype(out_ref.dtype)
            for row in range(part):
                out_ref[:, at * part + row, :, columns] = traces[
                    row * lanes : (row + 1) * lanes
                ].reshape(high, rhs, width)
        rows = pl.ds(at * part, part)
        copies.append(
            pltpu.make_async_copy(out_ref.at[:, rows], out_hbm.at[:, rows], out_sems.at[at])
        )
        copies[-1].start()
    for copy in copies:
        copy.wait()


def gradient_of(parts, table, rhs, reps):
    _, _, _, low, lanes = parts[0].shape
    bins, length = table.shape
    high = lanes // rhs
    chunks = math.gcd(low, 4)
    shape = (high, low, rhs, length)
    out = pl.pallas_call(
        functools.partial(gradient_kernel, reps),
        in_specs=[pl.BlockSpec(memory_space=pltpu.VMEM)] * (1 + len(parts)),
        out_specs=pl.BlockSpec(memory_space=pltpu.HBM),
        out_shape=jax.ShapeDtypeStruct(shape, jnp.bfloat16),
        scratch_shapes=[
            pltpu.VMEM(shape, jnp.bfloat16),
            pltpu.VMEM((low * bins, lanes), jnp.float32),
            pltpu.SemaphoreType.DMA((chunks,)),
        ],
        compiler_params=pltpu.CompilerParams(vmem_limit_bytes=VMEM_LIMIT),
        name="gradient",
    )(table, *parts[::-1])
    return out.reshape(1, high * low, rhs, length)


def shards(model, green_left, green_right, ranks, data):
    freq_count = lax.axis_size("freq")
    tile_count = lax.axis_size("rtile")
    rep_count = lax.axis_size("rep")
    freq_local = ranks.shape[0]
    rhs_count = model.shape[2]
    table, spectrum = spectrum_of(model[0], freq_count, freq_local)
    spectrum = exchange(spectrum, "freq")
    limits = jnp.broadcast_to(ranks[..., None, None], ranks.shape + (1, LANES))
    per_tile = freq_count // green_right.shape[3]
    own = project(limits, spectrum[:per_tile], green_right)
    predicted = predict(limits, own, spectrum[per_tile:], green_right, green_left, tile_count)
    misfit, *residual = residual_of(exchange(predicted, "rtile")[::-1], data)
    misfit = exchange([misfit] * tile_count, "rtile")
    partial = back_project(limits, misfit, green_right, green_left, freq_count, rep_count)
    arrived = return_spectra(partial)
    return (jnp.stack(residual), gradient_of(arrived, table, rhs_count, rep_count))


def solution(mesh):
    return jax.shard_map(
        shards,
        mesh=mesh,
        in_specs=(
            P("rtile", "freq", None, None),
            P(None, "freq", "rep", "rtile", None, None),
            P(None, "freq", "rep", "rtile", None, None),
            P("freq", "rep", "rtile"),
            P(None, ("freq", "rtile"), "rep"),
        ),
        out_specs=(P(None, ("freq", "rtile"), "rep"), P("rtile", ("freq", "rep"), None, None)),
        check_vma=False,
    )
```

```python
import functools
import math

import jax
import jax.numpy as jnp
from jax import lax
from jax.experimental import pallas as pl
from jax.experimental.pallas import tpu as pltpu
from jax.sharding import PartitionSpec as P

LANES = 128
VMEM_LIMIT = 48 * 1024 * 1024


def tables(bins, length):
    row = lax.broadcasted_iota(jnp.int32, (bins, length), 0)
    sample = lax.broadcasted_iota(jnp.int32, (bins, length), 1)
    is_sine = row >= bins // 2
    freq_bin = jnp.where(is_sine, row - bins // 2, row) + 1
    phase = lax.rem(freq_bin * sample, length) + jnp.where(is_sine, length // 4, 0)
    quarter = lax.div(phase + length // 8, length // 4)
    angle = (phase - quarter * (length // 4)).astype(jnp.float32) * (2.0 * math.pi / length)
    square = angle * angle
    even = 1.0
    odd = 1.0
    for order in (8, 6, 4, 2):
        even = 1.0 - square * even * (1.0 / (order * (order - 1)))
        odd = 1.0 - square * odd * (1.0 / (order * (order + 1)))
    odd = odd * angle
    quarter = quarter & 3
    value = jnp.where((quarter & 1) == 0, even, odd)
    return jnp.where((quarter == 1) | (quarter == 2), -value, value).astype(jnp.bfloat16)


def dot(first, second, first_dim, second_dim):
    return lax.dot_general(
        first,
        second,
        (((first_dim,), (second_dim,)), ((), ())),
        preferred_element_type=jnp.float32,
    )


def turned(pair):
    half = pair.shape[1] // 2
    return jnp.concatenate([-pair[:, half:], pair[:, :half]], axis=1)


def target(me, step, count):
    return me ^ step if count & (count - 1) == 0 else lax.rem(me + step, count)


def origin(me, step, count):
    return me ^ step if count & (count - 1) == 0 else lax.rem(me + count - step, count)


def exchange(blocks, axis):
    count = len(blocks)
    arrived = []
    for step in range(count - 1, 0, -1):
        pairs = [(me, me ^ step if count & (count - 1) == 0 else (me + step) % count) for me in range(count)]
        arrived.append(lax.ppermute(blocks[step], axis, pairs))
    return [blocks[0]] + arrived[::-1]


def ramp(count):
    step = max(count // 4, 1)
    cuts = [0] + list(range(step // 2 or step, count, step)) + [count]
    return [(start, end - start) for start, end in zip(cuts, cuts[1:])]


def shared_steps(groups, reps):
    return groups == 4 and reps == 2


def spectrum_kernel(model_hbm, table_out_ref, *refs):
    out_refs = refs[:-3]
    model_ref, rows_ref, model_sems = refs[-3:]
    high, low, rhs, length = model_ref.shape
    dests = len(out_refs)
    freqs, _, _, lanes = out_refs[0].shape
    bins = 2 * dests * freqs
    chunks = ramp(low)
    copies = []
    for at, (start, length_of) in enumerate(chunks):
        rows = pl.ds(start, length_of)
        copies.append(
            pltpu.make_async_copy(
                model_hbm.at[:, rows], model_ref.at[:, rows], model_sems.at[at]
            )
        )
        copies[-1].start()
    table = tables(bins, length)
    table_out_ref[...] = table
    for copy, (begin, length_of) in zip(copies, chunks):
        copy.wait()
        for start in range(begin, begin + length_of, 2):
            width = min(2, begin + length_of - start)
            block = jnp.concatenate(
                [model_ref[:, start + row].reshape(lanes, length) for row in range(width)]
            )
            sums = dot(table, block, 1, 1)
            for row in range(width):
                place = (start + row) * bins
                rows_ref[place : place + bins] = sums[:, row * lanes : (row + 1) * lanes]
    me = lax.axis_index("freq")
    for at, out_ref in enumerate(out_refs):
        dest = target(me, at, dests)
        for f in range(freqs):
            for c in range(2):
                q = c * dests * freqs + dest * freqs + f
                out_ref[f, c] = rows_ref[pl.ds(q, low, stride=bins), :].astype(out_ref.dtype)


def spectrum_of(model, dests, freqs):
    traces, rhs, length = model.shape
    high = LANES // rhs
    low = traces // high
    chunks = len(ramp(low))
    bins = 2 * dests * freqs
    table, *blocks = pl.pallas_call(
        spectrum_kernel,
        in_specs=[pl.BlockSpec(memory_space=pltpu.HBM)],
        out_specs=[pl.BlockSpec(memory_space=pltpu.VMEM)] * (1 + dests),
        out_shape=[jax.ShapeDtypeStruct((bins, length), jnp.bfloat16)]
        + [jax.ShapeDtypeStruct((freqs, 2, low, LANES), jnp.bfloat16)] * dests,
        scratch_shapes=[
            pltpu.VMEM((high, low, rhs, length), model.dtype),
            pltpu.VMEM((low * bins, LANES), jnp.float32),
            pltpu.SemaphoreType.DMA((chunks,)),
        ],
        compiler_params=pltpu.CompilerParams(vmem_limit_bytes=VMEM_LIMIT),
        name="spectrum",
    )(model.reshape(high, low, rhs, length))
    return table, blocks


def tile_cost(count, size, tile, rhs):
    return pl.CostEstimate(
        flops=count * 2 * 8 * size * tile * rhs,
        bytes_accessed=count * 2 * 4 * size * tile,
        transcendentals=0,
    )


def limits_kernel(ranks_ref, table_ref, out_ref):
    freqs, row_tiles, col_tiles = ranks_ref.shape
    for f in range(freqs):
        for i in range(row_tiles):
            for j in range(col_tiles):
                rank = ranks_ref[f, i : i + 1, j : j + 1]
                out_ref[f, i, j] = jnp.broadcast_to(rank, (1, LANES))


def limits_of(ranks, table):
    return pl.pallas_call(
        limits_kernel,
        in_specs=[pl.BlockSpec(memory_space=pltpu.VMEM)] * 2,
        out_specs=pl.BlockSpec(memory_space=pltpu.VMEM),
        out_shape=jax.ShapeDtypeStruct(ranks.shape + (1, LANES), jnp.int32),
        compiler_params=pltpu.CompilerParams(vmem_limit_bytes=VMEM_LIMIT),
        name="limits",
    )(ranks, table)


def masked(product, limits_ref, places, size):
    columns = product.shape[1]
    row = lax.broadcasted_iota(jnp.int32, (size, columns), 0)
    kept = [
        jnp.where(row < limits_ref[place][:, :columns], product[at * size : (at + 1) * size], 0.0)
        for at, place in enumerate(places)
    ]
    return [part.astype(jnp.bfloat16) for part in kept]


def spans(first, count, size):
    found = []
    at = first
    while at < first + count:
        length = min(size - at % size, first + count - at)
        found.append((at // size, at % size, length))
        at += length
    return found


def project_tile(j, block_refs, tile_ref, limits_ref, right_ref):
    freqs, _, low, lanes = block_refs[0].shape
    _, _, row_tiles, _, size, tile = right_ref.shape
    high = tile // (len(block_refs) * low)
    rhs = lanes // high
    me = lax.axis_index("freq")
    for at, block_ref in enumerate(block_refs):
        tile_ref[(me ^ at) & (len(block_refs) - 1)] = block_ref[...]
    products = []
    for f in range(freqs):
        halves = []
        for c in range(2):
            blocks = []
            for g in range(len(block_refs)):
                got = tile_ref[g, f, c]
                if low % 16:
                    got = got.astype(jnp.float32)
                blocks += [got[:, h * rhs : (h + 1) * rhs] for h in range(high)]
            halves.append(jnp.concatenate(blocks))
        first = jnp.concatenate(halves, axis=1).astype(jnp.bfloat16)
        second = jnp.concatenate([halves[1], -halves[0]], axis=1).astype(jnp.bfloat16)
        right = [right_ref[c, f, :, j].reshape(row_tiles * size, tile) for c in range(2)]
        products.append(dot(right[0], first, 1, 0) + dot(right[1], second, 1, 0))
    return [
        masked(product, limits_ref, [(f, i, j) for i in range(row_tiles)], size)
        for f, product in enumerate(products)
    ]


def project_kernel(count, limits_ref, right_ref, *refs):
    block_refs, (out_ref, tile_ref) = refs[:count], refs[count:]
    j = lax.div(lax.axis_index("freq"), count)
    for f, parts in enumerate(project_tile(j, block_refs, tile_ref, limits_ref, right_ref)):
        for i, part in enumerate(parts):
            out_ref[f, i] = part


def project(limits, blocks, green_right):
    _, freqs, row_tiles, _, size, tile = green_right.shape
    _, _, low, _ = blocks[0].shape
    columns = 2 * LANES * len(blocks) * low // tile
    return pl.pallas_call(
        functools.partial(project_kernel, len(blocks)),
        in_specs=[pl.BlockSpec(memory_space=pltpu.VMEM)] * (2 + len(blocks)),
        out_specs=pl.BlockSpec(memory_space=pltpu.VMEM),
        out_shape=jax.ShapeDtypeStruct((freqs, row_tiles, size, columns), jnp.bfloat16),
        scratch_shapes=[pltpu.VMEM((len(blocks),) + blocks[0].shape, jnp.bfloat16)],
        compiler_params=pltpu.CompilerParams(vmem_limit_bytes=VMEM_LIMIT),
        cost_estimate=tile_cost(freqs * row_tiles, size, tile, columns // 4),
        name="project",
    )(limits, green_right, *blocks)


def predict_kernel(groups, parts, limits_ref, right_ref, left_ref, own_ref, *refs):
    _, freqs, row_tiles, col_tiles, size, tile = left_ref.shape
    per_tile = groups // col_tiles
    others = groups - per_tile
    block_refs, out_refs, (tile_ref, sum_ref) = (
        refs[:others][::-1],
        refs[others : others + parts],
        refs[others + parts :],
    )
    _, pairs, _ = out_refs[0].shape
    rhs = parts * pairs // freqs
    own = lax.div(lax.axis_index("freq"), per_tile)
    tiles = [own]
    projected = [[[own_ref[f, i] for i in range(row_tiles)] for f in range(freqs)]]
    for step in range(1, col_tiles):
        blocks = block_refs[(step - 1) * per_tile : step * per_tile]
        tiles.append(own ^ step)
        projected.append(project_tile(own ^ step, blocks, tile_ref, limits_ref, right_ref))
    factors = {}
    for f in range(freqs):
        for i in range(row_tiles):
            straight = [part[f][i] for part in projected]
            factors[f, i] = jnp.concatenate(straight + [turned(part) for part in straight])
    for f in range(freqs):
        for i in range(row_tiles):
            left = jnp.concatenate([left_ref[c, f, i, j] for c in range(2) for j in tiles])
            predicted = dot(factors[f, i], left, 0, 0)
            for c in range(2):
                row = c * rhs
                for part, start, length in spans(f * rhs, rhs, pairs):
                    sum_ref[part, c, start : start + length, i * tile : (i + 1) * tile] = predicted[
                        row : row + length
                    ]
                    row += length
    me = lax.axis_index("rtile")
    for at, out_ref in enumerate(out_refs):
        out_ref[...] = sum_ref[target(me, at, parts)].astype(out_ref.dtype)


def predict(limits, own, blocks, green_right, green_left, parts):
    freqs, row_tiles, col_tiles, size, tile = green_left.shape[1:]
    groups = len(blocks) * col_tiles // (col_tiles - 1)
    pairs = freqs * own.shape[3] // 2
    sources = row_tiles * tile
    return pl.pallas_call(
        functools.partial(predict_kernel, groups, parts),
        in_specs=[pl.BlockSpec(memory_space=pltpu.VMEM)] * (4 + len(blocks)),
        out_specs=[pl.BlockSpec(memory_space=pltpu.VMEM)] * parts,
        out_shape=[jax.ShapeDtypeStruct((2, pairs // parts, sources), jnp.bfloat16)] * parts,
        scratch_shapes=[
            pltpu.VMEM((groups // col_tiles,) + blocks[0].shape, jnp.bfloat16),
            pltpu.VMEM((parts, 2, pairs // parts, sources), jnp.float32),
        ],
        compiler_params=pltpu.CompilerParams(vmem_limit_bytes=VMEM_LIMIT),
        cost_estimate=tile_cost(freqs * row_tiles * col_tiles, size, tile, pairs // freqs),
        name="predict",
    )(limits, green_right, green_left, own, *blocks[::-1])


def residual_kernel(data_ref, *refs):
    block_refs, (misfit_ref, *part_refs) = refs[:-3], refs[-3:]
    residual = sum(block_ref[...].astype(jnp.float32) for block_ref in block_refs) - data_ref[...]
    for c, part_ref in enumerate(part_refs):
        part_ref[...] = residual[c]
    misfit_ref[...] = residual.astype(misfit_ref.dtype)


def residual_of(blocks, data):
    shape = blocks[0].shape
    return pl.pallas_call(
        residual_kernel,
        in_specs=[pl.BlockSpec(memory_space=pltpu.VMEM)] * (1 + len(blocks)),
        out_specs=[pl.BlockSpec(memory_space=pltpu.VMEM)] * 3,
        out_shape=[
            jax.ShapeDtypeStruct(shape, jnp.bfloat16),
            jax.ShapeDtypeStruct(shape[1:], jnp.float32),
            jax.ShapeDtypeStruct(shape[1:], jnp.float32),
        ],
        compiler_params=pltpu.CompilerParams(vmem_limit_bytes=VMEM_LIMIT),
        name="residual",
    )(data, *blocks)


def back_kernel(parts, groups, reps, limits_ref, right_ref, left_ref, *refs):
    misfit_refs, out_refs = refs[:parts], refs[parts : parts + reps]
    misfit_all_ref, grad_ref = refs[parts + reps :]
    _, freqs, row_tiles, col_tiles, size, tile = left_ref.shape
    _, pairs, _ = misfit_refs[0].shape
    rhs = parts * pairs // freqs
    _, _, _, low, lanes = out_refs[0].shape
    high = lanes // rhs
    per_tile = groups * reps // col_tiles
    me = lax.axis_index("rtile")
    for at, misfit_ref in enumerate(misfit_refs):
        misfit_all_ref[origin(me, at, parts)] = misfit_ref[...].astype(jnp.float32)
    products = {}
    for f in range(freqs):
        for i in range(row_tiles):
            rows = [
                jnp.concatenate(
                    [
                        misfit_all_ref[part, c, start : start + length, i * tile : (i + 1) * tile]
                        for part, start, length in spans(f * rhs, rhs, pairs)
                    ]
                )
                for c in range(2)
            ]
            first = jnp.concatenate(rows).astype(jnp.bfloat16)
            second = jnp.concatenate([rows[1], -rows[0]]).astype(jnp.bfloat16)
            left = [left_ref[c, f, i].reshape(col_tiles * size, tile) for c in range(2)]
            products[f, i] = dot(left[0], first, 1, 1) + dot(left[1], second, 1, 1)
    factors = {}
    for f in range(freqs):
        back = [
            masked(products[f, i], limits_ref, [(f, i, j) for j in range(col_tiles)], size)
            for i in range(row_tiles)
        ]
        for j in range(col_tiles):
            straight = [part[j] for part in back]
            factors[f, j] = jnp.concatenate(straight + [turned(part) for part in straight])
    for f in range(freqs):
        for j in range(col_tiles):
            right = jnp.concatenate(
                [right_ref[c, f, :, j].reshape(row_tiles * size, tile) for c in range(2)]
            )
            grad = dot(factors[f, j], right, 0, 0)
            grad = (grad if low % 16 else grad.astype(out_refs[0].dtype)).T
            for at in range(per_tile):
                rows = at * high * low
                for c in range(2):
                    blocks = [
                        grad[rows + h * low : rows + (h + 1) * low, c * rhs : (c + 1) * rhs]
                        for h in range(high)
                    ]
                    grad_ref[j * per_tile + at, f, c] = jnp.concatenate(blocks, axis=1).astype(
                        grad_ref.dtype
                    )
    me, own = lax.axis_index("freq"), lax.axis_index("rep")
    for at, out_ref in enumerate(out_refs):
        rep = target(own, at, reps)
        if shared_steps(groups, reps):
            places = [((1 + rep), 0), ((1 + rep), 1), (3, rep), (0, rep)]
        else:
            places = [(step, rep) for step in range(groups)]
        for slot, (step, core) in enumerate(places):
            out_ref[slot] = grad_ref[target(me, step, groups) * reps + core]


def back_project(limits, misfit, green_right, green_left, groups, reps):
    parts = len(misfit)
    _, pairs, sources = misfit[0].shape
    freqs, row_tiles, col_tiles, size, tile = green_left.shape[1:]
    rhs = parts * pairs // freqs
    low = col_tiles * tile * rhs // (groups * reps * LANES)
    block = (freqs, 2, low, LANES)
    return pl.pallas_call(
        functools.partial(back_kernel, parts, groups, reps),
        in_specs=[pl.BlockSpec(memory_space=pltpu.VMEM)] * (3 + parts),
        out_specs=[pl.BlockSpec(memory_space=pltpu.VMEM)] * reps,
        out_shape=[jax.ShapeDtypeStruct((groups,) + block, jnp.bfloat16)] * reps,
        scratch_shapes=[
            pltpu.VMEM((parts, 2, pairs, sources), jnp.float32),
            pltpu.VMEM((groups * reps,) + block, jnp.bfloat16),
        ],
        compiler_params=pltpu.CompilerParams(vmem_limit_bytes=VMEM_LIMIT),
        cost_estimate=tile_cost(freqs * row_tiles * col_tiles, size, tile, rhs),
        name="back_project",
    )(limits, green_right, green_left, *misfit)


def gather_kernel(reps, *refs):
    part_refs, out_refs = refs[:reps], refs[reps:]
    slot = 0
    for out_ref in out_refs:
        for at in range(out_ref.shape[0]):
            total = sum(part_ref[slot].astype(jnp.float32) for part_ref in part_refs)
            out_ref[at] = total.astype(out_ref.dtype)
            slot += 1


def gather(parts, counts):
    shape = parts[0].shape[1:]
    return pl.pallas_call(
        functools.partial(gather_kernel, len(parts)),
        in_specs=[pl.BlockSpec(memory_space=pltpu.VMEM)] * len(parts),
        out_specs=[pl.BlockSpec(memory_space=pltpu.VMEM)] * len(counts),
        out_shape=[jax.ShapeDtypeStruct((count,) + shape, jnp.bfloat16) for count in counts],
        compiler_params=pltpu.CompilerParams(vmem_limit_bytes=VMEM_LIMIT),
        name="gather",
    )(*parts)


def other_kernel(pair_ref, out_ref):
    out_ref[0] = pair_ref[1 - lax.axis_index("rep")]


def other(pair):
    return pl.pallas_call(
        other_kernel,
        in_specs=[pl.BlockSpec(memory_space=pltpu.VMEM)],
        out_specs=pl.BlockSpec(memory_space=pltpu.VMEM),
        out_shape=jax.ShapeDtypeStruct((1,) + pair.shape[1:], pair.dtype),
        compiler_params=pltpu.CompilerParams(vmem_limit_bytes=VMEM_LIMIT),
        name="other",
    )(pair)


def return_spectra(parts):
    groups, reps = parts[0].shape[0], len(parts)
    parts = exchange(parts, "rep")
    if not shared_steps(groups, reps):
        return exchange(gather(parts, [1] * groups), "freq")
    pair, last, own = gather(parts, [2, 1, 1])
    devices = [(chip, core) for chip in range(groups) for core in range(reps)]
    near = [(chip * reps + core, (chip ^ (1 + core)) * reps + core) for chip, core in devices]
    far = [(chip * reps + core, (chip ^ 3) * reps + core) for chip, core in devices]
    pair = lax.ppermute(pair, ("freq", "rep"), near)
    last = lax.ppermute(last, ("freq", "rep"), far)
    swapped = lax.ppermute(other(pair), "rep", [(0, 1), (1, 0)])
    return [own, pair, swapped, last]


def gradient_kernel(reps, table_ref, *refs):
    part_refs, (out_hbm, out_ref, rows_ref, out_sems) = refs[-5::-1], refs[-4:]
    groups = len(part_refs)
    _, freqs, _, low, lanes = part_refs[0].shape
    high, _, rhs, length = out_ref.shape
    bins = table_ref.shape[0]
    me = lax.axis_index("freq")
    if shared_steps(groups, reps):
        core = lax.axis_index("rep")
        places = [(0, 0), (1 + core, core), (2 - core, 0), (3, 0)]
    else:
        places = [(step, 0) for step in range(groups)]
    for part_ref, (step, place) in zip(part_refs, places):
        g = origin(me, step, groups)
        for f in range(freqs):
            for c in range(2):
                rows = pl.ds(c * groups * freqs + g * freqs + f, low, stride=bins)
                rows_ref[rows, :] = part_ref[place, f, c].astype(jnp.float32)
    table = table_ref[...]
    width = math.gcd(length, 256)
    copies = []
    for at, (start, part) in enumerate(ramp(low)):
        coefficients = jnp.concatenate(
            [rows_ref[row * bins : (row + 1) * bins] for row in range(start, start + part)],
            axis=1,
        ).astype(jnp.bfloat16)
        for column in range(0, length, width):
            columns = slice(column, column + width)
            traces = dot(coefficients, table[:, columns], 0, 0).astype(out_ref.dtype)
            for row in range(part):
                out_ref[:, start + row, :, columns] = traces[
                    row * lanes : (row + 1) * lanes
                ].reshape(high, rhs, width)
        rows = pl.ds(start, part)
        copies.append(
            pltpu.make_async_copy(out_ref.at[:, rows], out_hbm.at[:, rows], out_sems.at[at])
        )
        copies[-1].start()
    for copy in copies:
        copy.wait()


def gradient_of(parts, table, rhs, reps):
    _, _, _, low, lanes = parts[0].shape
    bins, length = table.shape
    high = lanes // rhs
    chunks = len(ramp(low))
    shape = (high, low, rhs, length)
    out = pl.pallas_call(
        functools.partial(gradient_kernel, reps),
        in_specs=[pl.BlockSpec(memory_space=pltpu.VMEM)] * (1 + len(parts)),
        out_specs=pl.BlockSpec(memory_space=pltpu.HBM),
        out_shape=jax.ShapeDtypeStruct(shape, jnp.bfloat16),
        scratch_shapes=[
            pltpu.VMEM(shape, jnp.bfloat16),
            pltpu.VMEM((low * bins, lanes), jnp.float32),
            pltpu.SemaphoreType.DMA((chunks,)),
        ],
        compiler_params=pltpu.CompilerParams(vmem_limit_bytes=VMEM_LIMIT),
        name="gradient",
    )(table, *parts[::-1])
    return out.reshape(1, high * low, rhs, length)


def shards(model, green_left, green_right, ranks, data):
    freq_count = lax.axis_size("freq")
    tile_count = lax.axis_size("rtile")
    rep_count = lax.axis_size("rep")
    freq_local = ranks.shape[0]
    rhs_count = model.shape[2]
    table, spectrum = spectrum_of(model[0], freq_count, freq_local)
    spectrum = exchange(spectrum, "freq")
    limits = limits_of(ranks, table)
    per_tile = freq_count // green_right.shape[3]
    own = project(limits, spectrum[:per_tile], green_right)
    predicted = predict(limits, own, spectrum[per_tile:], green_right, green_left, tile_count)
    misfit, *residual = residual_of(exchange(predicted, "rtile")[::-1], data)
    misfit = exchange([misfit] * tile_count, "rtile")
    partial = back_project(limits, misfit, green_right, green_left, freq_count, rep_count)
    arrived = return_spectra(partial)
    return (jnp.stack(residual), gradient_of(arrived, table, rhs_count, rep_count))


def solution(mesh):
    return jax.shard_map(
        shards,
        mesh=mesh,
        in_specs=(
            P("rtile", "freq", None, None),
            P(None, "freq", "rep", "rtile", None, None),
            P(None, "freq", "rep", "rtile", None, None),
            P("freq", "rep", "rtile"),
            P(None, ("freq", "rtile"), "rep"),
        ),
        out_specs=(P(None, ("freq", "rtile"), "rep"), P("rtile", ("freq", "rep"), None, None)),
        check_vma=False,
    )
```

```python
import functools
import math

import jax
import jax.numpy as jnp
from jax import lax
from jax.experimental import pallas as pl
from jax.experimental.pallas import tpu as pltpu
from jax.sharding import PartitionSpec as P

LANES = 128
VMEM_LIMIT = 48 * 1024 * 1024


def tables(bins, length):
    row = lax.broadcasted_iota(jnp.int32, (bins, length), 0)
    sample = lax.broadcasted_iota(jnp.int32, (bins, length), 1)
    is_sine = row >= bins // 2
    freq_bin = jnp.where(is_sine, row - bins // 2, row) + 1
    phase = lax.rem(freq_bin * sample, length) + jnp.where(is_sine, length // 4, 0)
    quarter = lax.div(phase + length // 8, length // 4)
    angle = (phase - quarter * (length // 4)).astype(jnp.float32) * (2.0 * math.pi / length)
    square = angle * angle
    even = 1.0
    odd = 1.0
    for order in (8, 6, 4, 2):
        even = 1.0 - square * even * (1.0 / (order * (order - 1)))
        odd = 1.0 - square * odd * (1.0 / (order * (order + 1)))
    odd = odd * angle
    quarter = quarter & 3
    value = jnp.where((quarter & 1) == 0, even, odd)
    return jnp.where((quarter == 1) | (quarter == 2), -value, value).astype(jnp.bfloat16)


def dot(first, second, first_dim, second_dim):
    return lax.dot_general(
        first,
        second,
        (((first_dim,), (second_dim,)), ((), ())),
        preferred_element_type=jnp.float32,
    )


def turned(pair):
    half = pair.shape[1] // 2
    return jnp.concatenate([-pair[:, half:], pair[:, :half]], axis=1)


def target(me, step, count):
    return me ^ step if count & (count - 1) == 0 else lax.rem(me + step, count)


def origin(me, step, count):
    return me ^ step if count & (count - 1) == 0 else lax.rem(me + count - step, count)


def exchange(blocks, axis):
    count = len(blocks)
    arrived = []
    for step in range(count - 1, 0, -1):
        pairs = [(me, me ^ step if count & (count - 1) == 0 else (me + step) % count) for me in range(count)]
        arrived.append(lax.ppermute(blocks[step], axis, pairs))
    return [blocks[0]] + arrived[::-1]


def ramp(count):
    step = max(count // 4, 1)
    cuts = [0] + list(range(step // 2 or step, count, step)) + [count]
    return [(start, end - start) for start, end in zip(cuts, cuts[1:])]


def shared_steps(groups, reps):
    return groups == 4 and reps == 2


def spectrum_kernel(model_hbm, table_out_ref, *refs):
    out_refs = refs[:-3]
    model_ref, rows_ref, model_sems = refs[-3:]
    high, low, rhs, length = model_ref.shape
    dests = len(out_refs)
    freqs, _, _, lanes = out_refs[0].shape
    bins = 2 * dests * freqs
    chunks = ramp(low)
    copies = []
    for at, (start, length_of) in enumerate(chunks):
        rows = pl.ds(start, length_of)
        copies.append(
            pltpu.make_async_copy(
                model_hbm.at[:, rows], model_ref.at[:, rows], model_sems.at[at]
            )
        )
        copies[-1].start(priority=at % 2)
    table = tables(bins, length)
    table_out_ref[...] = table
    for copy, (begin, length_of) in zip(copies, chunks):
        copy.wait()
        for start in range(begin, begin + length_of, 2):
            width = min(2, begin + length_of - start)
            block = jnp.concatenate(
                [model_ref[:, start + row].reshape(lanes, length) for row in range(width)]
            )
            sums = dot(table, block, 1, 1)
            for row in range(width):
                place = (start + row) * bins
                rows_ref[place : place + bins] = sums[:, row * lanes : (row + 1) * lanes]
    me = lax.axis_index("freq")
    for at, out_ref in enumerate(out_refs):
        dest = target(me, at, dests)
        for f in range(freqs):
            for c in range(2):
                q = c * dests * freqs + dest * freqs + f
                out_ref[f, c] = rows_ref[pl.ds(q, low, stride=bins), :].astype(out_ref.dtype)


def spectrum_of(model, dests, freqs):
    traces, rhs, length = model.shape
    high = LANES // rhs
    low = traces // high
    chunks = len(ramp(low))
    bins = 2 * dests * freqs
    table, *blocks = pl.pallas_call(
        spectrum_kernel,
        in_specs=[pl.BlockSpec(memory_space=pltpu.HBM)],
        out_specs=[pl.BlockSpec(memory_space=pltpu.VMEM)] * (1 + dests),
        out_shape=[jax.ShapeDtypeStruct((bins, length), jnp.bfloat16)]
        + [jax.ShapeDtypeStruct((freqs, 2, low, LANES), jnp.bfloat16)] * dests,
        scratch_shapes=[
            pltpu.VMEM((high, low, rhs, length), model.dtype),
            pltpu.VMEM((low * bins, LANES), jnp.float32),
            pltpu.SemaphoreType.DMA((chunks,)),
        ],
        compiler_params=pltpu.CompilerParams(vmem_limit_bytes=VMEM_LIMIT),
        name="spectrum",
    )(model.reshape(high, low, rhs, length))
    return table, blocks


def tile_cost(count, size, tile, rhs):
    return pl.CostEstimate(
        flops=count * 2 * 8 * size * tile * rhs,
        bytes_accessed=count * 2 * 4 * size * tile,
        transcendentals=0,
    )


def limits_kernel(ranks_ref, table_ref, out_ref):
    freqs, row_tiles, col_tiles = ranks_ref.shape
    for f in range(freqs):
        for i in range(row_tiles):
            for j in range(col_tiles):
                rank = ranks_ref[f, i : i + 1, j : j + 1]
                out_ref[f, i, j] = jnp.broadcast_to(rank, (1, LANES))


def limits_of(ranks, table):
    return pl.pallas_call(
        limits_kernel,
        in_specs=[pl.BlockSpec(memory_space=pltpu.VMEM)] * 2,
        out_specs=pl.BlockSpec(memory_space=pltpu.VMEM),
        out_shape=jax.ShapeDtypeStruct(ranks.shape + (1, LANES), jnp.int32),
        compiler_params=pltpu.CompilerParams(vmem_limit_bytes=VMEM_LIMIT),
        name="limits",
    )(ranks, table)


def masked(product, limits_ref, places, size):
    columns = product.shape[1]
    row = lax.broadcasted_iota(jnp.int32, (size, columns), 0)
    kept = [
        jnp.where(row < limits_ref[place][:, :columns], product[at * size : (at + 1) * size], 0.0)
        for at, place in enumerate(places)
    ]
    return [part.astype(jnp.bfloat16) for part in kept]


def spans(first, count, size):
    found = []
    at = first
    while at < first + count:
        length = min(size - at % size, first + count - at)
        found.append((at // size, at % size, length))
        at += length
    return found


def project_tile(j, block_refs, tile_ref, limits_ref, right_ref):
    freqs, _, low, lanes = block_refs[0].shape
    _, _, row_tiles, _, size, tile = right_ref.shape
    high = tile // (len(block_refs) * low)
    rhs = lanes // high
    me = lax.axis_index("freq")
    for at, block_ref in enumerate(block_refs):
        tile_ref[(me ^ at) & (len(block_refs) - 1)] = block_ref[...]
    products = []
    for f in range(freqs):
        halves = []
        for c in range(2):
            blocks = []
            for g in range(len(block_refs)):
                got = tile_ref[g, f, c]
                if low % 16:
                    got = got.astype(jnp.float32)
                blocks += [got[:, h * rhs : (h + 1) * rhs] for h in range(high)]
            halves.append(jnp.concatenate(blocks))
        first = jnp.concatenate(halves, axis=1).astype(jnp.bfloat16)
        second = jnp.concatenate([halves[1], -halves[0]], axis=1).astype(jnp.bfloat16)
        right = [right_ref[c, f, :, j].reshape(row_tiles * size, tile) for c in range(2)]
        products.append(dot(right[0], first, 1, 0) + dot(right[1], second, 1, 0))
    return [
        masked(product, limits_ref, [(f, i, j) for i in range(row_tiles)], size)
        for f, product in enumerate(products)
    ]


def project_kernel(count, limits_ref, right_ref, *refs):
    block_refs, (out_ref, tile_ref) = refs[:count], refs[count:]
    j = lax.div(lax.axis_index("freq"), count)
    for f, parts in enumerate(project_tile(j, block_refs, tile_ref, limits_ref, right_ref)):
        for i, part in enumerate(parts):
            out_ref[f, i] = part


def project(limits, blocks, green_right):
    _, freqs, row_tiles, _, size, tile = green_right.shape
    _, _, low, _ = blocks[0].shape
    columns = 2 * LANES * len(blocks) * low // tile
    return pl.pallas_call(
        functools.partial(project_kernel, len(blocks)),
        in_specs=[pl.BlockSpec(memory_space=pltpu.VMEM)] * (2 + len(blocks)),
        out_specs=pl.BlockSpec(memory_space=pltpu.VMEM),
        out_shape=jax.ShapeDtypeStruct((freqs, row_tiles, size, columns), jnp.bfloat16),
        scratch_shapes=[pltpu.VMEM((len(blocks),) + blocks[0].shape, jnp.bfloat16)],
        compiler_params=pltpu.CompilerParams(vmem_limit_bytes=VMEM_LIMIT),
        cost_estimate=tile_cost(freqs * row_tiles, size, tile, columns // 4),
        name="project",
    )(limits, green_right, *blocks)


def predict_kernel(groups, parts, limits_ref, right_ref, left_ref, own_ref, *refs):
    _, freqs, row_tiles, col_tiles, size, tile = left_ref.shape
    per_tile = groups // col_tiles
    others = groups - per_tile
    block_refs, out_refs, (tile_ref, sum_ref) = (
        refs[:others][::-1],
        refs[others : others + parts],
        refs[others + parts :],
    )
    _, pairs, _ = out_refs[0].shape
    rhs = parts * pairs // freqs
    own = lax.div(lax.axis_index("freq"), per_tile)
    tiles = [own]
    projected = [[[own_ref[f, i] for i in range(row_tiles)] for f in range(freqs)]]
    for step in range(1, col_tiles):
        blocks = block_refs[(step - 1) * per_tile : step * per_tile]
        tiles.append(own ^ step)
        projected.append(project_tile(own ^ step, blocks, tile_ref, limits_ref, right_ref))
    factors = {}
    for f in range(freqs):
        for i in range(row_tiles):
            straight = [part[f][i] for part in projected]
            factors[f, i] = jnp.concatenate(straight + [turned(part) for part in straight])
    for f in range(freqs):
        for i in range(row_tiles):
            left = jnp.concatenate([left_ref[c, f, i, j] for c in range(2) for j in tiles])
            predicted = dot(factors[f, i], left, 0, 0)
            for c in range(2):
                row = c * rhs
                for part, start, length in spans(f * rhs, rhs, pairs):
                    sum_ref[part, c, start : start + length, i * tile : (i + 1) * tile] = predicted[
                        row : row + length
                    ]
                    row += length
    me = lax.axis_index("rtile")
    for at, out_ref in enumerate(out_refs):
        out_ref[...] = sum_ref[target(me, at, parts)].astype(out_ref.dtype)


def predict(limits, own, blocks, green_right, green_left, parts):
    freqs, row_tiles, col_tiles, size, tile = green_left.shape[1:]
    groups = len(blocks) * col_tiles // (col_tiles - 1)
    pairs = freqs * own.shape[3] // 2
    sources = row_tiles * tile
    return pl.pallas_call(
        functools.partial(predict_kernel, groups, parts),
        in_specs=[pl.BlockSpec(memory_space=pltpu.VMEM)] * (4 + len(blocks)),
        out_specs=[pl.BlockSpec(memory_space=pltpu.VMEM)] * parts,
        out_shape=[jax.ShapeDtypeStruct((2, pairs // parts, sources), jnp.bfloat16)] * parts,
        scratch_shapes=[
            pltpu.VMEM((groups // col_tiles,) + blocks[0].shape, jnp.bfloat16),
            pltpu.VMEM((parts, 2, pairs // parts, sources), jnp.float32),
        ],
        compiler_params=pltpu.CompilerParams(vmem_limit_bytes=VMEM_LIMIT),
        cost_estimate=tile_cost(freqs * row_tiles * col_tiles, size, tile, pairs // freqs),
        name="predict",
    )(limits, green_right, green_left, own, *blocks[::-1])


def residual_kernel(data_ref, *refs):
    block_refs, (misfit_ref, *part_refs) = refs[:-3], refs[-3:]
    residual = sum(block_ref[...].astype(jnp.float32) for block_ref in block_refs) - data_ref[...]
    for c, part_ref in enumerate(part_refs):
        part_ref[...] = residual[c]
    misfit_ref[...] = residual.astype(misfit_ref.dtype)


def residual_of(blocks, data):
    shape = blocks[0].shape
    return pl.pallas_call(
        residual_kernel,
        in_specs=[pl.BlockSpec(memory_space=pltpu.VMEM)] * (1 + len(blocks)),
        out_specs=[pl.BlockSpec(memory_space=pltpu.VMEM)] * 3,
        out_shape=[
            jax.ShapeDtypeStruct(shape, jnp.bfloat16),
            jax.ShapeDtypeStruct(shape[1:], jnp.float32),
            jax.ShapeDtypeStruct(shape[1:], jnp.float32),
        ],
        compiler_params=pltpu.CompilerParams(vmem_limit_bytes=VMEM_LIMIT),
        name="residual",
    )(data, *blocks)


def back_kernel(parts, groups, reps, limits_ref, right_ref, left_ref, *refs):
    misfit_refs, out_refs = refs[:parts], refs[parts : parts + reps]
    misfit_all_ref, grad_ref = refs[parts + reps :]
    _, freqs, row_tiles, col_tiles, size, tile = left_ref.shape
    _, pairs, _ = misfit_refs[0].shape
    rhs = parts * pairs // freqs
    _, _, _, low, lanes = out_refs[0].shape
    high = lanes // rhs
    per_tile = groups * reps // col_tiles
    me = lax.axis_index("rtile")
    for at, misfit_ref in enumerate(misfit_refs):
        misfit_all_ref[origin(me, at, parts)] = misfit_ref[...].astype(jnp.float32)
    products = {}
    for f in range(freqs):
        for i in range(row_tiles):
            rows = [
                jnp.concatenate(
                    [
                        misfit_all_ref[part, c, start : start + length, i * tile : (i + 1) * tile]
                        for part, start, length in spans(f * rhs, rhs, pairs)
                    ]
                )
                for c in range(2)
            ]
            first = jnp.concatenate(rows).astype(jnp.bfloat16)
            second = jnp.concatenate([rows[1], -rows[0]]).astype(jnp.bfloat16)
            left = [left_ref[c, f, i].reshape(col_tiles * size, tile) for c in range(2)]
            products[f, i] = dot(left[0], first, 1, 1) + dot(left[1], second, 1, 1)
    factors = {}
    for f in range(freqs):
        back = [
            masked(products[f, i], limits_ref, [(f, i, j) for j in range(col_tiles)], size)
            for i in range(row_tiles)
        ]
        for j in range(col_tiles):
            straight = [part[j] for part in back]
            factors[f, j] = jnp.concatenate(straight + [turned(part) for part in straight])
    for f in range(freqs):
        for j in range(col_tiles):
            right = jnp.concatenate(
                [right_ref[c, f, :, j].reshape(row_tiles * size, tile) for c in range(2)]
            )
            grad = dot(factors[f, j], right, 0, 0)
            grad = (grad if low % 16 else grad.astype(out_refs[0].dtype)).T
            for at in range(per_tile):
                rows = at * high * low
                for c in range(2):
                    blocks = [
                        grad[rows + h * low : rows + (h + 1) * low, c * rhs : (c + 1) * rhs]
                        for h in range(high)
                    ]
                    grad_ref[j * per_tile + at, f, c] = jnp.concatenate(blocks, axis=1).astype(
                        grad_ref.dtype
                    )
    me, own = lax.axis_index("freq"), lax.axis_index("rep")
    for at, out_ref in enumerate(out_refs):
        rep = target(own, at, reps)
        if shared_steps(groups, reps):
            places = [((1 + rep), 0), ((1 + rep), 1), (3, rep), (0, rep)]
        else:
            places = [(step, rep) for step in range(groups)]
        for slot, (step, core) in enumerate(places):
            out_ref[slot] = grad_ref[target(me, step, groups) * reps + core]


def back_project(limits, misfit, green_right, green_left, groups, reps):
    parts = len(misfit)
    _, pairs, sources = misfit[0].shape
    freqs, row_tiles, col_tiles, size, tile = green_left.shape[1:]
    rhs = parts * pairs // freqs
    low = col_tiles * tile * rhs // (groups * reps * LANES)
    block = (freqs, 2, low, LANES)
    return pl.pallas_call(
        functools.partial(back_kernel, parts, groups, reps),
        in_specs=[pl.BlockSpec(memory_space=pltpu.VMEM)] * (3 + parts),
        out_specs=[pl.BlockSpec(memory_space=pltpu.VMEM)] * reps,
        out_shape=[jax.ShapeDtypeStruct((groups,) + block, jnp.bfloat16)] * reps,
        scratch_shapes=[
            pltpu.VMEM((parts, 2, pairs, sources), jnp.float32),
            pltpu.VMEM((groups * reps,) + block, jnp.bfloat16),
        ],
        compiler_params=pltpu.CompilerParams(vmem_limit_bytes=VMEM_LIMIT),
        cost_estimate=tile_cost(freqs * row_tiles * col_tiles, size, tile, rhs),
        name="back_project",
    )(limits, green_right, green_left, *misfit)


def gather_kernel(reps, *refs):
    part_refs, out_refs = refs[:reps], refs[reps:]
    slot = 0
    for out_ref in out_refs:
        for at in range(out_ref.shape[0]):
            total = sum(part_ref[slot].astype(jnp.float32) for part_ref in part_refs)
            out_ref[at] = total.astype(out_ref.dtype)
            slot += 1


def gather(parts, counts):
    shape = parts[0].shape[1:]
    return pl.pallas_call(
        functools.partial(gather_kernel, len(parts)),
        in_specs=[pl.BlockSpec(memory_space=pltpu.VMEM)] * len(parts),
        out_specs=[pl.BlockSpec(memory_space=pltpu.VMEM)] * len(counts),
        out_shape=[jax.ShapeDtypeStruct((count,) + shape, jnp.bfloat16) for count in counts],
        compiler_params=pltpu.CompilerParams(vmem_limit_bytes=VMEM_LIMIT),
        name="gather",
    )(*parts)


def other_kernel(pair_ref, out_ref):
    out_ref[0] = pair_ref[1 - lax.axis_index("rep")]


def other(pair):
    return pl.pallas_call(
        other_kernel,
        in_specs=[pl.BlockSpec(memory_space=pltpu.VMEM)],
        out_specs=pl.BlockSpec(memory_space=pltpu.VMEM),
        out_shape=jax.ShapeDtypeStruct((1,) + pair.shape[1:], pair.dtype),
        compiler_params=pltpu.CompilerParams(vmem_limit_bytes=VMEM_LIMIT),
        name="other",
    )(pair)


def return_spectra(parts):
    groups, reps = parts[0].shape[0], len(parts)
    parts = exchange(parts, "rep")
    if not shared_steps(groups, reps):
        return exchange(gather(parts, [1] * groups), "freq")
    pair, last, own = gather(parts, [2, 1, 1])
    devices = [(chip, core) for chip in range(groups) for core in range(reps)]
    near = [(chip * reps + core, (chip ^ (1 + core)) * reps + core) for chip, core in devices]
    far = [(chip * reps + core, (chip ^ 3) * reps + core) for chip, core in devices]
    pair = lax.ppermute(pair, ("freq", "rep"), near)
    last = lax.ppermute(last, ("freq", "rep"), far)
    swapped = lax.ppermute(other(pair), "rep", [(0, 1), (1, 0)])
    return [own, pair, swapped, last]


def gradient_kernel(reps, table_ref, *refs):
    part_refs, (out_hbm, out_ref, rows_ref, out_sems) = refs[-5::-1], refs[-4:]
    groups = len(part_refs)
    _, freqs, _, low, lanes = part_refs[0].shape
    high, _, rhs, length = out_ref.shape
    bins = table_ref.shape[0]
    me = lax.axis_index("freq")
    if shared_steps(groups, reps):
        core = lax.axis_index("rep")
        places = [(0, 0), (1 + core, core), (2 - core, 0), (3, 0)]
    else:
        places = [(step, 0) for step in range(groups)]
    for part_ref, (step, place) in zip(part_refs, places):
        g = origin(me, step, groups)
        for f in range(freqs):
            for c in range(2):
                rows = pl.ds(c * groups * freqs + g * freqs + f, low, stride=bins)
                rows_ref[rows, :] = part_ref[place, f, c].astype(jnp.float32)
    table = table_ref[...]
    width = math.gcd(length, 256)
    copies = []
    for at, (start, part) in enumerate(ramp(low)):
        coefficients = jnp.concatenate(
            [rows_ref[row * bins : (row + 1) * bins] for row in range(start, start + part)],
            axis=1,
        ).astype(jnp.bfloat16)
        for column in range(0, length, width):
            columns = slice(column, column + width)
            traces = dot(coefficients, table[:, columns], 0, 0).astype(out_ref.dtype)
            for row in range(part):
                out_ref[:, start + row, :, columns] = traces[
                    row * lanes : (row + 1) * lanes
                ].reshape(high, rhs, width)
        rows = pl.ds(start, part)
        copies.append(
            pltpu.make_async_copy(out_ref.at[:, rows], out_hbm.at[:, rows], out_sems.at[at])
        )
        copies[-1].start(priority=at % 2)
    for copy in copies:
        copy.wait()


def gradient_of(parts, table, rhs, reps):
    _, _, _, low, lanes = parts[0].shape
    bins, length = table.shape
    high = lanes // rhs
    chunks = len(ramp(low))
    shape = (high, low, rhs, length)
    out = pl.pallas_call(
        functools.partial(gradient_kernel, reps),
        in_specs=[pl.BlockSpec(memory_space=pltpu.VMEM)] * (1 + len(parts)),
        out_specs=pl.BlockSpec(memory_space=pltpu.HBM),
        out_shape=jax.ShapeDtypeStruct(shape, jnp.bfloat16),
        scratch_shapes=[
            pltpu.VMEM(shape, jnp.bfloat16),
            pltpu.VMEM((low * bins, lanes), jnp.float32),
            pltpu.SemaphoreType.DMA((chunks,)),
        ],
        compiler_params=pltpu.CompilerParams(vmem_limit_bytes=VMEM_LIMIT),
        name="gradient",
    )(table, *parts[::-1])
    return out.reshape(1, high * low, rhs, length)


def shards(model, green_left, green_right, ranks, data):
    freq_count = lax.axis_size("freq")
    tile_count = lax.axis_size("rtile")
    rep_count = lax.axis_size("rep")
    freq_local = ranks.shape[0]
    rhs_count = model.shape[2]
    table, spectrum = spectrum_of(model[0], freq_count, freq_local)
    spectrum = exchange(spectrum, "freq")
    limits = limits_of(ranks, table)
    per_tile = freq_count // green_right.shape[3]
    own = project(limits, spectrum[:per_tile], green_right)
    predicted = predict(limits, own, spectrum[per_tile:], green_right, green_left, tile_count)
    misfit, *residual = residual_of(exchange(predicted, "rtile")[::-1], data)
    misfit = exchange([misfit] * tile_count, "rtile")
    partial = back_project(limits, misfit, green_right, green_left, freq_count, rep_count)
    arrived = return_spectra(partial)
    return (jnp.stack(residual), gradient_of(arrived, table, rhs_count, rep_count))


def solution(mesh):
    return jax.shard_map(
        shards,
        mesh=mesh,
        in_specs=(
            P("rtile", "freq", None, None),
            P(None, "freq", "rep", "rtile", None, None),
            P(None, "freq", "rep", "rtile", None, None),
            P("freq", "rep", "rtile"),
            P(None, ("freq", "rtile"), "rep"),
        ),
        out_specs=(P(None, ("freq", "rtile"), "rep"), P("rtile", ("freq", "rep"), None, None)),
        check_vma=False,
    )
```

```python
import functools
import math

import jax
import jax.numpy as jnp
from jax import lax
from jax.experimental import pallas as pl
from jax.experimental.pallas import tpu as pltpu
from jax.sharding import PartitionSpec as P

LANES = 128
VMEM_LIMIT = 48 * 1024 * 1024


def tables(bins, length):
    row = lax.broadcasted_iota(jnp.int32, (bins, length), 0)
    sample = lax.broadcasted_iota(jnp.int32, (bins, length), 1)
    is_sine = row >= bins // 2
    freq_bin = jnp.where(is_sine, row - bins // 2, row) + 1
    phase = lax.rem(freq_bin * sample, length) + jnp.where(is_sine, length // 4, 0)
    quarter = lax.div(phase + length // 8, length // 4)
    angle = (phase - quarter * (length // 4)).astype(jnp.float32) * (2.0 * math.pi / length)
    square = angle * angle
    even = 1.0
    odd = 1.0
    for order in (8, 6, 4, 2):
        even = 1.0 - square * even * (1.0 / (order * (order - 1)))
        odd = 1.0 - square * odd * (1.0 / (order * (order + 1)))
    odd = odd * angle
    quarter = quarter & 3
    value = jnp.where((quarter & 1) == 0, even, odd)
    return jnp.where((quarter == 1) | (quarter == 2), -value, value).astype(jnp.bfloat16)


def dot(first, second, first_dim, second_dim):
    return lax.dot_general(
        first,
        second,
        (((first_dim,), (second_dim,)), ((), ())),
        preferred_element_type=jnp.float32,
    )


def turned(pair):
    half = pair.shape[1] // 2
    return jnp.concatenate([-pair[:, half:], pair[:, :half]], axis=1)


def target(me, step, count):
    return me ^ step if count & (count - 1) == 0 else lax.rem(me + step, count)


def origin(me, step, count):
    return me ^ step if count & (count - 1) == 0 else lax.rem(me + count - step, count)


def exchange(blocks, axis):
    count = len(blocks)
    arrived = []
    for step in range(count - 1, 0, -1):
        pairs = [(me, me ^ step if count & (count - 1) == 0 else (me + step) % count) for me in range(count)]
        arrived.append(lax.ppermute(blocks[step], axis, pairs))
    return [blocks[0]] + arrived[::-1]


def ramp(count):
    step = max(count // 4, 1)
    cuts = [0] + list(range(step // 2 or step, count, step)) + [count]
    return [(start, end - start) for start, end in zip(cuts, cuts[1:])]


def shared_steps(groups, reps):
    return groups == 4 and reps == 2


def spectrum_kernel(model_hbm, table_out_ref, *refs):
    out_refs = refs[:-3]
    model_ref, rows_ref, model_sems = refs[-3:]
    high, low, rhs, length = model_ref.shape
    dests = len(out_refs)
    freqs, _, _, lanes = out_refs[0].shape
    bins = 2 * dests * freqs
    chunks = ramp(low)
    copies = []
    for at, (start, length_of) in enumerate(chunks):
        rows = pl.ds(start, length_of)
        copies.append(
            pltpu.make_async_copy(
                model_hbm.at[:, rows], model_ref.at[:, rows], model_sems.at[at]
            )
        )
        copies[-1].start(priority=1)
    table = tables(bins, length)
    table_out_ref[...] = table
    for copy, (begin, length_of) in zip(copies, chunks):
        copy.wait()
        for start in range(begin, begin + length_of, 2):
            width = min(2, begin + length_of - start)
            block = jnp.concatenate(
                [model_ref[:, start + row].reshape(lanes, length) for row in range(width)]
            )
            sums = dot(table, block, 1, 1)
            for row in range(width):
                place = (start + row) * bins
                rows_ref[place : place + bins] = sums[:, row * lanes : (row + 1) * lanes]
    me = lax.axis_index("freq")
    for at, out_ref in enumerate(out_refs):
        dest = target(me, at, dests)
        for f in range(freqs):
            for c in range(2):
                q = c * dests * freqs + dest * freqs + f
                out_ref[f, c] = rows_ref[pl.ds(q, low, stride=bins), :].astype(out_ref.dtype)


def spectrum_of(model, dests, freqs):
    traces, rhs, length = model.shape
    high = LANES // rhs
    low = traces // high
    chunks = len(ramp(low))
    bins = 2 * dests * freqs
    table, *blocks = pl.pallas_call(
        spectrum_kernel,
        in_specs=[pl.BlockSpec(memory_space=pltpu.HBM)],
        out_specs=[pl.BlockSpec(memory_space=pltpu.VMEM)] * (1 + dests),
        out_shape=[jax.ShapeDtypeStruct((bins, length), jnp.bfloat16)]
        + [jax.ShapeDtypeStruct((freqs, 2, low, LANES), jnp.bfloat16)] * dests,
        scratch_shapes=[
            pltpu.VMEM((high, low, rhs, length), model.dtype),
            pltpu.VMEM((low * bins, LANES), jnp.float32),
            pltpu.SemaphoreType.DMA((chunks,)),
        ],
        compiler_params=pltpu.CompilerParams(vmem_limit_bytes=VMEM_LIMIT),
        name="spectrum",
    )(model.reshape(high, low, rhs, length))
    return table, blocks


def tile_cost(count, size, tile, rhs):
    return pl.CostEstimate(
        flops=count * 2 * 8 * size * tile * rhs,
        bytes_accessed=count * 2 * 4 * size * tile,
        transcendentals=0,
    )


def limits_kernel(ranks_ref, table_ref, out_ref):
    freqs, row_tiles, col_tiles = ranks_ref.shape
    for f in range(freqs):
        for i in range(row_tiles):
            for j in range(col_tiles):
                rank = ranks_ref[f, i : i + 1, j : j + 1]
                out_ref[f, i, j] = jnp.broadcast_to(rank, (1, LANES))


def limits_of(ranks, table):
    return pl.pallas_call(
        limits_kernel,
        in_specs=[pl.BlockSpec(memory_space=pltpu.VMEM)] * 2,
        out_specs=pl.BlockSpec(memory_space=pltpu.VMEM),
        out_shape=jax.ShapeDtypeStruct(ranks.shape + (1, LANES), jnp.int32),
        compiler_params=pltpu.CompilerParams(vmem_limit_bytes=VMEM_LIMIT),
        name="limits",
    )(ranks, table)


def masked(product, limits_ref, places, size):
    columns = product.shape[1]
    row = lax.broadcasted_iota(jnp.int32, (size, columns), 0)
    kept = [
        jnp.where(row < limits_ref[place][:, :columns], product[at * size : (at + 1) * size], 0.0)
        for at, place in enumerate(places)
    ]
    return [part.astype(jnp.bfloat16) for part in kept]


def spans(first, count, size):
    found = []
    at = first
    while at < first + count:
        length = min(size - at % size, first + count - at)
        found.append((at // size, at % size, length))
        at += length
    return found


def project_tile(j, block_refs, tile_ref, limits_ref, right_ref):
    freqs, _, low, lanes = block_refs[0].shape
    _, _, row_tiles, _, size, tile = right_ref.shape
    high = tile // (len(block_refs) * low)
    rhs = lanes // high
    me = lax.axis_index("freq")
    for at, block_ref in enumerate(block_refs):
        tile_ref[(me ^ at) & (len(block_refs) - 1)] = block_ref[...]
    products = []
    for f in range(freqs):
        halves = []
        for c in range(2):
            blocks = []
            for g in range(len(block_refs)):
                got = tile_ref[g, f, c]
                if low % 16:
                    got = got.astype(jnp.float32)
                blocks += [got[:, h * rhs : (h + 1) * rhs] for h in range(high)]
            halves.append(jnp.concatenate(blocks))
        first = jnp.concatenate(halves, axis=1).astype(jnp.bfloat16)
        second = jnp.concatenate([halves[1], -halves[0]], axis=1).astype(jnp.bfloat16)
        right = [right_ref[c, f, :, j].reshape(row_tiles * size, tile) for c in range(2)]
        products.append(dot(right[0], first, 1, 0) + dot(right[1], second, 1, 0))
    return [
        masked(product, limits_ref, [(f, i, j) for i in range(row_tiles)], size)
        for f, product in enumerate(products)
    ]


def project_kernel(count, limits_ref, right_ref, *refs):
    block_refs, (out_ref, tile_ref) = refs[:count], refs[count:]
    j = lax.div(lax.axis_index("freq"), count)
    for f, parts in enumerate(project_tile(j, block_refs, tile_ref, limits_ref, right_ref)):
        for i, part in enumerate(parts):
            out_ref[f, i] = part


def project(limits, blocks, green_right):
    _, freqs, row_tiles, _, size, tile = green_right.shape
    _, _, low, _ = blocks[0].shape
    columns = 2 * LANES * len(blocks) * low // tile
    return pl.pallas_call(
        functools.partial(project_kernel, len(blocks)),
        in_specs=[pl.BlockSpec(memory_space=pltpu.VMEM)] * (2 + len(blocks)),
        out_specs=pl.BlockSpec(memory_space=pltpu.VMEM),
        out_shape=jax.ShapeDtypeStruct((freqs, row_tiles, size, columns), jnp.bfloat16),
        scratch_shapes=[pltpu.VMEM((len(blocks),) + blocks[0].shape, jnp.bfloat16)],
        compiler_params=pltpu.CompilerParams(vmem_limit_bytes=VMEM_LIMIT),
        cost_estimate=tile_cost(freqs * row_tiles, size, tile, columns // 4),
        name="project",
    )(limits, green_right, *blocks)


def predict_kernel(groups, parts, limits_ref, right_ref, left_ref, own_ref, *refs):
    _, freqs, row_tiles, col_tiles, size, tile = left_ref.shape
    per_tile = groups // col_tiles
    others = groups - per_tile
    block_refs, out_refs, (tile_ref, sum_ref) = (
        refs[:others][::-1],
        refs[others : others + parts],
        refs[others + parts :],
    )
    _, pairs, _ = out_refs[0].shape
    rhs = parts * pairs // freqs
    own = lax.div(lax.axis_index("freq"), per_tile)
    tiles = [own]
    projected = [[[own_ref[f, i] for i in range(row_tiles)] for f in range(freqs)]]
    for step in range(1, col_tiles):
        blocks = block_refs[(step - 1) * per_tile : step * per_tile]
        tiles.append(own ^ step)
        projected.append(project_tile(own ^ step, blocks, tile_ref, limits_ref, right_ref))
    factors = {}
    for f in range(freqs):
        for i in range(row_tiles):
            straight = [part[f][i] for part in projected]
            factors[f, i] = jnp.concatenate(straight + [turned(part) for part in straight])
    for f in range(freqs):
        for i in range(row_tiles):
            left = jnp.concatenate([left_ref[c, f, i, j] for c in range(2) for j in tiles])
            predicted = dot(factors[f, i], left, 0, 0)
            for c in range(2):
                row = c * rhs
                for part, start, length in spans(f * rhs, rhs, pairs):
                    sum_ref[part, c, start : start + length, i * tile : (i + 1) * tile] = predicted[
                        row : row + length
                    ]
                    row += length
    me = lax.axis_index("rtile")
    for at, out_ref in enumerate(out_refs):
        out_ref[...] = sum_ref[target(me, at, parts)].astype(out_ref.dtype)


def predict(limits, own, blocks, green_right, green_left, parts):
    freqs, row_tiles, col_tiles, size, tile = green_left.shape[1:]
    groups = len(blocks) * col_tiles // (col_tiles - 1)
    pairs = freqs * own.shape[3] // 2
    sources = row_tiles * tile
    return pl.pallas_call(
        functools.partial(predict_kernel, groups, parts),
        in_specs=[pl.BlockSpec(memory_space=pltpu.VMEM)] * (4 + len(blocks)),
        out_specs=[pl.BlockSpec(memory_space=pltpu.VMEM)] * parts,
        out_shape=[jax.ShapeDtypeStruct((2, pairs // parts, sources), jnp.bfloat16)] * parts,
        scratch_shapes=[
            pltpu.VMEM((groups // col_tiles,) + blocks[0].shape, jnp.bfloat16),
            pltpu.VMEM((parts, 2, pairs // parts, sources), jnp.float32),
        ],
        compiler_params=pltpu.CompilerParams(vmem_limit_bytes=VMEM_LIMIT),
        cost_estimate=tile_cost(freqs * row_tiles * col_tiles, size, tile, pairs // freqs),
        name="predict",
    )(limits, green_right, green_left, own, *blocks[::-1])


def residual_kernel(data_ref, *refs):
    block_refs, (misfit_ref, *part_refs) = refs[:-3], refs[-3:]
    residual = sum(block_ref[...].astype(jnp.float32) for block_ref in block_refs) - data_ref[...]
    for c, part_ref in enumerate(part_refs):
        part_ref[...] = residual[c]
    misfit_ref[...] = residual.astype(misfit_ref.dtype)


def residual_of(blocks, data):
    shape = blocks[0].shape
    return pl.pallas_call(
        residual_kernel,
        in_specs=[pl.BlockSpec(memory_space=pltpu.VMEM)] * (1 + len(blocks)),
        out_specs=[pl.BlockSpec(memory_space=pltpu.VMEM)] * 3,
        out_shape=[
            jax.ShapeDtypeStruct(shape, jnp.bfloat16),
            jax.ShapeDtypeStruct(shape[1:], jnp.float32),
            jax.ShapeDtypeStruct(shape[1:], jnp.float32),
        ],
        compiler_params=pltpu.CompilerParams(vmem_limit_bytes=VMEM_LIMIT),
        name="residual",
    )(data, *blocks)


def back_kernel(parts, groups, reps, limits_ref, right_ref, left_ref, *refs):
    misfit_refs, out_refs = refs[:parts], refs[parts : parts + reps]
    misfit_all_ref, grad_ref = refs[parts + reps :]
    _, freqs, row_tiles, col_tiles, size, tile = left_ref.shape
    _, pairs, _ = misfit_refs[0].shape
    rhs = parts * pairs // freqs
    _, _, _, low, lanes = out_refs[0].shape
    high = lanes // rhs
    per_tile = groups * reps // col_tiles
    me = lax.axis_index("rtile")
    for at, misfit_ref in enumerate(misfit_refs):
        misfit_all_ref[origin(me, at, parts)] = misfit_ref[...].astype(jnp.float32)
    products = {}
    for f in range(freqs):
        for i in range(row_tiles):
            rows = [
                jnp.concatenate(
                    [
                        misfit_all_ref[part, c, start : start + length, i * tile : (i + 1) * tile]
                        for part, start, length in spans(f * rhs, rhs, pairs)
                    ]
                )
                for c in range(2)
            ]
            first = jnp.concatenate(rows).astype(jnp.bfloat16)
            second = jnp.concatenate([rows[1], -rows[0]]).astype(jnp.bfloat16)
            left = [left_ref[c, f, i].reshape(col_tiles * size, tile) for c in range(2)]
            products[f, i] = dot(left[0], first, 1, 1) + dot(left[1], second, 1, 1)
    factors = {}
    for f in range(freqs):
        back = [
            masked(products[f, i], limits_ref, [(f, i, j) for j in range(col_tiles)], size)
            for i in range(row_tiles)
        ]
        for j in range(col_tiles):
            straight = [part[j] for part in back]
            factors[f, j] = jnp.concatenate(straight + [turned(part) for part in straight])
    for f in range(freqs):
        for j in range(col_tiles):
            right = jnp.concatenate(
                [right_ref[c, f, :, j].reshape(row_tiles * size, tile) for c in range(2)]
            )
            grad = dot(factors[f, j], right, 0, 0)
            grad = (grad if low % 16 else grad.astype(out_refs[0].dtype)).T
            for at in range(per_tile):
                rows = at * high * low
                for c in range(2):
                    blocks = [
                        grad[rows + h * low : rows + (h + 1) * low, c * rhs : (c + 1) * rhs]
                        for h in range(high)
                    ]
                    grad_ref[j * per_tile + at, f, c] = jnp.concatenate(blocks, axis=1).astype(
                        grad_ref.dtype
                    )
    me, own = lax.axis_index("freq"), lax.axis_index("rep")
    for at, out_ref in enumerate(out_refs):
        rep = target(own, at, reps)
        if shared_steps(groups, reps):
            places = [((1 + rep), 0), ((1 + rep), 1), (3, rep), (0, rep)]
        else:
            places = [(step, rep) for step in range(groups)]
        for slot, (step, core) in enumerate(places):
            out_ref[slot] = grad_ref[target(me, step, groups) * reps + core]


def back_project(limits, misfit, green_right, green_left, groups, reps):
    parts = len(misfit)
    _, pairs, sources = misfit[0].shape
    freqs, row_tiles, col_tiles, size, tile = green_left.shape[1:]
    rhs = parts * pairs // freqs
    low = col_tiles * tile * rhs // (groups * reps * LANES)
    block = (freqs, 2, low, LANES)
    return pl.pallas_call(
        functools.partial(back_kernel, parts, groups, reps),
        in_specs=[pl.BlockSpec(memory_space=pltpu.VMEM)] * (3 + parts),
        out_specs=[pl.BlockSpec(memory_space=pltpu.VMEM)] * reps,
        out_shape=[jax.ShapeDtypeStruct((groups,) + block, jnp.bfloat16)] * reps,
        scratch_shapes=[
            pltpu.VMEM((parts, 2, pairs, sources), jnp.float32),
            pltpu.VMEM((groups * reps,) + block, jnp.bfloat16),
        ],
        compiler_params=pltpu.CompilerParams(vmem_limit_bytes=VMEM_LIMIT),
        cost_estimate=tile_cost(freqs * row_tiles * col_tiles, size, tile, rhs),
        name="back_project",
    )(limits, green_right, green_left, *misfit)


def gather_kernel(reps, *refs):
    part_refs, out_refs = refs[:reps], refs[reps:]
    slot = 0
    for out_ref in out_refs:
        for at in range(out_ref.shape[0]):
            total = sum(part_ref[slot].astype(jnp.float32) for part_ref in part_refs)
            out_ref[at] = total.astype(out_ref.dtype)
            slot += 1


def gather(parts, counts):
    shape = parts[0].shape[1:]
    return pl.pallas_call(
        functools.partial(gather_kernel, len(parts)),
        in_specs=[pl.BlockSpec(memory_space=pltpu.VMEM)] * len(parts),
        out_specs=[pl.BlockSpec(memory_space=pltpu.VMEM)] * len(counts),
        out_shape=[jax.ShapeDtypeStruct((count,) + shape, jnp.bfloat16) for count in counts],
        compiler_params=pltpu.CompilerParams(vmem_limit_bytes=VMEM_LIMIT),
        name="gather",
    )(*parts)


def other_kernel(pair_ref, out_ref):
    out_ref[0] = pair_ref[1 - lax.axis_index("rep")]


def other(pair):
    return pl.pallas_call(
        other_kernel,
        in_specs=[pl.BlockSpec(memory_space=pltpu.VMEM)],
        out_specs=pl.BlockSpec(memory_space=pltpu.VMEM),
        out_shape=jax.ShapeDtypeStruct((1,) + pair.shape[1:], pair.dtype),
        compiler_params=pltpu.CompilerParams(vmem_limit_bytes=VMEM_LIMIT),
        name="other",
    )(pair)


def return_spectra(parts):
    groups, reps = parts[0].shape[0], len(parts)
    parts = exchange(parts, "rep")
    if not shared_steps(groups, reps):
        return exchange(gather(parts, [1] * groups), "freq")
    pair, last, own = gather(parts, [2, 1, 1])
    devices = [(chip, core) for chip in range(groups) for core in range(reps)]
    near = [(chip * reps + core, (chip ^ (1 + core)) * reps + core) for chip, core in devices]
    far = [(chip * reps + core, (chip ^ 3) * reps + core) for chip, core in devices]
    pair = lax.ppermute(pair, ("freq", "rep"), near)
    last = lax.ppermute(last, ("freq", "rep"), far)
    swapped = lax.ppermute(other(pair), "rep", [(0, 1), (1, 0)])
    return [own, pair, swapped, last]


def gradient_kernel(reps, table_ref, *refs):
    part_refs, (out_hbm, out_ref, rows_ref, out_sems) = refs[-5::-1], refs[-4:]
    groups = len(part_refs)
    _, freqs, _, low, lanes = part_refs[0].shape
    high, _, rhs, length = out_ref.shape
    bins = table_ref.shape[0]
    me = lax.axis_index("freq")
    if shared_steps(groups, reps):
        core = lax.axis_index("rep")
        places = [(0, 0), (1 + core, core), (2 - core, 0), (3, 0)]
    else:
        places = [(step, 0) for step in range(groups)]
    for part_ref, (step, place) in zip(part_refs, places):
        g = origin(me, step, groups)
        for f in range(freqs):
            for c in range(2):
                rows = pl.ds(c * groups * freqs + g * freqs + f, low, stride=bins)
                rows_ref[rows, :] = part_ref[place, f, c].astype(jnp.float32)
    table = table_ref[...]
    width = math.gcd(length, 256)
    copies = []
    for at, (start, part) in enumerate(ramp(low)):
        coefficients = jnp.concatenate(
            [rows_ref[row * bins : (row + 1) * bins] for row in range(start, start + part)],
            axis=1,
        ).astype(jnp.bfloat16)
        for column in range(0, length, width):
            columns = slice(column, column + width)
            traces = dot(coefficients, table[:, columns], 0, 0).astype(out_ref.dtype)
            for row in range(part):
                out_ref[:, start + row, :, columns] = traces[
                    row * lanes : (row + 1) * lanes
                ].reshape(high, rhs, width)
        rows = pl.ds(start, part)
        copies.append(
            pltpu.make_async_copy(out_ref.at[:, rows], out_hbm.at[:, rows], out_sems.at[at])
        )
        copies[-1].start()
    for copy in copies:
        copy.wait()


def gradient_of(parts, table, rhs, reps):
    _, _, _, low, lanes = parts[0].shape
    bins, length = table.shape
    high = lanes // rhs
    chunks = len(ramp(low))
    shape = (high, low, rhs, length)
    out = pl.pallas_call(
        functools.partial(gradient_kernel, reps),
        in_specs=[pl.BlockSpec(memory_space=pltpu.VMEM)] * (1 + len(parts)),
        out_specs=pl.BlockSpec(memory_space=pltpu.HBM),
        out_shape=jax.ShapeDtypeStruct(shape, jnp.bfloat16),
        scratch_shapes=[
            pltpu.VMEM(shape, jnp.bfloat16),
            pltpu.VMEM((low * bins, lanes), jnp.float32),
            pltpu.SemaphoreType.DMA((chunks,)),
        ],
        compiler_params=pltpu.CompilerParams(vmem_limit_bytes=VMEM_LIMIT),
        name="gradient",
    )(table, *parts[::-1])
    return out.reshape(1, high * low, rhs, length)


def shards(model, green_left, green_right, ranks, data):
    freq_count = lax.axis_size("freq")
    tile_count = lax.axis_size("rtile")
    rep_count = lax.axis_size("rep")
    freq_local = ranks.shape[0]
    rhs_count = model.shape[2]
    table, spectrum = spectrum_of(model[0], freq_count, freq_local)
    spectrum = exchange(spectrum, "freq")
    limits = limits_of(ranks, table)
    per_tile = freq_count // green_right.shape[3]
    own = project(limits, spectrum[:per_tile], green_right)
    predicted = predict(limits, own, spectrum[per_tile:], green_right, green_left, tile_count)
    misfit, *residual = residual_of(exchange(predicted, "rtile")[::-1], data)
    misfit = exchange([misfit] * tile_count, "rtile")
    partial = back_project(limits, misfit, green_right, green_left, freq_count, rep_count)
    arrived = return_spectra(partial)
    return (jnp.stack(residual), gradient_of(arrived, table, rhs_count, rep_count))


def solution(mesh):
    return jax.shard_map(
        shards,
        mesh=mesh,
        in_specs=(
            P("rtile", "freq", None, None),
            P(None, "freq", "rep", "rtile", None, None),
            P(None, "freq", "rep", "rtile", None, None),
            P("freq", "rep", "rtile"),
            P(None, ("freq", "rtile"), "rep"),
        ),
        out_specs=(P(None, ("freq", "rtile"), "rep"), P("rtile", ("freq", "rep"), None, None)),
        check_vma=False,
    )
```

```python
import functools
import math

import jax
import jax.numpy as jnp
from jax import lax
from jax.experimental import pallas as pl
from jax.experimental.pallas import tpu as pltpu
from jax.sharding import PartitionSpec as P

LANES = 128
VMEM_LIMIT = 48 * 1024 * 1024


def tables(bins, length):
    row = lax.broadcasted_iota(jnp.int32, (bins, length), 0)
    sample = lax.broadcasted_iota(jnp.int32, (bins, length), 1)
    is_sine = row >= bins // 2
    freq_bin = jnp.where(is_sine, row - bins // 2, row) + 1
    phase = freq_bin * sample + jnp.where(is_sine, length // 4, 0)
    if length & (length - 1) == 0:
        phase = phase & (length - 1)
        quarter = (phase + length // 8) >> (length.bit_length() - 3)
    else:
        phase = lax.rem(phase, length)
        quarter = lax.div(phase + length // 8, length // 4)
    angle = (phase - quarter * (length // 4)).astype(jnp.float32) * (2.0 * math.pi / length)
    square = angle * angle
    even = 1.0
    odd = 1.0
    for order in (8, 6, 4, 2):
        even = 1.0 - square * even * (1.0 / (order * (order - 1)))
        odd = 1.0 - square * odd * (1.0 / (order * (order + 1)))
    odd = odd * angle
    quarter = quarter & 3
    value = jnp.where((quarter & 1) == 0, even, odd)
    return jnp.where((quarter == 1) | (quarter == 2), -value, value).astype(jnp.bfloat16)


def dot(first, second, first_dim, second_dim):
    return lax.dot_general(
        first,
        second,
        (((first_dim,), (second_dim,)), ((), ())),
        preferred_element_type=jnp.float32,
    )


def turned(pair):
    half = pair.shape[1] // 2
    return jnp.concatenate([-pair[:, half:], pair[:, :half]], axis=1)


def target(me, step, count):
    return me ^ step if count & (count - 1) == 0 else lax.rem(me + step, count)


def origin(me, step, count):
    return me ^ step if count & (count - 1) == 0 else lax.rem(me + count - step, count)


def exchange(blocks, axis):
    count = len(blocks)
    arrived = []
    for step in range(count - 1, 0, -1):
        pairs = [(me, me ^ step if count & (count - 1) == 0 else (me + step) % count) for me in range(count)]
        arrived.append(lax.ppermute(blocks[step], axis, pairs))
    return [blocks[0]] + arrived[::-1]


def ramp(count):
    step = max(count // 4, 1)
    cuts = [0] + list(range(step // 2 or step, count, step)) + [count]
    return [(start, end - start) for start, end in zip(cuts, cuts[1:])]


def shared_steps(groups, reps):
    return groups == 4 and reps == 2


def spectrum_kernel(model_hbm, table_out_ref, *refs):
    out_refs = refs[:-3]
    model_ref, rows_ref, model_sems = refs[-3:]
    high, low, rhs, length = model_ref.shape
    dests = len(out_refs)
    freqs, _, _, lanes = out_refs[0].shape
    bins = 2 * dests * freqs
    chunks = ramp(low)
    copies = []
    for at, (start, length_of) in enumerate(chunks):
        rows = pl.ds(start, length_of)
        copies.append(
            pltpu.make_async_copy(
                model_hbm.at[:, rows], model_ref.at[:, rows], model_sems.at[at]
            )
        )
        copies[-1].start()
    table = tables(bins, length)
    table_out_ref[...] = table
    for copy, (begin, length_of) in zip(copies, chunks):
        copy.wait()
        for start in range(begin, begin + length_of, 2):
            width = min(2, begin + length_of - start)
            block = jnp.concatenate(
                [model_ref[:, start + row].reshape(lanes, length) for row in range(width)]
            )
            sums = dot(table, block, 1, 1)
            for row in range(width):
                place = (start + row) * bins
                rows_ref[place : place + bins] = sums[:, row * lanes : (row + 1) * lanes]
    me = lax.axis_index("freq")
    for at, out_ref in enumerate(out_refs):
        dest = target(me, at, dests)
        for f in range(freqs):
            for c in range(2):
                q = c * dests * freqs + dest * freqs + f
                out_ref[f, c] = rows_ref[pl.ds(q, low, stride=bins), :].astype(out_ref.dtype)


def spectrum_of(model, dests, freqs):
    traces, rhs, length = model.shape
    high = LANES // rhs
    low = traces // high
    chunks = len(ramp(low))
    bins = 2 * dests * freqs
    table, *blocks = pl.pallas_call(
        spectrum_kernel,
        in_specs=[pl.BlockSpec(memory_space=pltpu.HBM)],
        out_specs=[pl.BlockSpec(memory_space=pltpu.VMEM)] * (1 + dests),
        out_shape=[jax.ShapeDtypeStruct((bins, length), jnp.bfloat16)]
        + [jax.ShapeDtypeStruct((freqs, 2, low, LANES), jnp.bfloat16)] * dests,
        scratch_shapes=[
            pltpu.VMEM((high, low, rhs, length), model.dtype),
            pltpu.VMEM((low * bins, LANES), jnp.float32),
            pltpu.SemaphoreType.DMA((chunks,)),
        ],
        compiler_params=pltpu.CompilerParams(vmem_limit_bytes=VMEM_LIMIT),
        name="spectrum",
    )(model.reshape(high, low, rhs, length))
    return table, blocks


def tile_cost(count, size, tile, rhs):
    return pl.CostEstimate(
        flops=count * 2 * 8 * size * tile * rhs,
        bytes_accessed=count * 2 * 4 * size * tile,
        transcendentals=0,
    )


def limits_kernel(ranks_ref, table_ref, out_ref):
    freqs, row_tiles, col_tiles = ranks_ref.shape
    for f in range(freqs):
        for i in range(row_tiles):
            for j in range(col_tiles):
                rank = ranks_ref[f, i : i + 1, j : j + 1]
                out_ref[f, i, j] = jnp.broadcast_to(rank, (1, LANES))


def limits_of(ranks, table):
    return pl.pallas_call(
        limits_kernel,
        in_specs=[pl.BlockSpec(memory_space=pltpu.VMEM)] * 2,
        out_specs=pl.BlockSpec(memory_space=pltpu.VMEM),
        out_shape=jax.ShapeDtypeStruct(ranks.shape + (1, LANES), jnp.int32),
        compiler_params=pltpu.CompilerParams(vmem_limit_bytes=VMEM_LIMIT),
        name="limits",
    )(ranks, table)


def masked(product, limits_ref, places, size):
    columns = product.shape[1]
    row = lax.broadcasted_iota(jnp.int32, (size, columns), 0)
    kept = [
        jnp.where(row < limits_ref[place][:, :columns], product[at * size : (at + 1) * size], 0.0)
        for at, place in enumerate(places)
    ]
    return [part.astype(jnp.bfloat16) for part in kept]


def spans(first, count, size):
    found = []
    at = first
    while at < first + count:
        length = min(size - at % size, first + count - at)
        found.append((at // size, at % size, length))
        at += length
    return found


def project_tile(j, block_refs, tile_ref, limits_ref, right_ref):
    freqs, _, low, lanes = block_refs[0].shape
    _, _, row_tiles, _, size, tile = right_ref.shape
    high = tile // (len(block_refs) * low)
    rhs = lanes // high
    me = lax.axis_index("freq")
    for at, block_ref in enumerate(block_refs):
        tile_ref[(me ^ at) & (len(block_refs) - 1)] = block_ref[...]
    products = []
    for f in range(freqs):
        halves = []
        for c in range(2):
            blocks = []
            for g in range(len(block_refs)):
                got = tile_ref[g, f, c]
                if low % 16:
                    got = got.astype(jnp.float32)
                blocks += [got[:, h * rhs : (h + 1) * rhs] for h in range(high)]
            halves.append(jnp.concatenate(blocks))
        first = jnp.concatenate(halves, axis=1).astype(jnp.bfloat16)
        second = jnp.concatenate([halves[1], -halves[0]], axis=1).astype(jnp.bfloat16)
        right = [right_ref[c, f, :, j].reshape(row_tiles * size, tile) for c in range(2)]
        products.append(dot(right[0], first, 1, 0) + dot(right[1], second, 1, 0))
    return [
        masked(product, limits_ref, [(f, i, j) for i in range(row_tiles)], size)
        for f, product in enumerate(products)
    ]


def project_kernel(count, limits_ref, right_ref, *refs):
    block_refs, (out_ref, tile_ref) = refs[:count], refs[count:]
    j = lax.div(lax.axis_index("freq"), count)
    for f, parts in enumerate(project_tile(j, block_refs, tile_ref, limits_ref, right_ref)):
        for i, part in enumerate(parts):
            out_ref[f, i] = part


def project(limits, blocks, green_right):
    _, freqs, row_tiles, _, size, tile = green_right.shape
    _, _, low, _ = blocks[0].shape
    columns = 2 * LANES * len(blocks) * low // tile
    return pl.pallas_call(
        functools.partial(project_kernel, len(blocks)),
        in_specs=[pl.BlockSpec(memory_space=pltpu.VMEM)] * (2 + len(blocks)),
        out_specs=pl.BlockSpec(memory_space=pltpu.VMEM),
        out_shape=jax.ShapeDtypeStruct((freqs, row_tiles, size, columns), jnp.bfloat16),
        scratch_shapes=[pltpu.VMEM((len(blocks),) + blocks[0].shape, jnp.bfloat16)],
        compiler_params=pltpu.CompilerParams(vmem_limit_bytes=VMEM_LIMIT),
        cost_estimate=tile_cost(freqs * row_tiles, size, tile, columns // 4),
        name="project",
    )(limits, green_right, *blocks)


def predict_kernel(groups, parts, limits_ref, right_ref, left_ref, own_ref, *refs):
    _, freqs, row_tiles, col_tiles, size, tile = left_ref.shape
    per_tile = groups // col_tiles
    others = groups - per_tile
    block_refs, out_refs, (tile_ref, sum_ref) = (
        refs[:others][::-1],
        refs[others : others + parts],
        refs[others + parts :],
    )
    _, pairs, _ = out_refs[0].shape
    rhs = parts * pairs // freqs
    own = lax.div(lax.axis_index("freq"), per_tile)
    tiles = [own]
    projected = [[[own_ref[f, i] for i in range(row_tiles)] for f in range(freqs)]]
    for step in range(1, col_tiles):
        blocks = block_refs[(step - 1) * per_tile : step * per_tile]
        tiles.append(own ^ step)
        projected.append(project_tile(own ^ step, blocks, tile_ref, limits_ref, right_ref))
    factors = {}
    for f in range(freqs):
        for i in range(row_tiles):
            straight = [part[f][i] for part in projected]
            factors[f, i] = jnp.concatenate(straight + [turned(part) for part in straight])
    for f in range(freqs):
        for i in range(row_tiles):
            left = jnp.concatenate([left_ref[c, f, i, j] for c in range(2) for j in tiles])
            predicted = dot(factors[f, i], left, 0, 0)
            for c in range(2):
                row = c * rhs
                for part, start, length in spans(f * rhs, rhs, pairs):
                    sum_ref[part, c, start : start + length, i * tile : (i + 1) * tile] = predicted[
                        row : row + length
                    ]
                    row += length
    me = lax.axis_index("rtile")
    for at, out_ref in enumerate(out_refs):
        out_ref[...] = sum_ref[target(me, at, parts)].astype(out_ref.dtype)


def predict(limits, own, blocks, green_right, green_left, parts):
    freqs, row_tiles, col_tiles, size, tile = green_left.shape[1:]
    groups = len(blocks) * col_tiles // (col_tiles - 1)
    pairs = freqs * own.shape[3] // 2
    sources = row_tiles * tile
    return pl.pallas_call(
        functools.partial(predict_kernel, groups, parts),
        in_specs=[pl.BlockSpec(memory_space=pltpu.VMEM)] * (4 + len(blocks)),
        out_specs=[pl.BlockSpec(memory_space=pltpu.VMEM)] * parts,
        out_shape=[jax.ShapeDtypeStruct((2, pairs // parts, sources), jnp.bfloat16)] * parts,
        scratch_shapes=[
            pltpu.VMEM((groups // col_tiles,) + blocks[0].shape, jnp.bfloat16),
            pltpu.VMEM((parts, 2, pairs // parts, sources), jnp.float32),
        ],
        compiler_params=pltpu.CompilerParams(vmem_limit_bytes=VMEM_LIMIT),
        cost_estimate=tile_cost(freqs * row_tiles * col_tiles, size, tile, pairs // freqs),
        name="predict",
    )(limits, green_right, green_left, own, *blocks[::-1])


def residual_kernel(data_ref, *refs):
    block_refs, (misfit_ref, *part_refs) = refs[:-3], refs[-3:]
    residual = sum(block_ref[...].astype(jnp.float32) for block_ref in block_refs) - data_ref[...]
    for c, part_ref in enumerate(part_refs):
        part_ref[...] = residual[c]
    misfit_ref[...] = residual.astype(misfit_ref.dtype)


def residual_of(blocks, data):
    shape = blocks[0].shape
    return pl.pallas_call(
        residual_kernel,
        in_specs=[pl.BlockSpec(memory_space=pltpu.VMEM)] * (1 + len(blocks)),
        out_specs=[pl.BlockSpec(memory_space=pltpu.VMEM)] * 3,
        out_shape=[
            jax.ShapeDtypeStruct(shape, jnp.bfloat16),
            jax.ShapeDtypeStruct(shape[1:], jnp.float32),
            jax.ShapeDtypeStruct(shape[1:], jnp.float32),
        ],
        compiler_params=pltpu.CompilerParams(vmem_limit_bytes=VMEM_LIMIT),
        name="residual",
    )(data, *blocks)


def back_kernel(parts, groups, reps, limits_ref, right_ref, left_ref, *refs):
    misfit_refs, out_refs = refs[:parts], refs[parts : parts + reps]
    misfit_all_ref, grad_ref = refs[parts + reps :]
    _, freqs, row_tiles, col_tiles, size, tile = left_ref.shape
    _, pairs, _ = misfit_refs[0].shape
    rhs = parts * pairs // freqs
    _, _, _, low, lanes = out_refs[0].shape
    high = lanes // rhs
    per_tile = groups * reps // col_tiles
    me = lax.axis_index("rtile")
    for at, misfit_ref in enumerate(misfit_refs):
        misfit_all_ref[origin(me, at, parts)] = misfit_ref[...].astype(jnp.float32)
    products = {}
    for f in range(freqs):
        for i in range(row_tiles):
            rows = [
                jnp.concatenate(
                    [
                        misfit_all_ref[part, c, start : start + length, i * tile : (i + 1) * tile]
                        for part, start, length in spans(f * rhs, rhs, pairs)
                    ]
                )
                for c in range(2)
            ]
            first = jnp.concatenate(rows).astype(jnp.bfloat16)
            second = jnp.concatenate([rows[1], -rows[0]]).astype(jnp.bfloat16)
            left = [left_ref[c, f, i].reshape(col_tiles * size, tile) for c in range(2)]
            products[f, i] = dot(left[0], first, 1, 1) + dot(left[1], second, 1, 1)
    factors = {}
    for f in range(freqs):
        back = [
            masked(products[f, i], limits_ref, [(f, i, j) for j in range(col_tiles)], size)
            for i in range(row_tiles)
        ]
        for j in range(col_tiles):
            straight = [part[j] for part in back]
            factors[f, j] = jnp.concatenate(straight + [turned(part) for part in straight])
    for f in range(freqs):
        for j in range(col_tiles):
            right = jnp.concatenate(
                [right_ref[c, f, :, j].reshape(row_tiles * size, tile) for c in range(2)]
            )
            grad = dot(factors[f, j], right, 0, 0)
            grad = (grad if low % 16 else grad.astype(out_refs[0].dtype)).T
            for at in range(per_tile):
                rows = at * high * low
                for c in range(2):
                    blocks = [
                        grad[rows + h * low : rows + (h + 1) * low, c * rhs : (c + 1) * rhs]
                        for h in range(high)
                    ]
                    grad_ref[j * per_tile + at, f, c] = jnp.concatenate(blocks, axis=1).astype(
                        grad_ref.dtype
                    )
    me, own = lax.axis_index("freq"), lax.axis_index("rep")
    for at, out_ref in enumerate(out_refs):
        rep = target(own, at, reps)
        if shared_steps(groups, reps):
            places = [((1 + rep), 0), ((1 + rep), 1), (3, rep), (0, rep)]
        else:
            places = [(step, rep) for step in range(groups)]
        for slot, (step, core) in enumerate(places):
            out_ref[slot] = grad_ref[target(me, step, groups) * reps + core]


def back_project(limits, misfit, green_right, green_left, groups, reps):
    parts = len(misfit)
    _, pairs, sources = misfit[0].shape
    freqs, row_tiles, col_tiles, size, tile = green_left.shape[1:]
    rhs = parts * pairs // freqs
    low = col_tiles * tile * rhs // (groups * reps * LANES)
    block = (freqs, 2, low, LANES)
    return pl.pallas_call(
        functools.partial(back_kernel, parts, groups, reps),
        in_specs=[pl.BlockSpec(memory_space=pltpu.VMEM)] * (3 + parts),
        out_specs=[pl.BlockSpec(memory_space=pltpu.VMEM)] * reps,
        out_shape=[jax.ShapeDtypeStruct((groups,) + block, jnp.bfloat16)] * reps,
        scratch_shapes=[
            pltpu.VMEM((parts, 2, pairs, sources), jnp.float32),
            pltpu.VMEM((groups * reps,) + block, jnp.bfloat16),
        ],
        compiler_params=pltpu.CompilerParams(vmem_limit_bytes=VMEM_LIMIT),
        cost_estimate=tile_cost(freqs * row_tiles * col_tiles, size, tile, rhs),
        name="back_project",
    )(limits, green_right, green_left, *misfit)


def gather_kernel(reps, *refs):
    part_refs, out_refs = refs[:reps], refs[reps:]
    slot = 0
    for out_ref in out_refs:
        for at in range(out_ref.shape[0]):
            total = sum(part_ref[slot].astype(jnp.float32) for part_ref in part_refs)
            out_ref[at] = total.astype(out_ref.dtype)
            slot += 1


def gather(parts, counts):
    shape = parts[0].shape[1:]
    return pl.pallas_call(
        functools.partial(gather_kernel, len(parts)),
        in_specs=[pl.BlockSpec(memory_space=pltpu.VMEM)] * len(parts),
        out_specs=[pl.BlockSpec(memory_space=pltpu.VMEM)] * len(counts),
        out_shape=[jax.ShapeDtypeStruct((count,) + shape, jnp.bfloat16) for count in counts],
        compiler_params=pltpu.CompilerParams(vmem_limit_bytes=VMEM_LIMIT),
        name="gather",
    )(*parts)


def other_kernel(pair_ref, out_ref):
    out_ref[0] = pair_ref[1 - lax.axis_index("rep")]


def other(pair):
    return pl.pallas_call(
        other_kernel,
        in_specs=[pl.BlockSpec(memory_space=pltpu.VMEM)],
        out_specs=pl.BlockSpec(memory_space=pltpu.VMEM),
        out_shape=jax.ShapeDtypeStruct((1,) + pair.shape[1:], pair.dtype),
        compiler_params=pltpu.CompilerParams(vmem_limit_bytes=VMEM_LIMIT),
        name="other",
    )(pair)


def return_spectra(parts):
    groups, reps = parts[0].shape[0], len(parts)
    parts = exchange(parts, "rep")
    if not shared_steps(groups, reps):
        return exchange(gather(parts, [1] * groups), "freq")
    pair, last, own = gather(parts, [2, 1, 1])
    devices = [(chip, core) for chip in range(groups) for core in range(reps)]
    near = [(chip * reps + core, (chip ^ (1 + core)) * reps + core) for chip, core in devices]
    far = [(chip * reps + core, (chip ^ 3) * reps + core) for chip, core in devices]
    pair = lax.ppermute(pair, ("freq", "rep"), near)
    last = lax.ppermute(last, ("freq", "rep"), far)
    swapped = lax.ppermute(other(pair), "rep", [(0, 1), (1, 0)])
    return [own, pair, swapped, last]


def gradient_kernel(reps, table_ref, *refs):
    part_refs, (out_hbm, out_ref, rows_ref, out_sems) = refs[-5::-1], refs[-4:]
    groups = len(part_refs)
    _, freqs, _, low, lanes = part_refs[0].shape
    high, _, rhs, length = out_ref.shape
    bins = table_ref.shape[0]
    me = lax.axis_index("freq")
    if shared_steps(groups, reps):
        core = lax.axis_index("rep")
        places = [(0, 0), (1 + core, core), (2 - core, 0), (3, 0)]
    else:
        places = [(step, 0) for step in range(groups)]
    for part_ref, (step, place) in zip(part_refs, places):
        g = origin(me, step, groups)
        for f in range(freqs):
            for c in range(2):
                rows = pl.ds(c * groups * freqs + g * freqs + f, low, stride=bins)
                rows_ref[rows, :] = part_ref[place, f, c].astype(jnp.float32)
    table = table_ref[...]
    width = math.gcd(length, 256)
    copies = []
    for at, (start, part) in enumerate(ramp(low)):
        coefficients = jnp.concatenate(
            [rows_ref[row * bins : (row + 1) * bins] for row in range(start, start + part)],
            axis=1,
        ).astype(jnp.bfloat16)
        for column in range(0, length, width):
            columns = slice(column, column + width)
            traces = dot(coefficients, table[:, columns], 0, 0).astype(out_ref.dtype)
            for row in range(part):
                out_ref[:, start + row, :, columns] = traces[
                    row * lanes : (row + 1) * lanes
                ].reshape(high, rhs, width)
        rows = pl.ds(start, part)
        copies.append(
            pltpu.make_async_copy(out_ref.at[:, rows], out_hbm.at[:, rows], out_sems.at[at])
        )
        copies[-1].start()
    for copy in copies:
        copy.wait()


def gradient_of(parts, table, rhs, reps):
    _, _, _, low, lanes = parts[0].shape
    bins, length = table.shape
    high = lanes // rhs
    chunks = len(ramp(low))
    shape = (high, low, rhs, length)
    out = pl.pallas_call(
        functools.partial(gradient_kernel, reps),
        in_specs=[pl.BlockSpec(memory_space=pltpu.VMEM)] * (1 + len(parts)),
        out_specs=pl.BlockSpec(memory_space=pltpu.HBM),
        out_shape=jax.ShapeDtypeStruct(shape, jnp.bfloat16),
        scratch_shapes=[
            pltpu.VMEM(shape, jnp.bfloat16),
            pltpu.VMEM((low * bins, lanes), jnp.float32),
            pltpu.SemaphoreType.DMA((chunks,)),
        ],
        compiler_params=pltpu.CompilerParams(vmem_limit_bytes=VMEM_LIMIT),
        name="gradient",
    )(table, *parts[::-1])
    return out.reshape(1, high * low, rhs, length)


def shards(model, green_left, green_right, ranks, data):
    freq_count = lax.axis_size("freq")
    tile_count = lax.axis_size("rtile")
    rep_count = lax.axis_size("rep")
    freq_local = ranks.shape[0]
    rhs_count = model.shape[2]
    table, spectrum = spectrum_of(model[0], freq_count, freq_local)
    spectrum = exchange(spectrum, "freq")
    limits = limits_of(ranks, table)
    per_tile = freq_count // green_right.shape[3]
    own = project(limits, spectrum[:per_tile], green_right)
    predicted = predict(limits, own, spectrum[per_tile:], green_right, green_left, tile_count)
    misfit, *residual = residual_of(exchange(predicted, "rtile")[::-1], data)
    misfit = exchange([misfit] * tile_count, "rtile")
    partial = back_project(limits, misfit, green_right, green_left, freq_count, rep_count)
    arrived = return_spectra(partial)
    return (jnp.stack(residual), gradient_of(arrived, table, rhs_count, rep_count))


def solution(mesh):
    return jax.shard_map(
        shards,
        mesh=mesh,
        in_specs=(
            P("rtile", "freq", None, None),
            P(None, "freq", "rep", "rtile", None, None),
            P(None, "freq", "rep", "rtile", None, None),
            P("freq", "rep", "rtile"),
            P(None, ("freq", "rtile"), "rep"),
        ),
        out_specs=(P(None, ("freq", "rtile"), "rep"), P("rtile", ("freq", "rep"), None, None)),
        check_vma=False,
    )
```

```python
import functools
import math

import jax
import jax.numpy as jnp
from jax import lax
from jax.experimental import pallas as pl
from jax.experimental.pallas import tpu as pltpu
from jax.sharding import PartitionSpec as P

LANES = 128
VMEM_LIMIT = 48 * 1024 * 1024


def tables(bins, length):
    row = lax.broadcasted_iota(jnp.int32, (bins, length), 0)
    sample = lax.broadcasted_iota(jnp.int32, (bins, length), 1)
    is_sine = row >= bins // 2
    freq_bin = jnp.where(is_sine, row - bins // 2, row) + 1
    phase = lax.rem(freq_bin * sample, length) + jnp.where(is_sine, length // 4, 0)
    quarter = lax.div(phase + length // 8, length // 4)
    angle = (phase - quarter * (length // 4)).astype(jnp.float32) * (2.0 * math.pi / length)
    square = angle * angle
    even = 1.0
    odd = 1.0
    for order in (8, 6, 4, 2):
        even = 1.0 - square * even * (1.0 / (order * (order - 1)))
        odd = 1.0 - square * odd * (1.0 / (order * (order + 1)))
    odd = odd * angle
    quarter = quarter & 3
    value = jnp.where((quarter & 1) == 0, even, odd)
    return jnp.where((quarter == 1) | (quarter == 2), -value, value).astype(jnp.bfloat16)


def dot(first, second, first_dim, second_dim):
    return lax.dot_general(
        first,
        second,
        (((first_dim,), (second_dim,)), ((), ())),
        preferred_element_type=jnp.float32,
    )


def turned(pair):
    half = pair.shape[1] // 2
    return jnp.concatenate([-pair[:, half:], pair[:, :half]], axis=1)


def target(me, step, count):
    return me ^ step if count & (count - 1) == 0 else lax.rem(me + step, count)


def origin(me, step, count):
    return me ^ step if count & (count - 1) == 0 else lax.rem(me + count - step, count)


def exchange(blocks, axis):
    count = len(blocks)
    arrived = []
    for step in range(count - 1, 0, -1):
        pairs = [(me, me ^ step if count & (count - 1) == 0 else (me + step) % count) for me in range(count)]
        arrived.append(lax.ppermute(blocks[step], axis, pairs))
    return [blocks[0]] + arrived[::-1]


def ramp(count):
    step = max(count // 4, 1)
    cuts = [0] + list(range(step // 2 or step, count, step)) + [count]
    return [(start, end - start) for start, end in zip(cuts, cuts[1:])]


def shared_steps(groups, reps):
    return groups == 4 and reps == 2


def middle_first(blocks):
    return [blocks[step] for step in (2, 3, 1, 0)] if len(blocks) == 4 else blocks[::-1]


def spectrum_kernel(model_hbm, table_out_ref, *refs):
    out_refs = refs[:-3]
    model_ref, rows_ref, model_sems = refs[-3:]
    high, low, rhs, length = model_ref.shape
    dests = len(out_refs)
    freqs, _, _, lanes = out_refs[0].shape
    bins = 2 * dests * freqs
    chunks = ramp(low)
    copies = []
    for at, (start, length_of) in enumerate(chunks):
        rows = pl.ds(start, length_of)
        copies.append(
            pltpu.make_async_copy(
                model_hbm.at[:, rows], model_ref.at[:, rows], model_sems.at[at]
            )
        )
        copies[-1].start()
    table = tables(bins, length)
    table_out_ref[...] = table
    for copy, (begin, length_of) in zip(copies, chunks):
        copy.wait()
        for start in range(begin, begin + length_of, 2):
            width = min(2, begin + length_of - start)
            block = jnp.concatenate(
                [model_ref[:, start + row].reshape(lanes, length) for row in range(width)]
            )
            sums = dot(table, block, 1, 1)
            for row in range(width):
                place = (start + row) * bins
                rows_ref[place : place + bins] = sums[:, row * lanes : (row + 1) * lanes]
    me = lax.axis_index("freq")
    for at, out_ref in enumerate(out_refs):
        dest = target(me, at, dests)
        for f in range(freqs):
            for c in range(2):
                q = c * dests * freqs + dest * freqs + f
                out_ref[f, c] = rows_ref[pl.ds(q, low, stride=bins), :].astype(out_ref.dtype)


def spectrum_of(model, dests, freqs):
    traces, rhs, length = model.shape
    high = LANES // rhs
    low = traces // high
    chunks = len(ramp(low))
    bins = 2 * dests * freqs
    table, *blocks = pl.pallas_call(
        spectrum_kernel,
        in_specs=[pl.BlockSpec(memory_space=pltpu.HBM)],
        out_specs=[pl.BlockSpec(memory_space=pltpu.VMEM)] * (1 + dests),
        out_shape=[jax.ShapeDtypeStruct((bins, length), jnp.bfloat16)]
        + [jax.ShapeDtypeStruct((freqs, 2, low, LANES), jnp.bfloat16)] * dests,
        scratch_shapes=[
            pltpu.VMEM((high, low, rhs, length), model.dtype),
            pltpu.VMEM((low * bins, LANES), jnp.float32),
            pltpu.SemaphoreType.DMA((chunks,)),
        ],
        compiler_params=pltpu.CompilerParams(vmem_limit_bytes=VMEM_LIMIT),
        name="spectrum",
    )(model.reshape(high, low, rhs, length))
    return table, blocks


def tile_cost(count, size, tile, rhs):
    return pl.CostEstimate(
        flops=count * 2 * 8 * size * tile * rhs,
        bytes_accessed=count * 2 * 4 * size * tile,
        transcendentals=0,
    )


def limits_kernel(ranks_ref, table_ref, out_ref):
    freqs, row_tiles, col_tiles = ranks_ref.shape
    for f in range(freqs):
        for i in range(row_tiles):
            for j in range(col_tiles):
                rank = ranks_ref[f, i : i + 1, j : j + 1]
                out_ref[f, i, j] = jnp.broadcast_to(rank, (1, LANES))


def limits_of(ranks, table):
    return pl.pallas_call(
        limits_kernel,
        in_specs=[pl.BlockSpec(memory_space=pltpu.VMEM)] * 2,
        out_specs=pl.BlockSpec(memory_space=pltpu.VMEM),
        out_shape=jax.ShapeDtypeStruct(ranks.shape + (1, LANES), jnp.int32),
        compiler_params=pltpu.CompilerParams(vmem_limit_bytes=VMEM_LIMIT),
        name="limits",
    )(ranks, table)


def masked(product, limits_ref, places, size):
    columns = product.shape[1]
    row = lax.broadcasted_iota(jnp.int32, (size, columns), 0)
    kept = [
        jnp.where(row < limits_ref[place][:, :columns], product[at * size : (at + 1) * size], 0.0)
        for at, place in enumerate(places)
    ]
    return [part.astype(jnp.bfloat16) for part in kept]


def spans(first, count, size):
    found = []
    at = first
    while at < first + count:
        length = min(size - at % size, first + count - at)
        found.append((at // size, at % size, length))
        at += length
    return found


def project_tile(j, block_refs, tile_ref, limits_ref, right_ref):
    freqs, _, low, lanes = block_refs[0].shape
    _, _, row_tiles, _, size, tile = right_ref.shape
    high = tile // (len(block_refs) * low)
    rhs = lanes // high
    me = lax.axis_index("freq")
    for at, block_ref in enumerate(block_refs):
        tile_ref[(me ^ at) & (len(block_refs) - 1)] = block_ref[...]
    products = []
    for f in range(freqs):
        halves = []
        for c in range(2):
            blocks = []
            for g in range(len(block_refs)):
                got = tile_ref[g, f, c]
                if low % 16:
                    got = got.astype(jnp.float32)
                blocks += [got[:, h * rhs : (h + 1) * rhs] for h in range(high)]
            halves.append(jnp.concatenate(blocks))
        first = jnp.concatenate(halves, axis=1).astype(jnp.bfloat16)
        second = jnp.concatenate([halves[1], -halves[0]], axis=1).astype(jnp.bfloat16)
        right = [right_ref[c, f, :, j].reshape(row_tiles * size, tile) for c in range(2)]
        products.append(dot(right[0], first, 1, 0) + dot(right[1], second, 1, 0))
    return [
        masked(product, limits_ref, [(f, i, j) for i in range(row_tiles)], size)
        for f, product in enumerate(products)
    ]


def project_kernel(count, limits_ref, right_ref, *refs):
    block_refs, (out_ref, tile_ref) = refs[:count], refs[count:]
    j = lax.div(lax.axis_index("freq"), count)
    for f, parts in enumerate(project_tile(j, block_refs, tile_ref, limits_ref, right_ref)):
        for i, part in enumerate(parts):
            out_ref[f, i] = part


def project(limits, blocks, green_right):
    _, freqs, row_tiles, _, size, tile = green_right.shape
    _, _, low, _ = blocks[0].shape
    columns = 2 * LANES * len(blocks) * low // tile
    return pl.pallas_call(
        functools.partial(project_kernel, len(blocks)),
        in_specs=[pl.BlockSpec(memory_space=pltpu.VMEM)] * (2 + len(blocks)),
        out_specs=pl.BlockSpec(memory_space=pltpu.VMEM),
        out_shape=jax.ShapeDtypeStruct((freqs, row_tiles, size, columns), jnp.bfloat16),
        scratch_shapes=[pltpu.VMEM((len(blocks),) + blocks[0].shape, jnp.bfloat16)],
        compiler_params=pltpu.CompilerParams(vmem_limit_bytes=VMEM_LIMIT),
        cost_estimate=tile_cost(freqs * row_tiles, size, tile, columns // 4),
        name="project",
    )(limits, green_right, *blocks)


def predict_kernel(groups, parts, limits_ref, right_ref, left_ref, own_ref, *refs):
    _, freqs, row_tiles, col_tiles, size, tile = left_ref.shape
    per_tile = groups // col_tiles
    others = groups - per_tile
    block_refs, out_refs, (tile_ref, sum_ref) = (
        refs[:others][::-1],
        refs[others : others + parts],
        refs[others + parts :],
    )
    _, pairs, _ = out_refs[0].shape
    rhs = parts * pairs // freqs
    own = lax.div(lax.axis_index("freq"), per_tile)
    tiles = [own]
    projected = [[[own_ref[f, i] for i in range(row_tiles)] for f in range(freqs)]]
    for step in range(1, col_tiles):
        blocks = block_refs[(step - 1) * per_tile : step * per_tile]
        tiles.append(own ^ step)
        projected.append(project_tile(own ^ step, blocks, tile_ref, limits_ref, right_ref))
    factors = {}
    for f in range(freqs):
        for i in range(row_tiles):
            straight = [part[f][i] for part in projected]
            factors[f, i] = jnp.concatenate(straight + [turned(part) for part in straight])
    for f in range(freqs):
        for i in range(row_tiles):
            left = jnp.concatenate([left_ref[c, f, i, j] for c in range(2) for j in tiles])
            predicted = dot(factors[f, i], left, 0, 0)
            for c in range(2):
                row = c * rhs
                for part, start, length in spans(f * rhs, rhs, pairs):
                    sum_ref[part, c, start : start + length, i * tile : (i + 1) * tile] = predicted[
                        row : row + length
                    ]
                    row += length
    me = lax.axis_index("rtile")
    for at, out_ref in enumerate(out_refs):
        out_ref[...] = sum_ref[target(me, at, parts)].astype(out_ref.dtype)


def predict(limits, own, blocks, green_right, green_left, parts):
    freqs, row_tiles, col_tiles, size, tile = green_left.shape[1:]
    groups = len(blocks) * col_tiles // (col_tiles - 1)
    pairs = freqs * own.shape[3] // 2
    sources = row_tiles * tile
    return pl.pallas_call(
        functools.partial(predict_kernel, groups, parts),
        in_specs=[pl.BlockSpec(memory_space=pltpu.VMEM)] * (4 + len(blocks)),
        out_specs=[pl.BlockSpec(memory_space=pltpu.VMEM)] * parts,
        out_shape=[jax.ShapeDtypeStruct((2, pairs // parts, sources), jnp.bfloat16)] * parts,
        scratch_shapes=[
            pltpu.VMEM((groups // col_tiles,) + blocks[0].shape, jnp.bfloat16),
            pltpu.VMEM((parts, 2, pairs // parts, sources), jnp.float32),
        ],
        compiler_params=pltpu.CompilerParams(vmem_limit_bytes=VMEM_LIMIT),
        cost_estimate=tile_cost(freqs * row_tiles * col_tiles, size, tile, pairs // freqs),
        name="predict",
    )(limits, green_right, green_left, own, *blocks[::-1])


def residual_kernel(data_ref, *refs):
    block_refs, (misfit_ref, *part_refs) = refs[:-3], refs[-3:]
    residual = sum(block_ref[...].astype(jnp.float32) for block_ref in block_refs) - data_ref[...]
    for c, part_ref in enumerate(part_refs):
        part_ref[...] = residual[c]
    misfit_ref[...] = residual.astype(misfit_ref.dtype)


def residual_of(blocks, data):
    shape = blocks[0].shape
    return pl.pallas_call(
        residual_kernel,
        in_specs=[pl.BlockSpec(memory_space=pltpu.VMEM)] * (1 + len(blocks)),
        out_specs=[pl.BlockSpec(memory_space=pltpu.VMEM)] * 3,
        out_shape=[
            jax.ShapeDtypeStruct(shape, jnp.bfloat16),
            jax.ShapeDtypeStruct(shape[1:], jnp.float32),
            jax.ShapeDtypeStruct(shape[1:], jnp.float32),
        ],
        compiler_params=pltpu.CompilerParams(vmem_limit_bytes=VMEM_LIMIT),
        name="residual",
    )(data, *blocks)


def back_kernel(parts, groups, reps, limits_ref, right_ref, left_ref, *refs):
    misfit_refs, out_refs = refs[:parts], refs[parts : parts + reps]
    misfit_all_ref, grad_ref = refs[parts + reps :]
    _, freqs, row_tiles, col_tiles, size, tile = left_ref.shape
    _, pairs, _ = misfit_refs[0].shape
    rhs = parts * pairs // freqs
    _, _, _, low, lanes = out_refs[0].shape
    high = lanes // rhs
    per_tile = groups * reps // col_tiles
    me = lax.axis_index("rtile")
    for at, misfit_ref in enumerate(misfit_refs):
        misfit_all_ref[origin(me, at, parts)] = misfit_ref[...].astype(jnp.float32)
    products = {}
    for f in range(freqs):
        for i in range(row_tiles):
            rows = [
                jnp.concatenate(
                    [
                        misfit_all_ref[part, c, start : start + length, i * tile : (i + 1) * tile]
                        for part, start, length in spans(f * rhs, rhs, pairs)
                    ]
                )
                for c in range(2)
            ]
            first = jnp.concatenate(rows).astype(jnp.bfloat16)
            second = jnp.concatenate([rows[1], -rows[0]]).astype(jnp.bfloat16)
            left = [left_ref[c, f, i].reshape(col_tiles * size, tile) for c in range(2)]
            products[f, i] = dot(left[0], first, 1, 1) + dot(left[1], second, 1, 1)
    factors = {}
    for f in range(freqs):
        back = [
            masked(products[f, i], limits_ref, [(f, i, j) for j in range(col_tiles)], size)
            for i in range(row_tiles)
        ]
        for j in range(col_tiles):
            straight = [part[j] for part in back]
            factors[f, j] = jnp.concatenate(straight + [turned(part) for part in straight])
    for f in range(freqs):
        for j in range(col_tiles):
            right = jnp.concatenate(
                [right_ref[c, f, :, j].reshape(row_tiles * size, tile) for c in range(2)]
            )
            grad = dot(factors[f, j], right, 0, 0)
            grad = (grad if low % 16 else grad.astype(out_refs[0].dtype)).T
            for at in range(per_tile):
                rows = at * high * low
                for c in range(2):
                    blocks = [
                        grad[rows + h * low : rows + (h + 1) * low, c * rhs : (c + 1) * rhs]
                        for h in range(high)
                    ]
                    grad_ref[j * per_tile + at, f, c] = jnp.concatenate(blocks, axis=1).astype(
                        grad_ref.dtype
                    )
    me, own = lax.axis_index("freq"), lax.axis_index("rep")
    for at, out_ref in enumerate(out_refs):
        rep = target(own, at, reps)
        if shared_steps(groups, reps):
            places = [((1 + rep), 0), ((1 + rep), 1), (3, rep), (0, rep)]
        else:
            places = [(step, rep) for step in range(groups)]
        for slot, (step, core) in enumerate(places):
            out_ref[slot] = grad_ref[target(me, step, groups) * reps + core]


def back_project(limits, misfit, green_right, green_left, groups, reps):
    parts = len(misfit)
    _, pairs, sources = misfit[0].shape
    freqs, row_tiles, col_tiles, size, tile = green_left.shape[1:]
    rhs = parts * pairs // freqs
    low = col_tiles * tile * rhs // (groups * reps * LANES)
    block = (freqs, 2, low, LANES)
    return pl.pallas_call(
        functools.partial(back_kernel, parts, groups, reps),
        in_specs=[pl.BlockSpec(memory_space=pltpu.VMEM)] * (3 + parts),
        out_specs=[pl.BlockSpec(memory_space=pltpu.VMEM)] * reps,
        out_shape=[jax.ShapeDtypeStruct((groups,) + block, jnp.bfloat16)] * reps,
        scratch_shapes=[
            pltpu.VMEM((parts, 2, pairs, sources), jnp.float32),
            pltpu.VMEM((groups * reps,) + block, jnp.bfloat16),
        ],
        compiler_params=pltpu.CompilerParams(vmem_limit_bytes=VMEM_LIMIT),
        cost_estimate=tile_cost(freqs * row_tiles * col_tiles, size, tile, rhs),
        name="back_project",
    )(limits, green_right, green_left, *misfit)


def gather_kernel(reps, *refs):
    part_refs, out_refs = refs[:reps], refs[reps:]
    slot = 0
    for out_ref in out_refs:
        for at in range(out_ref.shape[0]):
            total = sum(part_ref[slot].astype(jnp.float32) for part_ref in part_refs)
            out_ref[at] = total.astype(out_ref.dtype)
            slot += 1


def gather(parts, counts):
    shape = parts[0].shape[1:]
    return pl.pallas_call(
        functools.partial(gather_kernel, len(parts)),
        in_specs=[pl.BlockSpec(memory_space=pltpu.VMEM)] * len(parts),
        out_specs=[pl.BlockSpec(memory_space=pltpu.VMEM)] * len(counts),
        out_shape=[jax.ShapeDtypeStruct((count,) + shape, jnp.bfloat16) for count in counts],
        compiler_params=pltpu.CompilerParams(vmem_limit_bytes=VMEM_LIMIT),
        name="gather",
    )(*parts)


def other_kernel(pair_ref, out_ref):
    out_ref[0] = pair_ref[1 - lax.axis_index("rep")]


def other(pair):
    return pl.pallas_call(
        other_kernel,
        in_specs=[pl.BlockSpec(memory_space=pltpu.VMEM)],
        out_specs=pl.BlockSpec(memory_space=pltpu.VMEM),
        out_shape=jax.ShapeDtypeStruct((1,) + pair.shape[1:], pair.dtype),
        compiler_params=pltpu.CompilerParams(vmem_limit_bytes=VMEM_LIMIT),
        name="other",
    )(pair)


def return_spectra(parts):
    groups, reps = parts[0].shape[0], len(parts)
    parts = exchange(parts, "rep")
    if not shared_steps(groups, reps):
        return exchange(gather(parts, [1] * groups), "freq")
    pair, last, own = gather(parts, [2, 1, 1])
    devices = [(chip, core) for chip in range(groups) for core in range(reps)]
    near = [(chip * reps + core, (chip ^ (1 + core)) * reps + core) for chip, core in devices]
    far = [(chip * reps + core, (chip ^ 3) * reps + core) for chip, core in devices]
    pair = lax.ppermute(pair, ("freq", "rep"), near)
    last = lax.ppermute(last, ("freq", "rep"), far)
    swapped = lax.ppermute(other(pair), "rep", [(0, 1), (1, 0)])
    return [own, pair, swapped, last]


def gradient_kernel(reps, table_ref, *refs):
    part_refs, (out_hbm, out_ref, rows_ref, out_sems) = refs[-5::-1], refs[-4:]
    groups = len(part_refs)
    _, freqs, _, low, lanes = part_refs[0].shape
    high, _, rhs, length = out_ref.shape
    bins = table_ref.shape[0]
    me = lax.axis_index("freq")
    if shared_steps(groups, reps):
        core = lax.axis_index("rep")
        places = [(0, 0), (1 + core, core), (2 - core, 0), (3, 0)]
    else:
        places = [(step, 0) for step in range(groups)]
    for part_ref, (step, place) in zip(part_refs, places):
        g = origin(me, step, groups)
        for f in range(freqs):
            for c in range(2):
                rows = pl.ds(c * groups * freqs + g * freqs + f, low, stride=bins)
                rows_ref[rows, :] = part_ref[place, f, c].astype(jnp.float32)
    table = table_ref[...]
    width = math.gcd(length, 256)
    copies = []
    for at, (start, part) in enumerate(ramp(low)):
        coefficients = jnp.concatenate(
            [rows_ref[row * bins : (row + 1) * bins] for row in range(start, start + part)],
            axis=1,
        ).astype(jnp.bfloat16)
        for column in range(0, length, width):
            columns = slice(column, column + width)
            traces = dot(coefficients, table[:, columns], 0, 0).astype(out_ref.dtype)
            for row in range(part):
                out_ref[:, start + row, :, columns] = traces[
                    row * lanes : (row + 1) * lanes
                ].reshape(high, rhs, width)
        rows = pl.ds(start, part)
        copies.append(
            pltpu.make_async_copy(out_ref.at[:, rows], out_hbm.at[:, rows], out_sems.at[at])
        )
        copies[-1].start()
    for copy in copies:
        copy.wait()


def gradient_of(parts, table, rhs, reps):
    _, _, _, low, lanes = parts[0].shape
    bins, length = table.shape
    high = lanes // rhs
    chunks = len(ramp(low))
    shape = (high, low, rhs, length)
    out = pl.pallas_call(
        functools.partial(gradient_kernel, reps),
        in_specs=[pl.BlockSpec(memory_space=pltpu.VMEM)] * (1 + len(parts)),
        out_specs=pl.BlockSpec(memory_space=pltpu.HBM),
        out_shape=jax.ShapeDtypeStruct(shape, jnp.bfloat16),
        scratch_shapes=[
            pltpu.VMEM(shape, jnp.bfloat16),
            pltpu.VMEM((low * bins, lanes), jnp.float32),
            pltpu.SemaphoreType.DMA((chunks,)),
        ],
        compiler_params=pltpu.CompilerParams(vmem_limit_bytes=VMEM_LIMIT),
        name="gradient",
    )(table, *parts[::-1])
    return out.reshape(1, high * low, rhs, length)


def shards(model, green_left, green_right, ranks, data):
    freq_count = lax.axis_size("freq")
    tile_count = lax.axis_size("rtile")
    rep_count = lax.axis_size("rep")
    freq_local = ranks.shape[0]
    rhs_count = model.shape[2]
    table, spectrum = spectrum_of(model[0], freq_count, freq_local)
    spectrum = exchange(spectrum, "freq")
    limits = limits_of(ranks, table)
    per_tile = freq_count // green_right.shape[3]
    own = project(limits, spectrum[:per_tile], green_right)
    predicted = predict(limits, own, spectrum[per_tile:], green_right, green_left, tile_count)
    misfit, *residual = residual_of(middle_first(exchange(predicted, "rtile")), data)
    misfit = exchange([misfit] * tile_count, "rtile")
    partial = back_project(limits, misfit, green_right, green_left, freq_count, rep_count)
    arrived = return_spectra(partial)
    return (jnp.stack(residual), gradient_of(arrived, table, rhs_count, rep_count))


def solution(mesh):
    return jax.shard_map(
        shards,
        mesh=mesh,
        in_specs=(
            P("rtile", "freq", None, None),
            P(None, "freq", "rep", "rtile", None, None),
            P(None, "freq", "rep", "rtile", None, None),
            P("freq", "rep", "rtile"),
            P(None, ("freq", "rtile"), "rep"),
        ),
        out_specs=(P(None, ("freq", "rtile"), "rep"), P("rtile", ("freq", "rep"), None, None)),
        check_vma=False,
    )
```
